32 devices in a mesh: dp: 8 (over z, y), row: 2 (over x), col: 2 (over core).
Axes of the slice: x: 2, y: 2, z: 4, core: 2. Of those that a mesh axis runs over, the one named last changes fastest.
Arguments:
- activations: bfloat16 [16384, 2048], P(('dp', 'row'), 'col'), may hold values from -6 to 6
- grad_out: bfloat16 [16384, 2048], P(('dp', 'row'), 'col'), may hold values from -6 to 6
- segments: int32 [8, 2048], P('dp'), may hold values from 0 to 15, never falling along the last dimension, each value on 1 to 1792 neighbouring positions
- first_gain: float32 [2048], P('col'), may hold values from 0.5 to 1.5
- query_weight: bfloat16 [2048, 2048], P('col', 'row'), may hold values from -0.125 to 0.125
- key_weight: bfloat16 [2048, 512], P('col', 'row'), may hold values from -0.125 to 0.125
- value_weight: bfloat16 [2048, 512], P('col', 'row'), may hold values from -0.125 to 0.125
- query_down: bfloat16 [2048, 8], P('col'), may hold values from -0.125 to 0.125
- query_up: bfloat16 [8, 2048], P(None, 'row'), may hold values from -1.5 to 1.5
- key_down: bfloat16 [2048, 8], P('col'), may hold values from -0.125 to 0.125
- key_up: bfloat16 [8, 512], P(None, 'row'), may hold values from -1.5 to 1.5
- value_down: bfloat16 [2048, 8], P('col'), may hold values from -0.125 to 0.125
- value_up: bfloat16 [8, 512], P(None, 'row'), may hold values from -1.5 to 1.5
- query_map: bfloat16 [32, 64, 64], P('row'), may hold values from -0.75 to 0.75
- key_map: bfloat16 [8, 64, 64], P('row'), may hold values from -0.75 to 0.75
- output_weight: bfloat16 [2048, 2048], P('row', 'col'), may hold values from -0.25 to 0.25
- output_down: bfloat16 [2048, 8], P('row'), may hold values from -0.25 to 0.25
- output_up: bfloat16 [8, 2048], P(None, 'col'), may hold values from -1.5 to 1.5
- second_gain: float32 [2048], P('col'), may hold values from 0.5 to 1.5
- gate_weight: bfloat16 [2048, 8192], P('col', 'row'), may hold values from -0.125 to 0.125
- up_weight: bfloat16 [2048, 8192], P('col', 'row'), may hold values from -0.125 to 0.125
- down_weight: bfloat16 [8192, 2048], P('row', 'col'), may hold values from -0.09375 to 0.09375
Outputs:
- result: bfloat16 [16384, 2048], P(('dp', 'row'), 'col')
- grad_activations: float32 [16384, 2048], P(('dp', 'row'), 'col')
- grad_first_gain: float32 [2048], P('col')
- grad_query_weight: float32 [2048, 2048], P(('col', 'dp'), 'row')
- grad_key_weight: float32 [2048, 512], P(('col', 'dp'), 'row')
- grad_value_weight: float32 [2048, 512], P(('col', 'dp'), 'row')
- grad_query_down: float32 [2048, 8], P('col')
- grad_query_up: float32 [8, 2048], P(None, 'row')
- grad_key_down: float32 [2048, 8], P('col')
- grad_key_up: float32 [8, 512], P(None, 'row')
- grad_value_down: float32 [2048, 8], P('col')
- grad_value_up: float32 [8, 512], P(None, 'row')
- grad_query_map: float32 [32, 64, 64], P('row')
- grad_key_map: float32 [8, 64, 64], P('row')
- grad_output_weight: float32 [2048, 2048], P(('row', 'dp'), 'col')
- grad_output_down: float32 [2048, 8], P('row')
- grad_output_up: float32 [8, 2048], P(None, 'col')
- grad_second_gain: float32 [2048], P('col')
- grad_gate_weight: float32 [2048, 8192], P(('col', 'dp'), 'row')
- grad_up_weight: float32 [2048, 8192], P(('col', 'dp'), 'row')
- grad_down_weight: float32 [8192, 2048], P('row', ('col', 'dp'))
The draws below stay inside these ranges and needn't reach their ends.
Inputs may be any that keep to these rules, and one draw needn't show every extreme that they name: `segments`: in every sequence the document numbers never fall, every number from 0 to 15 is used, each document has 1 to 1792 positions and one has exactly 1792.
All inputs are finite; a program needn't handle non-finite values.
Results may differ from the reference program's by a relative error of at most 0.02.
Values may be sent and summed in bfloat16 or wider, within the bound.
A program may use at most 448 MiB of HBM per device.

```python
import math
import jax
import jax.numpy as jnp
import numpy as np
from jax import lax

D = 2048
HEADS = 32
KV_HEADS = 8
HEAD_DIM = 64
FF = 8192
RANK = 8
WINDOW = 64
BLOCK = 512
SEQ = 2048
NSEQ = 8
TOKENS = 16384
DOCS = 16
DOC_MOST = 1792


def block_levels(own_key, dims, cuts, low, top_value):
    level = 1.0
    for dim, shards_of in cuts:
        heights = jax.random.uniform(jax.random.fold_in(jax.random.fold_in(own_key, 6), dim), (shards_of,), jnp.float32, low / len(cuts), top_value / len(cuts))
        level = level * jnp.repeat(jnp.exp(heights), dims[dim] // shards_of).reshape((-1,) + (1,) * (len(dims) - 1 - dim))
    return level


def length_profile(amount, total, bound, skew):
    weights = [(1 << 20) // math.isqrt(standing ** skew) + 1 for standing in range(2, amount + 1)]
    spare, holding = total - bound - (amount - 1), [1] * (amount - 1)
    while spare > 0:
        movable = [i for i in range(amount - 1) if holding[i] < bound]
        mass, left = sum([weights[i] for i in movable]), spare
        for i in movable:
            addition = min(bound - holding[i], max(1, left * weights[i] // mass), spare)
            holding[i] = holding[i] + addition
            spare = spare - addition
    return np.array([bound] + holding)


def uneven(stream_key, count, total, most, skew):
    if count == 2:
        one = jax.random.randint(stream_key, (), max(1, total - most), min(most, total - 1) + 1)
        return jnp.stack([one, total - one])
    lengths = jnp.asarray(length_profile(count, total, most, skew), jnp.int32)
    pairs = (count - 1) // 2
    giver, receiver = lengths[1:1 + 2 * pairs:2], lengths[2:2 + 2 * pairs:2]
    room = jnp.minimum(giver - 1, most - receiver)
    moved = jax.random.randint(jax.random.fold_in(stream_key, 1), (pairs,), 0, 1 << 20) % (room + 1)
    lengths = lengths.at[1:1 + 2 * pairs:2].set(giver - moved).at[2:2 + 2 * pairs:2].set(receiver + moved)
    return lengths[jax.random.permutation(jax.random.fold_in(stream_key, 2), count)]


def normal_values(key, dims, deviation, most, cuts=(), kind=jnp.bfloat16):
    gain = block_levels(key, dims, cuts, -0.22, 0.18) if cuts else 1.0
    result = jax.random.normal(key, dims, jnp.float32) * deviation * gain
    return jnp.minimum(jnp.maximum(result, -most), most).astype(kind)


def setup_inputs(seed: int = 0) -> dict:
    keys = jax.random.split(jax.random.key(seed), 23)
    activations = normal_values(keys[0], (TOKENS, D), 1.0, 6.0, ((0, 16), (1, 2)))
    grad_out = normal_values(keys[1], (TOKENS, D), 1.0, 6.0, ((0, 16), (1, 2)))
    segments = jax.vmap(lambda own: jnp.searchsorted(jnp.cumsum(uneven(own, DOCS, SEQ, DOC_MOST, 2)), jnp.arange(SEQ), side="right"))(jax.random.split(keys[2], NSEQ)).reshape((NSEQ, SEQ)).astype(jnp.int32)
    first_gain = jnp.clip(1.0 + 0.1 * jax.random.normal(keys[3], (D,), jnp.float32), 0.5, 1.5)
    query_weight = normal_values(keys[4], (D, HEADS * HEAD_DIM), D ** -0.5, 0.125, ((0, 2), (1, 2)))
    key_weight = normal_values(keys[5], (D, KV_HEADS * HEAD_DIM), D ** -0.5, 0.125, ((0, 2), (1, 2)))
    value_weight = normal_values(keys[6], (D, KV_HEADS * HEAD_DIM), D ** -0.5, 0.125, ((0, 2), (1, 2)))
    query_down = normal_values(keys[7], (D, RANK), D ** -0.5, 0.125, ((0, 2),))
    query_up = normal_values(keys[8], (RANK, HEADS * HEAD_DIM), (2 * RANK) ** -0.5, 1.5, ((1, 2),))
    key_down = normal_values(keys[9], (D, RANK), D ** -0.5, 0.125, ((0, 2),))
    key_up = normal_values(keys[10], (RANK, KV_HEADS * HEAD_DIM), (2 * RANK) ** -0.5, 1.5, ((1, 2),))
    value_down = normal_values(keys[11], (D, RANK), D ** -0.5, 0.125, ((0, 2),))
    value_up = normal_values(keys[12], (RANK, KV_HEADS * HEAD_DIM), (2 * RANK) ** -0.5, 1.5, ((1, 2),))
    query_map = normal_values(keys[13], (HEADS, HEAD_DIM, HEAD_DIM), HEAD_DIM ** -0.5, 0.75, ((0, 2),))
    key_map = normal_values(keys[14], (KV_HEADS, HEAD_DIM, HEAD_DIM), HEAD_DIM ** -0.5, 0.75, ((0, 2),))
    output_weight = normal_values(keys[15], (HEADS * HEAD_DIM, D), ((HEADS * HEAD_DIM) // 4) ** -0.5, 0.25, ((0, 2), (1, 2)))
    output_down = normal_values(keys[16], (HEADS * HEAD_DIM, RANK), ((HEADS * HEAD_DIM) // 4) ** -0.5, 0.25, ((0, 2),))
    output_up = normal_values(keys[17], (RANK, D), (2 * RANK) ** -0.5, 1.5, ((1, 2),))
    second_gain = jnp.clip(1.0 + 0.1 * jax.random.normal(keys[18], (D,), jnp.float32), 0.5, 1.5)
    gate_weight = normal_values(keys[19], (D, FF), D ** -0.5, 0.125, ((0, 2), (1, 2)))
    up_weight = normal_values(keys[20], (D, FF), D ** -0.5, 0.125, ((0, 2), (1, 2)))
    down_weight = normal_values(keys[21], (FF, D), (FF // 2) ** -0.5, 0.09375, ((0, 2), (1, 2)))
    return dict(activations=activations, grad_out=grad_out, segments=segments, first_gain=first_gain, query_weight=query_weight, key_weight=key_weight, value_weight=value_weight, query_down=query_down, query_up=query_up, key_down=key_down, key_up=key_up, value_down=value_down, value_up=value_up, query_map=query_map, key_map=key_map, output_weight=output_weight, output_down=output_down, output_up=output_up, second_gain=second_gain, gate_weight=gate_weight, up_weight=up_weight, down_weight=down_weight)


@jax.custom_vjp
def low(v):
    return lax.optimization_barrier(v.astype(jnp.bfloat16)).astype(jnp.float32)

@jax.custom_vjp
def low_back(v):
    return v

def low_keep(v):
    return (low(v), None)

def low_pass(kept, grad):
    return (grad,)

def back_keep(v):
    return (v, None)

def back_low(kept, grad):
    return (low(grad),)
low.defvjp(low_keep, low_pass)
low_back.defvjp(back_keep, back_low)
norm_eps = 1e-05

def matmul(left, right):
    return jnp.dot(left, right, precision=lax.Precision.HIGHEST, preferred_element_type=jnp.float32)

def rms_scale(values):
    return lax.rsqrt(lax.optimization_barrier(jnp.mean(values * values, axis=-1, keepdims=True)) + norm_eps)

def feature_map(heads, weights):
    before = jnp.einsum('lhd,hde->lhe', heads, weights, precision=lax.Precision.HIGHEST)
    return jnp.concatenate([jax.nn.softmax(before, axis=-1), jax.nn.softmax(-before, axis=-1)], axis=-1)

def block_masks(query_documents, tile_documents):
    offsets = jnp.arange(BLOCK, dtype=jnp.int32)[:, None] + WINDOW - jnp.arange(BLOCK + WINDOW, dtype=jnp.int32)[None, :]
    same_doc = query_documents[:, None] == tile_documents[None, :]
    window_mask = same_doc & (offsets >= 0) & (offsets < WINDOW)
    linear_mask = same_doc & (offsets >= WINDOW)
    return (window_mask, linear_mask)

def attend_block(carried, tensors):
    linear_state, norm_state, last_document = carried
    query_block, query_features, key_tile, value_tile, key_features, query_documents, tile_documents = tensors
    window_mask, linear_mask = block_masks(query_documents, tile_documents)
    score_scale = 1.0 / math.sqrt(HEAD_DIM)
    scores = low_back(jnp.einsum('qgrd,kgd->grqk', query_block, key_tile, precision=lax.Precision.HIGHEST) * score_scale)
    linear = low_back(jnp.einsum('qgrf,kgf->grqk', query_features, key_features, precision=lax.Precision.HIGHEST))
    weights = jnp.where(window_mask, jnp.exp(jnp.where(window_mask, scores, 0.0)), 0.0) + jnp.where(linear_mask, linear, 0.0)
    same_flag = (query_documents == last_document).astype(jnp.float32)
    carried_state = low_back(linear_state)
    through = low_back(jnp.einsum('qgrf,gfd->grqd', query_features, low(carried_state), precision=lax.Precision.HIGHEST))
    normal = jnp.einsum('qgrf,gf->grq', query_features, norm_state, precision=lax.Precision.HIGHEST)
    totals = lax.optimization_barrier(jnp.sum(weights, axis=-1)) + same_flag * normal
    probabilities = low(weights / totals[..., None])
    mixed_rows = jnp.einsum('grqk,kgd->grqd', probabilities, value_tile, precision=lax.Precision.HIGHEST) + (same_flag / totals)[..., None] * through
    next_document = tile_documents[BLOCK - 1]
    keep_flag = (last_document == next_document).astype(jnp.float32)
    member = (tile_documents[:BLOCK] == next_document).astype(jnp.float32)
    key_member = key_features[:BLOCK] * member[:, None, None]
    added_state = jnp.einsum('kgf,kgd->gfd', key_member, value_tile[:BLOCK], precision=lax.Precision.HIGHEST)
    new_state = keep_flag * carried_state + added_state
    new_norm = keep_flag * norm_state + lax.optimization_barrier(jnp.sum(key_member, axis=0))
    return ((new_state, new_norm, next_document), jnp.transpose(mixed_rows, (2, 0, 1, 3)))

def attend(query_heads, key_heads, value_heads, query_features, key_features, documents):
    length = query_heads.shape[0]
    groups = key_heads.shape[1]

    def pad_front(values):
        return jnp.concatenate([jnp.zeros((WINDOW,) + values.shape[1:], values.dtype), values], axis=0)
    key_pad = pad_front(key_heads)
    value_pad = pad_front(value_heads)
    feature_pad = pad_front(key_features)
    padded_documents = jnp.concatenate([jnp.full((WINDOW,), -1, jnp.int32), documents.astype(jnp.int32)])

    def block_step(carried, block_index):
        first_row = block_index * BLOCK
        tensors = (lax.dynamic_slice_in_dim(query_heads, first_row, BLOCK, 0), lax.dynamic_slice_in_dim(query_features, first_row, BLOCK, 0), lax.dynamic_slice_in_dim(key_pad, first_row, BLOCK + WINDOW, 0), lax.dynamic_slice_in_dim(value_pad, first_row, BLOCK + WINDOW, 0), lax.dynamic_slice_in_dim(feature_pad, first_row, BLOCK + WINDOW, 0), lax.dynamic_slice_in_dim(documents.astype(jnp.int32), first_row, BLOCK, 0), lax.dynamic_slice_in_dim(padded_documents, first_row, BLOCK + WINDOW, 0))
        return attend_block(carried, tensors)
    start_state = (jnp.zeros((groups, 2 * HEAD_DIM, HEAD_DIM), jnp.float32), jnp.zeros((groups, 2 * HEAD_DIM), jnp.float32), jnp.int32(-1))
    _, outputs = lax.scan(jax.checkpoint(block_step), start_state, jnp.arange(length // BLOCK, dtype=jnp.int32))
    return outputs.reshape(length, -1)

def layer(inputs, documents, params):
    first_gain, query_weight, key_weight, value_weight, query_down, query_up, key_down, key_up, value_down, value_up, query_map, key_map, output_weight, output_down, output_up, second_gain, gate_weight, up_weight, down_weight = params
    length = inputs.shape[0]
    ratio = HEADS // KV_HEADS
    first_normed = low(inputs * rms_scale(inputs) * first_gain)

    def project(weight, down, upper):
        adapter = low(low_back(matmul(first_normed, down)))
        return low(low_back(matmul(first_normed, weight) + matmul(adapter, upper)))
    queries = project(query_weight, query_down, query_up).reshape(length, HEADS, HEAD_DIM)
    key_rows = project(key_weight, key_down, key_up).reshape(length, KV_HEADS, HEAD_DIM)
    value_rows = project(value_weight, value_down, value_up).reshape(length, KV_HEADS, HEAD_DIM)
    query_features = low(feature_map(queries, query_map)).reshape(length, KV_HEADS, ratio, 2 * HEAD_DIM)
    key_features = low(feature_map(key_rows, key_map))
    mixed = low(low_back(attend(queries.reshape(length, KV_HEADS, ratio, HEAD_DIM), key_rows, value_rows, query_features, key_features, documents)))
    out_adapter = low(low_back(matmul(mixed, output_down)))
    attended = low_back(matmul(mixed, output_weight) + matmul(out_adapter, output_up))
    hidden_state = inputs + attended
    second_normed = low(hidden_state * rms_scale(hidden_state) * second_gain)
    gate_value = low_back(matmul(second_normed, gate_weight))
    up_value = low_back(matmul(second_normed, up_weight))
    hidden = low(jax.nn.silu(gate_value) * up_value)
    return hidden_state + matmul(hidden, down_weight)

def reference(activations, grad_out, segments, first_gain, query_weight, key_weight, value_weight, query_down, query_up, key_down, key_up, value_down, value_up, query_map, key_map, output_weight, output_down, output_up, second_gain, gate_weight, up_weight, down_weight):
    params = tuple((array.astype(jnp.float32) for array in (first_gain, query_weight, key_weight, value_weight, query_down, query_up, key_down, key_up, value_down, value_up, query_map, key_map, output_weight, output_down, output_up, second_gain, gate_weight, up_weight, down_weight)))

    def forward(inputs, *weights):
        sequences = inputs.reshape(NSEQ, SEQ, D)

        def one_sequence(carried, pieces):
            return (carried, layer(pieces[0], pieces[1], weights))
        _, outputs = lax.scan(jax.checkpoint(one_sequence), jnp.float32(0.0), (sequences, segments))
        return outputs.reshape(TOKENS, D)
    primal, pullback = jax.vjp(forward, activations.astype(jnp.float32), *params)
    gradients = pullback(grad_out.astype(jnp.float32))
    return (primal.astype(jnp.bfloat16), gradients[0], gradients[1], gradients[2], gradients[3], gradients[4], gradients[5], gradients[6], gradients[7], gradients[8], gradients[9], gradients[10], gradients[11], gradients[12], gradients[13], gradients[14], gradients[15], gradients[16], gradients[17], gradients[18], gradients[19])
```

```python
import functools
import jax
import jax.numpy as jnp
from jax import lax
from jax.experimental import pallas as pl
from jax.experimental.pallas import tpu as pltpu
from jax.sharding import PartitionSpec as P

HEAD_DIM = 64
WINDOW = 64
BLOCK = 512
SUB = 128
SCALE = 0.125
NSUB = BLOCK // SUB
LANES = 128
MLP_TILE = 512
SUM_TILE = 256
GRAD_TILE = 512
VMEM_LIMIT = 56 * 1024 * 1024
FINISH_ORDER = ("down_own", "down_got", "output", "proj")
norm_eps = 1e-05
F32 = jnp.float32
BF16 = jnp.bfloat16


def dot_nn(left, right):
    return lax.dot_general(left, right, (((1,), (0,)), ((), ())), preferred_element_type=F32)


def dot_nt(left, right):
    return lax.dot_general(left, right, (((1,), (1,)), ((), ())), preferred_element_type=F32)


def softmax_halves(before):
    def soft(values):
        powers = jnp.exp(values - jnp.max(values, axis=0, keepdims=True))
        return powers * (1.0 / jnp.sum(powers, axis=0, keepdims=True))

    return jnp.concatenate([soft(before[:HEAD_DIM]), soft(before[HEAD_DIM:])], axis=0)


def halves_backward(probs, grads):
    def half(p, g):
        return p * (g - jnp.sum(p * g, axis=0, keepdims=True))

    return half(probs[:HEAD_DIM], grads[:HEAD_DIM]) - half(probs[HEAD_DIM:], grads[HEAD_DIM:])


def side_by_side(parts, sub):
    return jnp.concatenate([part[:, sub * SUB : (sub + 1) * SUB] for part in parts], axis=1)


def key_side(kt_ref, vt_ref, kmap_ref, kft_ref, kfr_ref, kr_ref, vr_ref):
    features = softmax_halves(dot_nn(kmap_ref[0], kt_ref[...])).astype(BF16)
    kft_ref[...] = features
    kfr_ref[...] = jnp.transpose(features)
    kr_ref[...] = jnp.transpose(kt_ref[...])
    if vr_ref is not None:
        vr_ref[...] = jnp.transpose(vt_ref[...])


def tile_rows(start_ref, base, sub, ratio):
    low_one = start_ref[0, :, sub * SUB : (sub + 1) * SUB] + (WINDOW - base)
    low = jnp.concatenate([low_one] * ratio, axis=1)
    width = ratio * SUB
    place = sub * SUB + (lax.broadcasted_iota(jnp.int32, (1, width), 1) & (SUB - 1))
    same = jnp.where(low <= -1, 1.0, 0.0)
    return low, place, same


def tile_weights(kfr_ref, kr_ref, base, sub, low, place, q_sub, qf_sub):
    width = q_sub.shape[1]
    first = sub * SUB
    lin_keys = first + SUB
    win_keys = SUB + WINDOW
    link = dot_nn(kfr_ref[pl.ds(base, lin_keys), :], qf_sub)
    score = dot_nn(kr_ref[pl.ds(base + first, win_keys), :], q_sub) * SCALE
    lin_at = lax.broadcasted_iota(jnp.int32, (lin_keys, width), 0)
    win_at = lax.broadcasted_iota(jnp.int32, (win_keys, width), 0) + first
    lin_mask = (lin_at >= low) & (lin_at <= place)
    win_mask = (win_at >= jnp.maximum(low, place + 1)) & (win_at <= place + WINDOW)
    lin = jnp.where(lin_mask, link, 0.0)
    win = jnp.where(win_mask, jnp.exp(score), 0.0)
    return lin, win, lin_mask, win_mask


def member_lanes(base, mark):
    at = lax.broadcasted_iota(jnp.int32, (1, BLOCK), 1) + (base - WINDOW)
    return at >= mark


def forward_kernel(
    mark_ref, start_ref, qt_ref, kt_ref, vt_ref, qmap_ref, kmap_ref, mix_ref, inv_ref,
    kft_ref, kfr_ref, kr_ref, state_ref, norm_ref,
):
    b = pl.program_id(1)
    ratio = qmap_ref.shape[0]
    base = pl.multiple_of(b * BLOCK, BLOCK)

    @pl.when(b == 0)
    def _():
        key_side(kt_ref, vt_ref, kmap_ref, kft_ref, kfr_ref, kr_ref, None)
        state_ref[...] = jnp.zeros_like(state_ref)
        norm_ref[...] = jnp.zeros_like(norm_ref)

    queries = [qt_ref[h * HEAD_DIM : (h + 1) * HEAD_DIM, :] for h in range(ratio)]
    features = [softmax_halves(dot_nn(qmap_ref[h], queries[h])).astype(BF16) for h in range(ratio)]
    state_low = state_ref[...].astype(BF16)
    norm = norm_ref[...]
    for sub in range(NSUB):
        first = sub * SUB
        q_sub = side_by_side(queries, sub)
        qf_sub = side_by_side(features, sub)
        low, place, same = tile_rows(start_ref, base, sub, ratio)
        lin, win, _, _ = tile_weights(kfr_ref, kr_ref, base, sub, low, place, q_sub, qf_sub)
        carried = dot_nn(state_low, qf_sub)
        normal = jnp.sum(qf_sub.astype(F32) * norm, axis=0, keepdims=True)
        total = (
            jnp.sum(lin, axis=0, keepdims=True) + jnp.sum(win, axis=0, keepdims=True) + same * normal
        )
        inverse = 1.0 / total
        mixed = dot_nn(vt_ref[:, pl.ds(base, first + SUB)], lin.astype(BF16))
        mixed += dot_nn(vt_ref[:, pl.ds(base + first, SUB + WINDOW)], win.astype(BF16))
        mixed = ((mixed + same * carried) * inverse).astype(BF16)
        for h in range(ratio):
            lanes = slice(h * SUB, (h + 1) * SUB)
            mix_ref[h * HEAD_DIM : (h + 1) * HEAD_DIM, first : first + SUB] = mixed[:, lanes]
            inv_ref[0, h : h + 1, first : first + SUB] = inverse[:, lanes]

    mark = mark_ref[b + 1]
    keep = jnp.where((mark <= b * BLOCK - WINDOW - 1), 1.0, 0.0)
    tile = kft_ref[:, pl.ds(base, BLOCK)]
    member = jnp.where(member_lanes(base, mark), tile, jnp.zeros_like(tile))
    state_ref[...] = keep * state_ref[...] + dot_nt(vt_ref[:, pl.ds(base, BLOCK)], member)
    norm_ref[...] = keep * norm + jnp.sum(member.astype(F32), axis=1, keepdims=True)


def backward_kernel(
    mark_ref, start_ref, qt_ref, kt_ref, vt_ref, qmap_ref, kmap_ref, dmt_ref, mix_ref, inv_ref,
    qback_ref, kback_ref,
    dqt_ref, dkt_ref, dvt_ref, gqm_ref, gkm_ref,
    kft_ref, kfr_ref, kr_ref, vr_ref, states_ref, statet_ref, norms_ref,
    dk_acc, dkf_acc, dv_acc, dst_ref, dstt_ref, dnorm_ref,
):
    step = pl.program_id(1)
    blocks = pl.num_programs(1)
    count = states_ref.shape[0]
    b = blocks - 1 - step
    ratio = qmap_ref.shape[0]
    base = pl.multiple_of(b * BLOCK, BLOCK)

    @pl.when(step == 0)
    def _():
        key_side(kt_ref, vt_ref, kmap_ref, kft_ref, kfr_ref, kr_ref, vr_ref)
        state = jnp.zeros(statet_ref.shape[1:], F32)
        norm = jnp.zeros(norms_ref.shape[1:], F32)
        statet = jnp.zeros(states_ref.shape[1:], F32)
        for i in range(count):
            statet_ref[i] = state.astype(BF16)
            states_ref[i] = statet.astype(BF16)
            norms_ref[i] = norm
            if i + 1 < count:
                mark = mark_ref[i + 1]
                keep = jnp.where((mark <= i * BLOCK - WINDOW - 1), 1.0, 0.0)
                tile = kft_ref[:, i * BLOCK : (i + 1) * BLOCK]
                member = jnp.where(member_lanes(i * BLOCK, mark), tile, jnp.zeros_like(tile))
                values = vt_ref[:, i * BLOCK : (i + 1) * BLOCK]
                state = keep * state + dot_nt(values, member)
                statet = keep * statet + dot_nt(member, values)
                norm = keep * norm + jnp.sum(member.astype(F32), axis=1, keepdims=True)
        dk_acc[...] = jnp.zeros_like(dk_acc)
        dkf_acc[...] = jnp.zeros_like(dkf_acc)
        dv_acc[...] = jnp.zeros_like(dv_acc)
        dst_ref[...] = jnp.zeros_like(dst_ref)
        dstt_ref[...] = jnp.zeros_like(dstt_ref)
        dnorm_ref[...] = jnp.zeros_like(dnorm_ref)
        gqm_ref[...] = jnp.zeros_like(gqm_ref)

    mark = mark_ref[b + 1]
    keep = jnp.where((mark <= b * BLOCK - WINDOW - 1), 1.0, 0.0)
    tile_lanes = pl.ds(base, BLOCK)
    member = member_lanes(base, mark)
    dst_low = dst_ref[...].astype(BF16)
    dstt_low = dstt_ref[...].astype(BF16)
    dkf_acc[:, tile_lanes] += jnp.where(
        member, dot_nn(dst_low, vt_ref[:, tile_lanes]) + dnorm_ref[...], 0.0
    )
    dv_acc[:, tile_lanes] += jnp.where(member, dot_nn(dstt_low, kft_ref[:, tile_lanes]), 0.0)

    queries = [qt_ref[h * HEAD_DIM : (h + 1) * HEAD_DIM, :] for h in range(ratio)]
    gradients = [dmt_ref[h * HEAD_DIM : (h + 1) * HEAD_DIM, :] for h in range(ratio)]
    mixes = [mix_ref[h * HEAD_DIM : (h + 1) * HEAD_DIM, :] for h in range(ratio)]
    inverses = [inv_ref[0, h : h + 1, :] for h in range(ratio)]
    probabilities = [softmax_halves(dot_nn(qmap_ref[h], queries[h])) for h in range(ratio)]
    features = [p.astype(BF16) for p in probabilities]
    norm = norms_ref[b]
    state_low = states_ref[b]
    dnorm = jnp.zeros((2 * HEAD_DIM, SUB), F32)
    dst = keep * dst_ref[...]
    dstt = keep * dstt_ref[...]
    dq_parts, dpre_parts = [], []
    for sub in range(NSUB):
        first = sub * SUB
        lin_lanes = pl.ds(base, first + SUB)
        win_lanes = pl.ds(base + first, SUB + WINDOW)
        q_sub = side_by_side(queries, sub)
        qf_sub = side_by_side(features, sub)
        dm_sub = side_by_side(gradients, sub)
        inverse = side_by_side(inverses, sub)
        dm_float = dm_sub.astype(F32)
        low, place, same = tile_rows(start_ref, base, sub, ratio)
        lin, win, lin_mask, win_mask = tile_weights(
            kfr_ref, kr_ref, base, sub, low, place, q_sub, qf_sub
        )
        delta = jnp.sum(dm_float * side_by_side(mixes, sub).astype(F32), axis=0, keepdims=True)
        dv_acc[:, lin_lanes] += dot_nt(dm_sub, (lin * inverse).astype(BF16))
        dv_acc[:, win_lanes] += dot_nt(dm_sub, (win * inverse).astype(BF16))
        dlin = (dot_nn(vr_ref[lin_lanes, :], dm_sub) - delta) * inverse
        dwin = (dot_nn(vr_ref[win_lanes, :], dm_sub) - delta) * inverse
        dlink = jnp.where(lin_mask, dlin, 0.0).astype(BF16)
        dscore = (win * dwin).astype(BF16)
        dcarried = (dm_float * (same * inverse)).astype(BF16)
        dtotal = -delta * (same * inverse)
        dk_acc[:, win_lanes] += dot_nt(q_sub, dscore)
        dkf_acc[:, lin_lanes] += dot_nt(qf_sub, dlink)
        dq_parts.append(dot_nn(kt_ref[:, win_lanes], dscore) * SCALE)
        dqf = dot_nn(kft_ref[:, lin_lanes], dlink) + dot_nn(state_low, dcarried) + norm * dtotal
        dst = dst + dot_nt(qf_sub, dcarried)
        dstt = dstt + dot_nt(dcarried, qf_sub)
        weighted = qf_sub.astype(F32) * dtotal
        for h in range(ratio):
            dnorm = dnorm + weighted[:, h * SUB : (h + 1) * SUB]
        dpre_parts.append(halves_backward(side_by_side(probabilities, sub), dqf).astype(BF16))
    dst_ref[...] = dst.astype(BF16).astype(F32)
    dstt_ref[...] = dstt.astype(BF16).astype(F32)
    dnorm_ref[...] = jnp.sum(dnorm, axis=1, keepdims=True) + keep * dnorm_ref[...]
    for h in range(ratio):
        lanes = slice(h * SUB, (h + 1) * SUB)
        dpre = jnp.concatenate([part[:, lanes] for part in dpre_parts], axis=1)
        dq = jnp.concatenate([part[:, lanes] for part in dq_parts], axis=1)
        dq = dq + dot_nn(qback_ref[h], dpre)
        dqt_ref[h * HEAD_DIM : (h + 1) * HEAD_DIM, :] = dq.astype(BF16)
        gqm_ref[h] += dot_nt(queries[h], dpre)

    @pl.when(step == blocks - 1)
    def _():
        key_probs = softmax_halves(dot_nn(kmap_ref[0], kt_ref[...]))
        dpre = halves_backward(key_probs, dkf_acc[...]).astype(BF16)
        dk = dk_acc[...] * SCALE + dot_nn(kback_ref[0], dpre)
        dkt_ref[...] = dk.astype(BF16)
        dvt_ref[...] = dv_acc[...].astype(BF16)
        gkm_ref[0] = dot_nt(kt_ref[...], dpre)


def signed_maps(maps):
    turned = jnp.swapaxes(maps, 1, 2)
    return jnp.concatenate([turned, -turned], axis=1)


def attention_specs(groups, ratio, padded, block_of):
    rows = ratio * HEAD_DIM
    return [
        pl.BlockSpec((1, 1, BLOCK), lambda g, i, *_: (0, 0, block_of(i))),
        pl.BlockSpec((rows, BLOCK), lambda g, i, *_: (g, block_of(i))),
        pl.BlockSpec((HEAD_DIM, padded), lambda g, i, *_: (g, 0)),
        pl.BlockSpec((HEAD_DIM, padded), lambda g, i, *_: (groups + g, 0)),
        pl.BlockSpec((ratio, 2 * HEAD_DIM, HEAD_DIM), lambda g, i, *_: (g, 0, 0)),
        pl.BlockSpec((1, 2 * HEAD_DIM, HEAD_DIM), lambda g, i, *_: (g, 0, 0)),
    ]


def attention_forward(marks, starts, qt, kvt, qmap, kmap):
    length = qt.shape[1]
    padded = kvt.shape[1]
    groups = kmap.shape[0]
    ratio = qmap.shape[0] // groups
    rows = ratio * HEAD_DIM
    blocks = length // BLOCK
    return pl.pallas_call(
        forward_kernel,
        out_shape=(
            jax.ShapeDtypeStruct(qt.shape, BF16),
            jax.ShapeDtypeStruct((groups, ratio, length), F32),
        ),
        grid_spec=pltpu.PrefetchScalarGridSpec(
            num_scalar_prefetch=1,
            grid=(groups, blocks),
            in_specs=attention_specs(groups, ratio, padded, lambda i: i),
            out_specs=[
                pl.BlockSpec((rows, BLOCK), lambda g, i, *_: (g, i)),
                pl.BlockSpec((1, ratio, BLOCK), lambda g, i, *_: (g, 0, i)),
            ],
            scratch_shapes=[
                pltpu.VMEM((2 * HEAD_DIM, padded), BF16),
                pltpu.VMEM((padded, 2 * HEAD_DIM), BF16),
                pltpu.VMEM((padded, HEAD_DIM), BF16),
                pltpu.VMEM((HEAD_DIM, 2 * HEAD_DIM), F32),
                pltpu.VMEM((2 * HEAD_DIM, 1), F32),
            ],
        ),
        compiler_params=pltpu.CompilerParams(
            dimension_semantics=("arbitrary", "arbitrary"), vmem_limit_bytes=48 * 1024 * 1024
        ),
        cost_estimate=pl.CostEstimate(flops=1000, bytes_accessed=1000, transcendentals=0),
        name="attention_forward",
    )(marks, starts, qt, kvt, kvt, signed_maps(qmap), signed_maps(kmap))


def attention_backward(marks, starts, qt, kvt, qmap, kmap, dmt, mixt, inverse):
    length = qt.shape[1]
    padded = kvt.shape[1]
    groups = kmap.shape[0]
    ratio = qmap.shape[0] // groups
    rows = ratio * HEAD_DIM
    blocks = length // BLOCK
    back = lambda i: blocks - 1 - i
    query_spec = pl.BlockSpec((rows, BLOCK), lambda g, i, *_: (g, back(i)))
    key_spec = pl.BlockSpec((HEAD_DIM, padded), lambda g, i, *_: (g, 0))
    return pl.pallas_call(
        backward_kernel,
        out_shape=(
            jax.ShapeDtypeStruct(qt.shape, BF16),
            jax.ShapeDtypeStruct((groups * HEAD_DIM, padded), BF16),
            jax.ShapeDtypeStruct((groups * HEAD_DIM, padded), BF16),
            jax.ShapeDtypeStruct(qmap.shape, F32),
            jax.ShapeDtypeStruct(kmap.shape, F32),
        ),
        grid_spec=pltpu.PrefetchScalarGridSpec(
            num_scalar_prefetch=1,
            grid=(groups, blocks),
            in_specs=attention_specs(groups, ratio, padded, back)
            + [
                query_spec,
                query_spec,
                pl.BlockSpec((1, ratio, BLOCK), lambda g, i, *_: (g, 0, back(i))),
                pl.BlockSpec((ratio, HEAD_DIM, HEAD_DIM), lambda g, i, *_: (g, 0, 0)),
                pl.BlockSpec((1, HEAD_DIM, HEAD_DIM), lambda g, i, *_: (g, 0, 0)),
            ],
            out_specs=[
                query_spec,
                key_spec,
                key_spec,
                pl.BlockSpec((ratio, HEAD_DIM, HEAD_DIM), lambda g, i, *_: (g, 0, 0)),
                pl.BlockSpec((1, HEAD_DIM, HEAD_DIM), lambda g, i, *_: (g, 0, 0)),
            ],
            scratch_shapes=[
                pltpu.VMEM((2 * HEAD_DIM, padded), BF16),
                pltpu.VMEM((padded, 2 * HEAD_DIM), BF16),
                pltpu.VMEM((padded, HEAD_DIM), BF16),
                pltpu.VMEM((padded, HEAD_DIM), BF16),
                pltpu.VMEM((blocks, 2 * HEAD_DIM, HEAD_DIM), BF16),
                pltpu.VMEM((blocks, HEAD_DIM, 2 * HEAD_DIM), BF16),
                pltpu.VMEM((blocks, 2 * HEAD_DIM, 1), F32),
                pltpu.VMEM((HEAD_DIM, padded), F32),
                pltpu.VMEM((2 * HEAD_DIM, padded), F32),
                pltpu.VMEM((HEAD_DIM, padded), F32),
                pltpu.VMEM((2 * HEAD_DIM, HEAD_DIM), F32),
                pltpu.VMEM((HEAD_DIM, 2 * HEAD_DIM), F32),
                pltpu.VMEM((2 * HEAD_DIM, 1), F32),
            ],
        ),
        compiler_params=pltpu.CompilerParams(
            dimension_semantics=("arbitrary", "arbitrary"), vmem_limit_bytes=48 * 1024 * 1024
        ),
        cost_estimate=pl.CostEstimate(flops=1000, bytes_accessed=1000, transcendentals=0),
        name="attention_backward",
    )(
        marks, starts, qt, kvt, kvt, signed_maps(qmap), signed_maps(kmap), dmt, mixt, inverse, qmap, kmap
    )


FREE = pl.CostEstimate(flops=1000, bytes_accessed=1000, transcendentals=0)


def grid_call(kernel, name, grid, out_shape, in_specs, out_specs, scratch=(), aliases=None):
    return pl.pallas_call(
        kernel,
        out_shape=out_shape,
        grid_spec=pltpu.PrefetchScalarGridSpec(
            num_scalar_prefetch=1,
            grid=grid,
            in_specs=in_specs,
            out_specs=out_specs,
            scratch_shapes=list(scratch),
        ),
        input_output_aliases=aliases or {},
        compiler_params=pltpu.CompilerParams(
            dimension_semantics=("arbitrary",) * len(grid), vmem_limit_bytes=VMEM_LIMIT
        ),
        cost_estimate=FREE,
        name=name,
    )


MESH = pl.DeviceIdType.MESH
FAR_CHUNKS = 4


def exchange_kernel(query_cols, key_cols, *refs):
    inputs, grads, query, key, value, gate, up, down, output = refs[:9]
    thin = refs[9:15]
    far, near_other, far_other, grads_other, proj_got, gate_got, up_got, down_got, output_got = (
        refs[15:24]
    )
    thin_got = refs[24:30]
    proj_own, proj_both, output_both = refs[30:33]
    send_sem, recv_sem, local_sem, proj_all, output_all = refs[33:]
    row, col = lax.axis_index("row"), lax.axis_index("col")

    barrier = pltpu.get_barrier_semaphore()
    pl.semaphore_signal(barrier, inc=1, device_id={"row": 1 - row}, device_id_type=MESH)
    pl.semaphore_signal(barrier, inc=1, device_id={"col": 1 - col}, device_id_type=MESH)
    pl.semaphore_wait(barrier, 2)

    copies = []

    def remote(source, target, axis, place):
        n = len(copies)
        copy = pltpu.make_async_remote_copy(
            src_ref=source,
            dst_ref=target,
            send_sem=send_sem.at[n],
            recv_sem=recv_sem.at[n],
            device_id={axis: 1 - place},
            device_id_type=MESH,
        )
        copy.start()
        copies.append(copy)
        return copy

    def columns(ref, index, width):
        return ref.at[:, pl.ds(pl.multiple_of(index * width, width), width)]

    def rows_of(ref, index, height):
        return ref.at[pl.ds(pl.multiple_of(index * height, height), height), :]

    size = inputs.shape[0] // FAR_CHUNKS
    chunks = [pl.ds(i * size, size) for i in range(FAR_CHUNKS)]
    arriving = [remote(inputs.at[at, :], far.at[at, :], "row", row) for at in chunks]
    remote(inputs, near_other, "col", col)
    first = 0
    for weight, width in ((query, query_cols), (key, key_cols), (value, key_cols)):
        remote(
            columns(weight, 1 - col, width), proj_got.at[:, pl.ds(first, width)], "col", col
        )
        first += width
    for source, target in zip(thin, thin_got):
        remote(source, target, "col", col)
    remote(columns(gate, 1 - col, gate_got.shape[1]), gate_got, "col", col)
    remote(columns(up, 1 - col, up_got.shape[1]), up_got, "col", col)
    remote(rows_of(down, 1 - col, down_got.shape[0]), down_got, "col", col)
    remote(rows_of(output, 1 - col, output_got.shape[0]), output_got, "col", col)
    remote(grads, grads_other, "col", col)

    def local(source, target, n):
        copy = pltpu.make_async_copy(source, target, local_sem.at[n])
        copy.start()
        return copy

    whole = proj_own.shape[1]
    height = output_got.shape[0]
    loads, first = [], 0
    for weight, width in ((query, query_cols), (key, key_cols), (value, key_cols)):
        for side in range(2):
            loads.append(
                local(
                    columns(weight, col ^ side, width),
                    proj_all.at[:, pl.ds(side * whole + first, width)],
                    len(loads),
                )
            )
        first += width
    for side in range(2):
        loads.append(
            local(
                rows_of(output, col ^ side, height),
                output_all.at[pl.ds(side * height, height), :],
                len(loads),
            )
        )
    for copy in loads:
        copy.wait()
    stores = [
        local(proj_all.at[:, pl.ds(0, whole)], proj_own, 8),
        local(proj_all, proj_both, 9),
        local(output_all, output_both, 10),
    ]

    for copy, at in zip(arriving, chunks):
        copy.wait_recv()
        remote(far.at[at, :], far_other.at[at, :], "col", col)
    for copy in stores:
        copy.wait()
    for n, copy in enumerate(copies):
        copy.wait_send()
        if n >= FAR_CHUNKS:
            copy.wait_recv()


def exchange(inputs, grads, projections, gate, up, down, output, thin):
    query, key, value = projections
    rows, half = inputs.shape
    query_cols, key_cols = query.shape[1] // 2, key.shape[1] // 2
    columns = query_cols + 2 * key_cols
    like = lambda *shape: jax.ShapeDtypeStruct(shape, BF16)
    outs = [
        like(rows, half),
        like(rows, half),
        like(rows, half),
        like(rows, half),
        like(half, columns),
        like(half, gate.shape[1] // 2),
        like(half, up.shape[1] // 2),
        like(down.shape[0] // 2, half),
        like(output.shape[0] // 2, half),
    ]
    outs += [jax.ShapeDtypeStruct(values.shape, values.dtype) for values in thin]
    outs += [like(half, columns), like(half, 2 * columns), like(output.shape[0], half)]
    copies = 2 * FAR_CHUNKS + 1 + 3 + len(thin) + 5
    return pl.pallas_call(
        functools.partial(exchange_kernel, query_cols, key_cols),
        out_shape=tuple(outs),
        in_specs=[pl.BlockSpec(memory_space=pl.ANY)] * (9 + len(thin)),
        out_specs=tuple([pl.BlockSpec(memory_space=pl.ANY)] * len(outs)),
        scratch_shapes=[
            pltpu.SemaphoreType.DMA((copies,)),
            pltpu.SemaphoreType.DMA((copies,)),
            pltpu.SemaphoreType.DMA((11,)),
            pltpu.VMEM((half, 2 * columns), BF16),
            pltpu.VMEM(output.shape, BF16),
        ],
        compiler_params=pltpu.CompilerParams(
            collective_id=0, has_side_effects=True, vmem_limit_bytes=VMEM_LIMIT
        ),
        cost_estimate=FREE,
        name="exchange",
    )(inputs, grads, query, key, value, gate, up, down, output, *thin)


def hidden_grad_kernel(place_ref, gm_own, go_own, gm_far, go_far, down_own, down_got, out_ref):
    half = gm_own.shape[0]
    out_ref[:half] = (
        dot_nt(gm_own[...], down_own[...]) + dot_nt(go_own[...], down_got[...])
    ).astype(BF16)
    out_ref[half:] = (
        dot_nt(gm_far[...], down_own[...]) + dot_nt(go_far[...], down_got[...])
    ).astype(BF16)


def hidden_grad(place, grads, down_weight, down_got):
    half, width = grads[0].shape
    hidden_cols = down_got.shape[0]
    tiles = hidden_cols // MLP_TILE
    whole = pl.BlockSpec((half, width), lambda i, s: (0, 0))
    return grid_call(
        hidden_grad_kernel,
        "hidden_grad",
        (tiles,),
        jax.ShapeDtypeStruct((2 * half, hidden_cols), BF16),
        [whole] * 4
        + [
            pl.BlockSpec((MLP_TILE, width), lambda i, s: (s[0] * tiles + i, 0)),
            pl.BlockSpec((MLP_TILE, width), lambda i, s: (i, 0)),
        ],
        pl.BlockSpec((2 * half, MLP_TILE), lambda i, s: (0, i)),
    )(place, *grads, down_weight, down_got)


def project_kernel(
    place_ref, mine_ref, other_ref, gain_ref, proj_own, proj_got, down_ref, up_ref, *refs
):
    normed_ref, queries_ref, keys_ref, adapters_ref, scale_ref = refs[-5:]
    half = mine_ref.shape[1]
    mine, other = mine_ref[...].astype(F32), other_ref[...].astype(F32)
    squares = jnp.sum(mine * mine, axis=1, keepdims=True) + jnp.sum(
        other * other, axis=1, keepdims=True
    )
    scale = lax.rsqrt(squares / (2 * half) + norm_eps)
    left = (mine * scale * gain_ref[:, :half]).astype(BF16)
    right = (other * scale * gain_ref[:, half:]).astype(BF16)
    normed_ref[:, :half] = left
    normed_ref[:, half:] = right
    scale_ref[...] = scale
    adapters = (dot_nn(left, down_ref[:half]) + dot_nn(right, down_ref[half:])).astype(BF16)
    adapters_ref[...] = adapters
    sums = dot_nn(left, proj_own[...]) + dot_nn(right, proj_got[...]) + dot_nn(adapters, up_ref[...])
    turned = jnp.transpose(sums.astype(BF16))
    rows = queries_ref.shape[0]
    queries_ref[...] = turned[:rows]
    keys_ref[...] = turned[rows:]


def global_block(local, flip, half_blocks):
    return ((local // half_blocks) ^ flip) * half_blocks + local % half_blocks


def project_block(index, place, mine, other, gain, proj_own, proj_got, down, up, query_part, kept):
    rows, half = mine.shape
    length = 2 * half_rows_of(kept, rows)
    blocks, half_blocks = length // BLOCK, length // BLOCK // 2
    columns = proj_own.shape[1]
    whole = lambda values: pl.BlockSpec(values.shape, lambda i, s: (0, 0))
    lanes = lambda i, s: (0, global_block(index + i, s[1], half_blocks))
    local = lambda i, s: (index + i, 0)
    shapes = (
        jax.ShapeDtypeStruct((length, 2 * half), BF16),
        jax.ShapeDtypeStruct((query_part, length), BF16),
        jax.ShapeDtypeStruct((columns - query_part, length), BF16),
        jax.ShapeDtypeStruct((length, LANES), BF16),
        jax.ShapeDtypeStruct((length, 1), F32),
    )
    return grid_call(
        project_kernel,
        "project_block",
        (rows // BLOCK,),
        shapes,
        [
            pl.BlockSpec((BLOCK, half), lambda i, s: (i, 0)),
            pl.BlockSpec((BLOCK, half), lambda i, s: (i, 0)),
            whole(gain),
            whole(proj_own),
            whole(proj_got),
            whole(down),
            whole(up),
        ]
        + [pl.BlockSpec(memory_space=pl.ANY)] * len(kept),
        [
            pl.BlockSpec((BLOCK, 2 * half), local),
            pl.BlockSpec((query_part, BLOCK), lanes),
            pl.BlockSpec((columns - query_part, BLOCK), lanes),
            pl.BlockSpec((BLOCK, LANES), local),
            pl.BlockSpec((BLOCK, 1), local),
        ],
        aliases={8 + i: i for i in range(len(kept))},
    )(place, mine, other, gain, proj_own, proj_got, down, up, *kept)


def half_rows_of(kept, rows):
    return kept[0].shape[0] // 2 if kept else rows


def mlp_kernel(
    count,
    place_ref,
    in_mine,
    in_other,
    at_mine,
    at_other,
    far_mine,
    far_other,
    adapter_ref,
    up_ref,
    gain_ref,
    gate_own,
    gate_got,
    up_own,
    up_got,
    dh_ref,
    *refs,
):
    hidden_ref, dgate_ref, dup_ref, normed_ref, scale_ref = refs[-1 - count : -1][:5]
    left_ref = refs[-1]
    half = in_mine.shape[1]

    @pl.when(pl.program_id(0) == 0)
    def _():
        def state(inputs, own, far, adapted):
            return inputs[...].astype(F32) + (
                own[...].astype(F32) + far[...].astype(F32) + adapted
            )

        adapter = adapter_ref[...]
        mine = state(in_mine, at_mine, far_mine, dot_nn(adapter, up_ref[:, :half]))
        other = state(in_other, at_other, far_other, dot_nn(adapter, up_ref[:, half:]))
        squares = jnp.sum(mine * mine, axis=1, keepdims=True) + jnp.sum(
            other * other, axis=1, keepdims=True
        )
        scale = lax.rsqrt(squares / (2 * half) + norm_eps)
        scale_ref[...] = scale
        if count == 6:
            refs[-2][...] = mine
        left_ref[:, :half] = (mine * scale * gain_ref[:, :half]).astype(BF16)
        left_ref[:, half:] = (other * scale * gain_ref[:, half:]).astype(BF16)
        normed_ref[...] = left_ref[...]

    left, right = left_ref[:, :half], left_ref[:, half:]
    gate = dot_nn(left, gate_own[...]) + dot_nn(right, gate_got[...])
    up = dot_nn(left, up_own[...]) + dot_nn(right, up_got[...])
    d_hidden = dh_ref[...].astype(F32)
    sig = 1.0 / (1.0 + jnp.exp(-gate))
    silu = gate * sig
    hidden_ref[...] = (silu * up).astype(BF16)
    dup_ref[...] = (d_hidden * silu).astype(BF16)
    dgate_ref[...] = (d_hidden * up * (sig * (1.0 + gate * (1.0 - sig)))).astype(BF16)


def mlp_block(
    index,
    place,
    inputs,
    input_block,
    attended,
    adapter,
    output_up,
    gain,
    gate_weight,
    gate_got,
    up_weight,
    up_got,
    d_hidden,
    kept,
    state_kept,
    with_state,
):
    half, hidden_cols = gate_got.shape
    width = 2 * half
    length = d_hidden.shape[0]
    tiles = hidden_cols // MLP_TILE
    own_spec = pl.BlockSpec((half, MLP_TILE), lambda i, s: (0, s[0] * tiles + i))
    got_spec = pl.BlockSpec((half, MLP_TILE), lambda i, s: (0, i))
    kept_spec = pl.BlockSpec((BLOCK, MLP_TILE), lambda i, s: (index, i))
    here = lambda columns: pl.BlockSpec((BLOCK, columns), lambda i, s: (index, 0))
    whole = lambda values: pl.BlockSpec(values.shape, lambda i, s: (0, 0))
    input_spec = pl.BlockSpec((BLOCK, half), lambda i, s: (input_block, 0))
    block_spec = pl.BlockSpec((BLOCK, half), lambda i, s: (0, 0))
    shapes = (jax.ShapeDtypeStruct((length, hidden_cols), BF16),) * 3 + (
        jax.ShapeDtypeStruct((length, width), BF16),
        jax.ShapeDtypeStruct((length, 1), F32),
    )
    out_specs = [kept_spec] * 3 + [here(width), here(1)]
    aliases = {15 + i: i for i in range(len(kept))}
    passed = tuple(kept)
    if with_state:
        shapes += (jax.ShapeDtypeStruct((length // 2, half), F32),)
        out_specs.append(here(half))
        if state_kept is not None:
            aliases[15 + len(passed)] = 5
            passed += (state_kept,)
    return grid_call(
        functools.partial(mlp_kernel, len(shapes)),
        "mlp_block",
        (tiles,),
        shapes,
        [input_spec, input_spec]
        + [block_spec] * 4
        + [here(adapter.shape[1]), whole(output_up), whole(gain)]
        + [own_spec, got_spec, own_spec, got_spec, kept_spec]
        + [pl.BlockSpec(memory_space=pl.ANY)] * len(passed),
        out_specs,
        [pltpu.VMEM((BLOCK, width), BF16)],
        aliases,
    )(
        place,
        *inputs,
        *attended,
        adapter,
        output_up,
        gain,
        gate_weight,
        gate_got,
        up_weight,
        up_got,
        d_hidden,
        *passed,
    )


def norm_back_kernel(
    count,
    place_ref,
    total_mine,
    total_other,
    normed_ref,
    scale_ref,
    grad_mine,
    grad_other,
    gain_ref,
    out_own,
    out_got,
    up_ref,
    down_ref,
    *refs,
):
    mixed_ref, mine_ref, adapter_ref, gain_sum = refs[-count:][:4]
    half = total_mine.shape[1]
    gain_left, gain_right = gain_ref[:, :half], gain_ref[:, half:]
    d_left, d_right = total_mine[...].astype(F32), total_other[...].astype(F32)
    hat_left = normed_ref[:, :half].astype(F32) * (1.0 / gain_left)
    hat_right = normed_ref[:, half:].astype(F32) * (1.0 / gain_right)
    term = jnp.sum(d_left * hat_left, axis=0, keepdims=True)
    g_left, g_right = d_left * gain_left, d_right * gain_right
    inner = (
        jnp.sum(g_left * hat_left, axis=1, keepdims=True)
        + jnp.sum(g_right * hat_right, axis=1, keepdims=True)
    ) / (2 * half)
    scale = scale_ref[...]
    left = grad_mine[...].astype(F32) + scale * (g_left - hat_left * inner)
    right = grad_other[...].astype(F32) + scale * (g_right - hat_right * inner)
    if count == 5:
        refs[-1][...] = left
    left, right = left.astype(BF16), right.astype(BF16)
    mine_ref[...] = left
    adapter = (dot_nt(left, up_ref[:, :half]) + dot_nt(right, up_ref[:, half:])).astype(BF16)
    adapter_ref[...] = adapter
    mixed_ref[...] = (
        dot_nt(out_own[...], left) + dot_nt(out_got[...], right) + dot_nt(down_ref[...], adapter)
    ).astype(BF16)

    @pl.when(pl.program_id(0) == 0)
    def _():
        gain_sum[...] = term

    @pl.when(pl.program_id(0) > 0)
    def _():
        gain_sum[...] += term


def norm_back(
    index, place, totals, normed, scale, grads, gain, out_own, out_got, up, down, kept, with_state
):
    half_rows, half = totals[0].shape
    length = 2 * half_rows
    half_blocks = half_rows // BLOCK
    heads = out_own.shape[0]
    base = index * half_blocks
    whole = lambda values: pl.BlockSpec(values.shape, lambda i, s: (0, 0))
    near = pl.BlockSpec((BLOCK, half), lambda i, s: (i, 0))
    here = lambda columns: pl.BlockSpec((BLOCK, columns), lambda i, s: (base + i, 0))
    shapes = (
        jax.ShapeDtypeStruct((heads, length), BF16),
        jax.ShapeDtypeStruct((length, half), BF16),
        jax.ShapeDtypeStruct((length, LANES), BF16),
        jax.ShapeDtypeStruct((1, half), F32),
    )
    out_specs = [
        pl.BlockSpec((heads, BLOCK), lambda i, s: (0, global_block(base + i, s[1], half_blocks))),
        here(half),
        here(LANES),
        pl.BlockSpec((1, half), lambda i, s: (0, 0)),
    ]
    if with_state:
        shapes += (jax.ShapeDtypeStruct((half_rows, half), F32),)
        out_specs.append(near)
    return grid_call(
        functools.partial(norm_back_kernel, len(shapes)),
        "norm_back",
        (half_blocks,),
        shapes,
        [near, near, here(2 * half), here(1), near, near]
        + [whole(values) for values in (gain, out_own, out_got, up, down)]
        + [pl.BlockSpec(memory_space=pl.ANY)] * len(kept),
        out_specs,
        aliases={12 + i: i for i in range(len(kept))},
    )(place, *totals, normed, scale, *grads, gain, out_own, out_got, up, down, *kept)


def second_grad_kernel(
    place_ref, dg_ref, du_ref, gate_own, gate_got, up_own, up_got, own_ref, other_ref
):
    own_ref[...] = (dot_nt(dg_ref[...], gate_own[...]) + dot_nt(du_ref[...], up_own[...])).astype(
        BF16
    )
    other_ref[...] = (
        dot_nt(dg_ref[...], gate_got[...]) + dot_nt(du_ref[...], up_got[...])
    ).astype(BF16)


def second_grad(index, place, d_gate, d_up, gate_weight, gate_got, up_weight, up_got):
    half, hidden_cols = gate_got.shape
    tile = min(SUM_TILE, half)
    rows = d_gate.shape[0] // 2
    left = pl.BlockSpec((rows, hidden_cols), lambda i, s: (index, 0))
    own_spec = pl.BlockSpec((tile, hidden_cols), lambda i, s: (i, s[0]))
    got_spec = pl.BlockSpec((tile, hidden_cols), lambda i, s: (i, 0))
    out_spec = pl.BlockSpec((rows, tile), lambda i, s: (0, i))
    return grid_call(
        second_grad_kernel,
        "second_grad",
        (half // tile,),
        (jax.ShapeDtypeStruct((rows, half), BF16),) * 2,
        [left, left, own_spec, got_spec, own_spec, got_spec],
        [out_spec, out_spec],
    )(place, d_gate, d_up, gate_weight, gate_got, up_weight, up_got)


def down_kernel(place_ref, hidden_ref, down_own, down_got, own_ref, other_ref):
    own_ref[...] = dot_nn(hidden_ref[...], down_own[...]).astype(BF16)
    other_ref[...] = dot_nn(hidden_ref[...], down_got[...]).astype(BF16)


def down_product(place, hidden, down_weight, down_got):
    length, hidden_cols = hidden.shape
    half = down_got.shape[1]
    tile = min(SUM_TILE, half)
    out_spec = pl.BlockSpec((length, tile), lambda i, s: (0, i))
    return grid_call(
        down_kernel,
        "down_product",
        (half // tile,),
        (jax.ShapeDtypeStruct((length, half), BF16),) * 2,
        [
            pl.BlockSpec((length, hidden_cols), lambda i, s: (0, 0)),
            pl.BlockSpec((hidden_cols, tile), lambda i, s: (s[0], i)),
            pl.BlockSpec((hidden_cols, tile), lambda i, s: (0, i)),
        ],
        [out_spec, out_spec],
    )(place, hidden, down_weight, down_got)


def weight_grad_kernel(sets, chunks, pieces, turned, right_turned, place_ref, *refs):
    outs = refs[-1 - pieces * sets : -1]
    right_ref, left_ref = refs[-2 - pieces * sets], refs[-1]
    lefts = refs[: -2 - pieces * sets]
    length = left_ref.shape[1]
    rows = left_ref.shape[0] // sets
    count = rows // LANES

    @pl.when(pl.program_id(0) == 0)
    def _():
        for p in range(sets * count):
            lanes = slice(p * LANES, (p + 1) * LANES)
            if turned:
                left_ref[lanes, :] = lefts[p][...]
            else:
                size = length // chunks
                for i in range(chunks):
                    left_ref[lanes, i * size : (i + 1) * size] = jnp.transpose(
                        lefts[p * chunks + i][...]
                    )

    for which in range(sets):
        left = left_ref[which * rows : (which + 1) * rows, :]
        sums = (dot_nt if right_turned else dot_nn)(left, right_ref[...])
        size = rows // pieces
        for i in range(pieces):
            outs[pieces * which + i][...] = sums[i * size : (i + 1) * size].astype(BF16)


def weight_grad(places, sets, right, pieces=2, turned=False, right_turned=False):
    chunks = len(sets[0][0])
    length = sets[0][0][0].shape[1] if turned else sum(c.shape[0] for c in sets[0][0])
    count = (places.shape[0] - 2) // len(sets)
    columns = right.shape[0] if right_turned else right.shape[1]
    tile = min(GRAD_TILE, columns)
    in_specs, operands = [], []
    for n, (lefts, base) in enumerate(sets):
        for p in range(count):
            at = 2 + n * count + p
            for left in lefts:
                if turned:
                    spec = pl.BlockSpec((LANES, length), lambda j, s, at=at: (s[at], 0))
                else:
                    spec = pl.BlockSpec(
                        (left.shape[0], LANES), lambda j, s, at=at, base=base: (0, base + s[at])
                    )
                in_specs.append(spec)
                operands.append(left)
    if right_turned:
        in_specs.append(pl.BlockSpec((tile, length), lambda j, s: (j, 0)))
    else:
        in_specs.append(pl.BlockSpec((length, tile), lambda j, s: (0, j)))
    size = count * LANES // pieces
    out_spec = pl.BlockSpec((size, tile), lambda j, s: (0, j))
    return grid_call(
        functools.partial(weight_grad_kernel, len(sets), chunks, pieces, turned, right_turned),
        "weight_grad",
        (columns // tile,),
        (jax.ShapeDtypeStruct((size, columns), BF16),) * (pieces * len(sets)),
        in_specs,
        [out_spec] * (pieces * len(sets)),
        [pltpu.VMEM((len(sets) * count * LANES, length), BF16)],
    )(places, *operands, right)


def after(value, *others):
    return lax.optimization_barrier((value,) + others)[0]


def swap(values, axis):
    return lax.ppermute(values, axis, [(0, 1), (1, 0)])


def part(values, index, count, axis):
    width = values.shape[axis] // count
    return lax.dynamic_slice_in_dim(values, index * width, width, axis)


def contract(left, right, left_dim, right_dim):
    return lax.dot_general(
        left, right, (((left_dim,), (right_dim,)), ((), ())), preferred_element_type=F32
    )


def exchange_order(bits, first):
    return [(first + k) % bits for k in range(bits)]


def relative_index(position, order):
    bits = len(order)
    return sum(((position >> (bits - 1 - k)) & 1) << order[k] for k in range(bits))


def relative_blocks(values, axis, device, order):
    count = 1 << len(order)
    return jnp.concatenate(
        [part(values, device ^ relative_index(p, order), count, axis) for p in range(count)],
        axis=axis,
    )


class Reduction:
    def __init__(self, keep, send, size, order):
        self.keep, self.size, self.order, self.step = keep, size, order, 0
        self.launch(send)

    def launch(self, send):
        bit = 1 << self.order[self.step]
        self.got = lax.ppermute(send, "dp", [(i, i ^ bit) for i in range(self.size)])

    def combine(self):
        got = self.got
        self.step += 1
        if self.step == len(self.order):
            self.keep = self.keep.astype(F32) + got.astype(F32)
            return self.keep
        half = self.keep.shape[0] // 2
        sums = (
            (self.keep[rows].astype(F32) + got[rows].astype(F32)).astype(BF16)
            for rows in (slice(0, half), slice(half, 2 * half))
        )
        self.keep, send = sums
        self.launch(send)
        return self.keep

    @property
    def done(self):
        return self.step == len(self.order)


def total_over(values, size, bits):
    for k in range(bits):
        values = values + lax.ppermute(values, "dp", [(i, i ^ (1 << k)) for i in range(size)])
    return values


def ordered(own, other, index, axis):
    return jnp.where(
        index == 0,
        jnp.concatenate([own, other], axis=axis),
        jnp.concatenate([other, own], axis=axis),
    )


def on_device(
    activations,
    grad_out,
    segments,
    first_gain,
    query_weight,
    key_weight,
    value_weight,
    query_down,
    query_up,
    key_down,
    key_up,
    value_down,
    value_up,
    query_map,
    key_map,
    output_weight,
    output_down,
    output_up,
    second_gain,
    gate_weight,
    up_weight,
    down_weight,
):
    size = lax.axis_size("dp")
    bits = size.bit_length() - 1
    device = lax.axis_index("dp")
    row = lax.axis_index("row")
    col = lax.axis_index("col")
    seq_rows = segments.shape[1]
    half_rows, feature_cols = activations.shape
    width = 2 * feature_cols
    blocks = seq_rows // BLOCK
    half_blocks = blocks // 2
    rank = query_down.shape[1]
    query_part = query_weight.shape[1] // 2
    key_part = key_weight.shape[1] // 2
    part_cols = query_part + 2 * key_part
    order = exchange_order(bits, 0)
    turned_order = exchange_order(bits, 1)

    def other_half(values, axis):
        return jnp.roll(values, values.shape[axis] // 2, axis)

    def sequence_order(values, axis):
        return jnp.where(row == 0, values, other_half(values, axis))

    def rows_of(index):
        return slice(index * BLOCK, (index + 1) * BLOCK)

    lane_blocks = feature_cols // LANES
    direct = lane_blocks == size

    def block_order(which, rows_of_pair=False):
        if not direct:
            return [jnp.int32(p) for p in range(lane_blocks)]
        blocks_of = [device ^ relative_index(p, which) for p in range(size)]
        if rows_of_pair:
            return [((b // (size // 2)) ^ col) * (size // 2) + b % (size // 2) for b in blocks_of]
        return blocks_of

    def places(*orders, rows_of_pair=False):
        entries = [col, row]
        for which in orders:
            entries += block_order(which, rows_of_pair)
        return jnp.stack([jnp.asarray(v, jnp.int32) for v in entries])

    place = places(order)

    def grads_of(sets, right, orders, right_turned=False):
        if not direct:
            sets = [
                (
                    [
                        relative_blocks(
                            left[:, base * LANES : base * LANES + feature_cols], 1, device, which
                        )
                        for left in lefts
                    ],
                    0,
                )
                for (lefts, base), which in zip(sets, orders)
            ]
        outs = weight_grad(places(*orders), sets, right, 2, False, right_turned)
        return [outs[2 * n : 2 * n + 2] for n in range(len(sets))]

    def ups(index):
        zeros_key = jnp.zeros((rank, key_part), BF16)
        zeros_query = jnp.zeros((rank, query_part), BF16)
        return jnp.concatenate(
            [
                jnp.concatenate([part(query_up, index, 2, 1), zeros_key, zeros_key], axis=1),
                jnp.concatenate([zeros_query, part(key_up, index, 2, 1), zeros_key], axis=1),
                jnp.concatenate([zeros_query, zeros_key, part(value_up, index, 2, 1)], axis=1),
            ],
            axis=0,
        )

    (
        inputs_far,
        inputs_other,
        inputs_far_other,
        grads_other,
        proj_got,
        gate_got,
        up_got,
        mlp_down_got,
        output_got,
        first_gain_got,
        second_gain_got,
        query_down_got,
        key_down_got,
        value_down_got,
        output_up_got,
        proj_own,
        proj_native,
        output_native,
    ) = exchange(
        activations,
        grad_out,
        (query_weight, key_weight, value_weight),
        gate_weight,
        up_weight,
        down_weight,
        output_weight,
        (first_gain, second_gain, query_down, key_down, value_down, output_up),
    )
    grads_far = swap(after(grad_out, inputs_far), "row")
    up_own = ups(col)
    up_native = jnp.concatenate([up_own, ups(1 - col)], axis=1)
    down_own = jnp.concatenate([query_down, key_down, value_down], axis=1)
    down_got = jnp.concatenate([query_down_got, key_down_got, value_down_got], axis=1)
    down_full = jnp.concatenate([down_own, down_got], axis=0)
    down_full = jnp.pad(down_full, ((0, 0), (0, LANES - 3 * rank)))
    up_padded = jnp.pad(up_own, ((0, LANES - 3 * rank), (0, 0)))
    gain_full = jnp.concatenate([first_gain, first_gain_got])[None]
    second_gain_full = jnp.concatenate([second_gain, second_gain_got])[None]
    output_up_full = jnp.concatenate([output_up, output_up_got], axis=1)
    output_up_full = jnp.pad(output_up_full, ((0, LANES - rank), (0, 0)))
    output_rows_own = part(output_weight, col, 2, 0)
    output_down_own = part(output_down, col, 2, 0)
    output_down_native = jnp.concatenate(
        [output_down_own, part(output_down, 1 - col, 2, 0)], axis=0
    )
    output_down_padded = jnp.pad(output_down_own, ((0, 0), (0, LANES - rank)))
    query_map_own = part(query_map, col, 2, 0)
    key_map_own = part(key_map, col, 2, 0)

    documents = segments[0]
    starts = jnp.sum((documents[None, :] < documents[:, None]).astype(jnp.int32), axis=1)
    marks = jnp.concatenate(
        [jnp.full((1,), seq_rows, jnp.int32), starts[BLOCK - WINDOW - 1 :: BLOCK]]
    )
    starts = starts.reshape(1, 1, seq_rows)

    def project(index, mine, other, kept):
        return project_block(
            index,
            place,
            mine,
            other,
            gain_full,
            proj_own,
            proj_got,
            down_full,
            up_padded,
            query_part,
            kept,
        )

    kept = project(0, activations, inputs_other, ())
    kept = project(half_blocks, inputs_far, inputs_far_other, kept)
    normed_first, queries, keys_values, adapters, first_scale = kept
    keys_values = jnp.pad(keys_values, ((0, 0), (WINDOW, WINDOW)))
    mixed, inverse = attention_forward(
        marks, starts, queries, keys_values, query_map_own, key_map_own
    )

    mixed, grads_far = lax.optimization_barrier((mixed, grads_far))
    mixed_local = sequence_order(mixed, 1)
    mixed_pair = jnp.concatenate([mixed_local, swap(mixed_local, "col")], axis=0)
    adapter_sum = contract(mixed_pair, output_down_native, 0, 0)
    adapter_far = swap(other_half(adapter_sum, 0), "row")
    grads_far_other = swap(after(grads_far, mixed), "col")
    send_order = [(b + half_blocks) % blocks for b in range(blocks)]
    attended, attended_far = [None] * blocks, [None] * blocks
    pair = after(mixed_pair, grads_far)
    for b in send_order:
        attended[b] = contract(pair[:, rows_of(b)], output_native, 0, 0).astype(BF16)
        attended_far[send_order[b]] = swap(after(attended[b], adapter_far), "row")
        pair = after(pair, attended[b])
    out_adapter = (adapter_sum + adapter_far).astype(BF16)
    adapter_padded = jnp.pad(out_adapter, ((0, 0), (0, LANES - rank)))
    attended_other = [swap(attended[0], "col")] + [None] * (blocks - 1)
    d_hidden = hidden_grad(
        place,
        [after(grad_out, *attended, adapter_padded), grads_other, grads_far, grads_far_other],
        down_weight,
        mlp_down_got,
    )

    clock = (d_hidden,)
    kept, state = (), None
    for b in range(blocks):
        far = after(attended_far[b], *clock)
        far_other = swap(far, "col")
        if b + 1 < blocks:
            attended_other[b + 1] = swap(after(attended[b + 1], far), "col")
        inputs = (
            (activations, inputs_other)
            if b < half_blocks
            else (inputs_far, inputs_far_other)
        )
        outs = mlp_block(
            b,
            place,
            inputs,
            b % half_blocks,
            (attended[b], attended_other[b], far, far_other),
            adapter_padded,
            output_up_full,
            second_gain_full,
            gate_weight,
            gate_got,
            up_weight,
            up_got,
            d_hidden,
            kept,
            state,
            b < half_blocks,
        )
        kept = outs[:5]
        state = outs[5] if b < half_blocks else state
        clock = (kept[0],)
    hidden, d_gate, d_up, second_normed, second_scale = kept

    sums = {}

    def reduction(name, pair, which):
        sums[name] = Reduction(*pair, size, which)

    def given(pair, clock):
        return [swap(after(values, *clock), "col") for values in pair]

    def settle(clock, *names):
        for name in names:
            sums[name].got = after(sums[name].got, *clock)
            clock = (sums[name].combine(),)
        return clock

    def scattered(values):
        return lax.psum_scatter(values, "dp", scatter_dimension=0, tiled=True).astype(F32)

    natural = jnp.stack(
        [jnp.asarray(v, jnp.int32) for v in [col, row] + 2 * list(range(lane_blocks))]
    )
    both = [([second_normed], 0), ([second_normed], lane_blocks)]
    own_gate, other_gate = weight_grad(natural, both, d_gate, 1)
    grad_gate_own = scattered(own_gate)
    got_gate = swap(other_gate, "col")
    own_down, other_down = grads_of(
        [([grad_out, grads_far], 0), ([grads_other, grads_far_other], 0)],
        after(hidden, own_gate, got_gate),
        (order, turned_order),
    )
    reduction("down_own", own_down, order)
    down_given = given(other_down, ())

    def half_second(index, *clock):
        own, other = second_grad(
            index, place, after(d_gate, *clock), d_up, gate_weight, gate_got, up_weight, up_got
        )
        got = swap(other, "col")
        return (own.astype(F32) + got.astype(F32)).astype(BF16)

    chip_far = half_second(1, own_down[0])
    reduction("down_got", [after(v, chip_far) for v in down_given], turned_order)
    far_got_own = swap(chip_far, "row")
    chip_own = half_second(0, chip_far)
    far_got_far = swap(chip_own, "row")
    grad_gate_got = scattered(after(got_gate, chip_own))
    own_up, other_up = weight_grad(natural, both, after(d_up, chip_own), 1)
    got_up = swap(other_up, "col")
    y_own, y_other = down_product(place, after(hidden, own_up), down_weight, mlp_down_got)
    clock = settle((y_own,), "down_own", "down_got")

    y_got = swap(y_other, "col")
    totals = []
    for chip, got in ((chip_own, far_got_own), (chip_far, far_got_far)):
        total = (chip.astype(F32) + after(got, *clock).astype(F32)).astype(BF16)
        totals.append(total)
        clock = (total,)
    totals = [(total, swap(after(total, *clock), "col")) for total in totals]

    def back(index, grads, kept):
        return norm_back(
            index,
            place,
            totals[index],
            second_normed,
            second_scale,
            grads,
            second_gain_full,
            output_rows_own,
            output_got,
            output_up_full,
            output_down_padded,
            kept,
            index == 0,
        )

    outs = back(0, (grad_out, grads_other), ())
    kept, gain_sum, grad_state = outs[:3], outs[3], outs[4]
    grad_up_own = scattered(after(own_up, kept[0]))
    outs = back(1, (grads_far, grads_far_other), kept)
    kept = outs[:3]
    d_mixed, d_mine, d_out_padded = kept
    grad_second_gain = (gain_sum + outs[3])[0]
    d_out_adapter = d_out_padded[:, :rank]
    y_send = (y_own[half_rows:].astype(F32) + y_got[half_rows:].astype(F32)).astype(BF16)
    y_far = swap(y_send, "row")
    lefts = mixed_pair
    if not direct:
        lefts = relative_blocks(
            ordered(mixed_local, mixed_pair[query_part:], col, 0), 0, device, order
        )
    output_pair = weight_grad(
        places(order, rows_of_pair=True), [([lefts], 0)], after(d_mine, y_send), 2, True
    )
    reduction("output", output_pair, order)
    clock = (output_pair[0],)

    d_queries, d_keys, d_values, grad_query_map, grad_key_map = attention_backward(
        marks,
        starts,
        queries,
        keys_values,
        query_map_own,
        key_map_own,
        after(d_mixed, *clock),
        mixed,
        inverse,
    )
    clock = settle((d_queries,), "down_own", "down_got", "output")
    d_queries = after(d_queries, y_far, *clock)
    grad_up_got = scattered(after(got_up, d_queries))

    d_projected = sequence_order(
        jnp.concatenate(
            [
                d_queries,
                d_keys[:, WINDOW : WINDOW + seq_rows],
                d_values[:, WINDOW : WINDOW + seq_rows],
            ],
            axis=0,
        ),
        1,
    )
    d_pair = jnp.concatenate([d_projected, swap(d_projected, "col")], axis=0)
    adapter_sum = contract(up_native, d_pair, 1, 0)
    adapter_far = swap(other_half(adapter_sum, 1), "row")
    inverse_first = 1.0 / first_gain
    hat_near = normed_first[:half_rows, :feature_cols]
    hat_far = normed_first[half_rows:, :feature_cols]
    d_first_far = contract(d_pair[:, half_rows:], proj_native, 0, 1)
    gain_far = jnp.sum(d_first_far * hat_far.astype(F32), axis=0)
    d_first_far = swap(d_first_far.astype(BF16), "row")
    (proj_pair,) = grads_of([([normed_first], 0)], after(d_pair, gain_far), (order,), True)
    reduction("proj", proj_pair, order)
    d_adapter = (adapter_sum + after(adapter_far, proj_pair[0])).astype(BF16)
    d_first = contract(d_pair[:, :half_rows], proj_native, 0, 1) + contract(
        d_adapter[:, :half_rows], down_own, 0, 1
    )
    grad_first_gain = (
        gain_far + jnp.sum(d_first * hat_near.astype(F32), axis=0)
    ) * inverse_first
    grad_first_gain = grad_first_gain + swap(grad_first_gain, "row")
    clock = ()
    grad_down = contract(d_adapter, normed_first[:, :feature_cols], 1, 0)
    grad_up = contract(adapters[:, : 3 * rank], d_projected, 0, 1)
    grad_output_up = contract(out_adapter, d_mine, 0, 0)
    grad_output_down = contract(d_out_adapter, mixed_local, 0, 1)
    small = (
        grad_first_gain,
        grad_second_gain,
        grad_output_up,
        grad_down,
        grad_output_down,
        grad_up[:rank, :query_part],
        grad_up[rank : 2 * rank, query_part : query_part + key_part],
        grad_up[2 * rank :, query_part + key_part :],
        grad_query_map,
        grad_key_map,
    )
    flat = [values.reshape(-1, LANES) for values in small]
    packed = total_over(jnp.concatenate(flat, axis=0), size, bits)
    shared_rows = sum(values.shape[0] for values in flat[:4])
    packed_other = swap(packed[shared_rows:], "col")

    result = (
        state
        + (y_own[:half_rows].astype(F32) + y_got[:half_rows].astype(F32))
        + y_far.astype(F32)
    ).astype(BF16)
    d_first = d_first + after(d_first_far, d_first, result, *clock).astype(F32)
    first_scale = first_scale[:half_rows]
    hat_own = activations.astype(F32) * first_scale
    grad_hat = d_first * first_gain
    inner = jnp.sum(grad_hat * hat_own, axis=1)
    inner = ((inner + swap(inner, "col")) / width)[:, None]
    grad_activations = grad_state + first_scale * (
        grad_hat - hat_own * inner
    )
    clock = (grad_activations,)
    waiting = FINISH_ORDER
    while any(not sums[name].done for name in waiting):
        for name in waiting:
            if not sums[name].done:
                clock = settle(clock, name)

    def unpacked(index, source, base):
        first = sum(values.shape[0] for values in flat[:index]) - base
        return source[first : first + flat[index].shape[0]].reshape(small[index].shape)

    def joined(index, axis):
        return ordered(
            unpacked(index, packed, 0), unpacked(index, packed_other, shared_rows), col, axis
        )

    down_total = jnp.transpose(unpacked(3, packed, 0))
    grad_proj = sums["proj"].keep
    proj_grads = [
        ordered(
            grad_proj[:, first : first + count],
            grad_proj[:, part_cols + first : part_cols + first + count],
            col,
            1,
        )
        for first, count in (
            (0, query_part),
            (query_part, key_part),
            (query_part + key_part, key_part),
        )
    ]

    grad_gate = ordered(grad_gate_own, grad_gate_got, col, 1)
    grad_up_weight = ordered(grad_up_own, grad_up_got, col, 1)
    grad_down_weight = ordered(sums["down_own"].keep, sums["down_got"].keep, col, 1)
    return (
        result,
        grad_activations,
        unpacked(0, packed, 0),
        proj_grads[0],
        proj_grads[1],
        proj_grads[2],
        down_total[:, :rank],
        joined(5, 1),
        down_total[:, rank : 2 * rank],
        joined(6, 1),
        down_total[:, 2 * rank :],
        joined(7, 1),
        joined(8, 0),
        joined(9, 0),
        sums["output"].keep,
        jnp.transpose(joined(4, 1)),
        unpacked(2, packed, 0),
        unpacked(1, packed, 0),
        grad_gate,
        grad_up_weight,
        jnp.transpose(grad_down_weight),
    )


def solution(mesh):
    placed = (
        P(("dp", "row"), "col"),
        P(("dp", "row"), "col"),
        P("dp", None),
        P("col"),
        P("col", "row"),
        P("col", "row"),
        P("col", "row"),
        P("col", None),
        P(None, "row"),
        P("col", None),
        P(None, "row"),
        P("col", None),
        P(None, "row"),
        P("row", None, None),
        P("row", None, None),
        P("row", "col"),
        P("row", None),
        P(None, "col"),
        P("col"),
        P("col", "row"),
        P("col", "row"),
        P("row", "col"),
    )
    return jax.shard_map(
        on_device,
        mesh=mesh,
        in_specs=placed,
        out_specs=(
            P(("dp", "row"), "col"),
            P(("dp", "row"), "col"),
            P("col"),
            P(("col", "dp"), "row"),
            P(("col", "dp"), "row"),
            P(("col", "dp"), "row"),
            P("col", None),
            P(None, "row"),
            P("col", None),
            P(None, "row"),
            P("col", None),
            P(None, "row"),
            P("row", None, None),
            P("row", None, None),
            P(("row", "dp"), "col"),
            P("row", None),
            P(None, "col"),
            P("col"),
            P(("col", "dp"), "row"),
            P(("col", "dp"), "row"),
            P("row", ("col", "dp")),
        ),
        check_vma=False,
    )
```

```python
import functools
import jax
import jax.numpy as jnp
from jax import lax
from jax.experimental import pallas as pl
from jax.experimental.pallas import tpu as pltpu
from jax.sharding import PartitionSpec as P

HEAD_DIM = 64
WINDOW = 64
BLOCK = 512
SUB = 128
SCALE = 0.125
NSUB = BLOCK // SUB
LANES = 128
MLP_TILE = 512
SUM_TILE = 256
GRAD_TILE = 512
VMEM_LIMIT = 56 * 1024 * 1024
FINISH_ORDER = ("up_got", "output", "down_own", "down_got")
norm_eps = 1e-05
F32 = jnp.float32
BF16 = jnp.bfloat16


def dot_nn(left, right):
    return lax.dot_general(left, right, (((1,), (0,)), ((), ())), preferred_element_type=F32)


def dot_nt(left, right):
    return lax.dot_general(left, right, (((1,), (1,)), ((), ())), preferred_element_type=F32)


def softmax_halves(before):
    def soft(values):
        powers = jnp.exp(values - jnp.max(values, axis=0, keepdims=True))
        return powers * (1.0 / jnp.sum(powers, axis=0, keepdims=True))

    return jnp.concatenate([soft(before[:HEAD_DIM]), soft(before[HEAD_DIM:])], axis=0)


def halves_backward(probs, grads):
    def half(p, g):
        return p * (g - jnp.sum(p * g, axis=0, keepdims=True))

    return half(probs[:HEAD_DIM], grads[:HEAD_DIM]) - half(probs[HEAD_DIM:], grads[HEAD_DIM:])


def side_by_side(parts, sub):
    return jnp.concatenate([part[:, sub * SUB : (sub + 1) * SUB] for part in parts], axis=1)


def key_side(kt_ref, vt_ref, kmap_ref, kft_ref, kfr_ref, kr_ref, vr_ref):
    features = softmax_halves(dot_nn(kmap_ref[0], kt_ref[...])).astype(BF16)
    kft_ref[...] = features
    kfr_ref[...] = jnp.transpose(features)
    kr_ref[...] = jnp.transpose(kt_ref[...])
    if vr_ref is not None:
        vr_ref[...] = jnp.transpose(vt_ref[...])


def tile_rows(start_ref, base, sub, ratio):
    low_one = start_ref[0, :, sub * SUB : (sub + 1) * SUB] + (WINDOW - base)
    low = jnp.concatenate([low_one] * ratio, axis=1)
    width = ratio * SUB
    place = sub * SUB + (lax.broadcasted_iota(jnp.int32, (1, width), 1) & (SUB - 1))
    same = jnp.where(low <= -1, 1.0, 0.0)
    return low, place, same


def tile_weights(kfr_ref, kr_ref, base, sub, low, place, q_sub, qf_sub):
    width = q_sub.shape[1]
    first = sub * SUB
    lin_keys = first + SUB
    win_keys = SUB + WINDOW
    link = dot_nn(kfr_ref[pl.ds(base, lin_keys), :], qf_sub)
    score = dot_nn(kr_ref[pl.ds(base + first, win_keys), :], q_sub) * SCALE
    lin_at = lax.broadcasted_iota(jnp.int32, (lin_keys, width), 0)
    win_at = lax.broadcasted_iota(jnp.int32, (win_keys, width), 0) + first
    lin_mask = (lin_at >= low) & (lin_at <= place)
    win_mask = (win_at >= jnp.maximum(low, place + 1)) & (win_at <= place + WINDOW)
    lin = jnp.where(lin_mask, link, 0.0)
    win = jnp.where(win_mask, jnp.exp(score), 0.0)
    return lin, win, lin_mask, win_mask


def member_lanes(base, mark):
    at = lax.broadcasted_iota(jnp.int32, (1, BLOCK), 1) + (base - WINDOW)
    return at >= mark


def forward_kernel(
    mark_ref, start_ref, qt_ref, kt_ref, vt_ref, qmap_ref, kmap_ref, mix_ref, inv_ref,
    kft_ref, kfr_ref, kr_ref, state_ref, norm_ref,
):
    b = pl.program_id(1)
    ratio = qmap_ref.shape[0]
    base = pl.multiple_of(b * BLOCK, BLOCK)

    @pl.when(b == 0)
    def _():
        key_side(kt_ref, vt_ref, kmap_ref, kft_ref, kfr_ref, kr_ref, None)
        state_ref[...] = jnp.zeros_like(state_ref)
        norm_ref[...] = jnp.zeros_like(norm_ref)

    queries = [qt_ref[h * HEAD_DIM : (h + 1) * HEAD_DIM, :] for h in range(ratio)]
    features = [softmax_halves(dot_nn(qmap_ref[h], queries[h])).astype(BF16) for h in range(ratio)]
    state_low = state_ref[...].astype(BF16)
    norm = norm_ref[...]
    for sub in range(NSUB):
        first = sub * SUB
        q_sub = side_by_side(queries, sub)
        qf_sub = side_by_side(features, sub)
        low, place, same = tile_rows(start_ref, base, sub, ratio)
        lin, win, _, _ = tile_weights(kfr_ref, kr_ref, base, sub, low, place, q_sub, qf_sub)
        carried = dot_nn(state_low, qf_sub)
        normal = jnp.sum(qf_sub.astype(F32) * norm, axis=0, keepdims=True)
        total = (
            jnp.sum(lin, axis=0, keepdims=True) + jnp.sum(win, axis=0, keepdims=True) + same * normal
        )
        inverse = 1.0 / total
        mixed = dot_nn(vt_ref[:, pl.ds(base, first + SUB)], lin.astype(BF16))
        mixed += dot_nn(vt_ref[:, pl.ds(base + first, SUB + WINDOW)], win.astype(BF16))
        mixed = ((mixed + same * carried) * inverse).astype(BF16)
        for h in range(ratio):
            lanes = slice(h * SUB, (h + 1) * SUB)
            mix_ref[h * HEAD_DIM : (h + 1) * HEAD_DIM, first : first + SUB] = mixed[:, lanes]
            inv_ref[0, h : h + 1, first : first + SUB] = inverse[:, lanes]

    mark = mark_ref[b + 1]
    keep = jnp.where((mark <= b * BLOCK - WINDOW - 1), 1.0, 0.0)
    tile = kft_ref[:, pl.ds(base, BLOCK)]
    member = jnp.where(member_lanes(base, mark), tile, jnp.zeros_like(tile))
    state_ref[...] = keep * state_ref[...] + dot_nt(vt_ref[:, pl.ds(base, BLOCK)], member)
    norm_ref[...] = keep * norm + jnp.sum(member.astype(F32), axis=1, keepdims=True)


def backward_kernel(
    mark_ref, start_ref, qt_ref, kt_ref, vt_ref, qmap_ref, kmap_ref, dmt_ref, mix_ref, inv_ref,
    qback_ref, kback_ref,
    dqt_ref, dkt_ref, dvt_ref, gqm_ref, gkm_ref,
    kft_ref, kfr_ref, kr_ref, vr_ref, states_ref, statet_ref, norms_ref,
    dk_acc, dkf_acc, dv_acc, dst_ref, dstt_ref, dnorm_ref,
):
    step = pl.program_id(1)
    blocks = pl.num_programs(1)
    count = states_ref.shape[0]
    b = blocks - 1 - step
    ratio = qmap_ref.shape[0]
    base = pl.multiple_of(b * BLOCK, BLOCK)

    @pl.when(step == 0)
    def _():
        key_side(kt_ref, vt_ref, kmap_ref, kft_ref, kfr_ref, kr_ref, vr_ref)
        state = jnp.zeros(statet_ref.shape[1:], F32)
        norm = jnp.zeros(norms_ref.shape[1:], F32)
        statet = jnp.zeros(states_ref.shape[1:], F32)
        for i in range(count):
            statet_ref[i] = state.astype(BF16)
            states_ref[i] = statet.astype(BF16)
            norms_ref[i] = norm
            if i + 1 < count:
                mark = mark_ref[i + 1]
                keep = jnp.where((mark <= i * BLOCK - WINDOW - 1), 1.0, 0.0)
                tile = kft_ref[:, i * BLOCK : (i + 1) * BLOCK]
                member = jnp.where(member_lanes(i * BLOCK, mark), tile, jnp.zeros_like(tile))
                values = vt_ref[:, i * BLOCK : (i + 1) * BLOCK]
                state = keep * state + dot_nt(values, member)
                statet = keep * statet + dot_nt(member, values)
                norm = keep * norm + jnp.sum(member.astype(F32), axis=1, keepdims=True)
        dk_acc[...] = jnp.zeros_like(dk_acc)
        dkf_acc[...] = jnp.zeros_like(dkf_acc)
        dv_acc[...] = jnp.zeros_like(dv_acc)
        dst_ref[...] = jnp.zeros_like(dst_ref)
        dstt_ref[...] = jnp.zeros_like(dstt_ref)
        dnorm_ref[...] = jnp.zeros_like(dnorm_ref)
        gqm_ref[...] = jnp.zeros_like(gqm_ref)

    mark = mark_ref[b + 1]
    keep = jnp.where((mark <= b * BLOCK - WINDOW - 1), 1.0, 0.0)
    tile_lanes = pl.ds(base, BLOCK)
    member = member_lanes(base, mark)
    dst_low = dst_ref[...].astype(BF16)
    dstt_low = dstt_ref[...].astype(BF16)
    dkf_acc[:, tile_lanes] += jnp.where(
        member, dot_nn(dst_low, vt_ref[:, tile_lanes]) + dnorm_ref[...], 0.0
    )
    dv_acc[:, tile_lanes] += jnp.where(member, dot_nn(dstt_low, kft_ref[:, tile_lanes]), 0.0)

    queries = [qt_ref[h * HEAD_DIM : (h + 1) * HEAD_DIM, :] for h in range(ratio)]
    gradients = [dmt_ref[h * HEAD_DIM : (h + 1) * HEAD_DIM, :] for h in range(ratio)]
    mixes = [mix_ref[h * HEAD_DIM : (h + 1) * HEAD_DIM, :] for h in range(ratio)]
    inverses = [inv_ref[0, h : h + 1, :] for h in range(ratio)]
    probabilities = [softmax_halves(dot_nn(qmap_ref[h], queries[h])) for h in range(ratio)]
    features = [p.astype(BF16) for p in probabilities]
    norm = norms_ref[b]
    state_low = states_ref[b]
    dnorm = jnp.zeros((2 * HEAD_DIM, SUB), F32)
    dst = keep * dst_ref[...]
    dstt = keep * dstt_ref[...]
    dq_parts, dpre_parts = [], []
    for sub in range(NSUB):
        first = sub * SUB
        lin_lanes = pl.ds(base, first + SUB)
        win_lanes = pl.ds(base + first, SUB + WINDOW)
        q_sub = side_by_side(queries, sub)
        qf_sub = side_by_side(features, sub)
        dm_sub = side_by_side(gradients, sub)
        inverse = side_by_side(inverses, sub)
        dm_float = dm_sub.astype(F32)
        low, place, same = tile_rows(start_ref, base, sub, ratio)
        lin, win, lin_mask, win_mask = tile_weights(
            kfr_ref, kr_ref, base, sub, low, place, q_sub, qf_sub
        )
        delta = jnp.sum(dm_float * side_by_side(mixes, sub).astype(F32), axis=0, keepdims=True)
        dv_acc[:, lin_lanes] += dot_nt(dm_sub, (lin * inverse).astype(BF16))
        dv_acc[:, win_lanes] += dot_nt(dm_sub, (win * inverse).astype(BF16))
        dlin = (dot_nn(vr_ref[lin_lanes, :], dm_sub) - delta) * inverse
        dwin = (dot_nn(vr_ref[win_lanes, :], dm_sub) - delta) * inverse
        dlink = jnp.where(lin_mask, dlin, 0.0).astype(BF16)
        dscore = (win * dwin).astype(BF16)
        dcarried = (dm_float * (same * inverse)).astype(BF16)
        dtotal = -delta * (same * inverse)
        dk_acc[:, win_lanes] += dot_nt(q_sub, dscore)
        dkf_acc[:, lin_lanes] += dot_nt(qf_sub, dlink)
        dq_parts.append(dot_nn(kt_ref[:, win_lanes], dscore) * SCALE)
        dqf = dot_nn(kft_ref[:, lin_lanes], dlink) + dot_nn(state_low, dcarried) + norm * dtotal
        dst = dst + dot_nt(qf_sub, dcarried)
        dstt = dstt + dot_nt(dcarried, qf_sub)
        weighted = qf_sub.astype(F32) * dtotal
        for h in range(ratio):
            dnorm = dnorm + weighted[:, h * SUB : (h + 1) * SUB]
        dpre_parts.append(halves_backward(side_by_side(probabilities, sub), dqf).astype(BF16))
    dst_ref[...] = dst.astype(BF16).astype(F32)
    dstt_ref[...] = dstt.astype(BF16).astype(F32)
    dnorm_ref[...] = jnp.sum(dnorm, axis=1, keepdims=True) + keep * dnorm_ref[...]
    for h in range(ratio):
        lanes = slice(h * SUB, (h + 1) * SUB)
        dpre = jnp.concatenate([part[:, lanes] for part in dpre_parts], axis=1)
        dq = jnp.concatenate([part[:, lanes] for part in dq_parts], axis=1)
        dq = dq + dot_nn(qback_ref[h], dpre)
        dqt_ref[h * HEAD_DIM : (h + 1) * HEAD_DIM, :] = dq.astype(BF16)
        gqm_ref[h] += dot_nt(queries[h], dpre)

    @pl.when(step == blocks - 1)
    def _():
        key_probs = softmax_halves(dot_nn(kmap_ref[0], kt_ref[...]))
        dpre = halves_backward(key_probs, dkf_acc[...]).astype(BF16)
        dk = (dk_acc[...] * SCALE + dot_nn(kback_ref[0], dpre)).astype(BF16)
        dv = dv_acc[...].astype(BF16)
        half = dkt_ref.shape[1] // 2
        flip = mark_ref[count + 1]
        for i in range(2):
            lanes = pl.ds(pl.multiple_of((i ^ flip) * half, half), half)
            dkt_ref[:, lanes] = dk[:, WINDOW + i * half : WINDOW + (i + 1) * half]
            dvt_ref[:, lanes] = dv[:, WINDOW + i * half : WINDOW + (i + 1) * half]
        gkm_ref[0] = dot_nt(kt_ref[...], dpre)


def signed_maps(maps):
    turned = jnp.swapaxes(maps, 1, 2)
    return jnp.concatenate([turned, -turned], axis=1)


def local_block(block, marks, blocks):
    half = blocks // 2
    return ((block // half) ^ marks[blocks + 1]) * half + block % half


def attention_specs(groups, ratio, padded, block_of):
    rows = ratio * HEAD_DIM
    return [
        pl.BlockSpec((1, 1, BLOCK), lambda g, i, *_: (0, 0, block_of(i))),
        pl.BlockSpec((rows, BLOCK), lambda g, i, *_: (g, block_of(i))),
        pl.BlockSpec((HEAD_DIM, padded), lambda g, i, *_: (g, 0)),
        pl.BlockSpec((HEAD_DIM, padded), lambda g, i, *_: (groups + g, 0)),
        pl.BlockSpec((ratio, 2 * HEAD_DIM, HEAD_DIM), lambda g, i, *_: (g, 0, 0)),
        pl.BlockSpec((1, 2 * HEAD_DIM, HEAD_DIM), lambda g, i, *_: (g, 0, 0)),
    ]


def attention_forward(marks, starts, qt, kvt, qmap, kmap):
    length = qt.shape[1]
    padded = kvt.shape[1]
    groups = kmap.shape[0]
    ratio = qmap.shape[0] // groups
    rows = ratio * HEAD_DIM
    blocks = length // BLOCK
    return pl.pallas_call(
        forward_kernel,
        out_shape=(
            jax.ShapeDtypeStruct(qt.shape, BF16),
            jax.ShapeDtypeStruct((groups, ratio, length), F32),
        ),
        grid_spec=pltpu.PrefetchScalarGridSpec(
            num_scalar_prefetch=1,
            grid=(groups, blocks),
            in_specs=attention_specs(groups, ratio, padded, lambda i: i),
            out_specs=[
                pl.BlockSpec((rows, BLOCK), lambda g, i, s: (g, local_block(i, s, blocks))),
                pl.BlockSpec((1, ratio, BLOCK), lambda g, i, *_: (g, 0, i)),
            ],
            scratch_shapes=[
                pltpu.VMEM((2 * HEAD_DIM, padded), BF16),
                pltpu.VMEM((padded, 2 * HEAD_DIM), BF16),
                pltpu.VMEM((padded, HEAD_DIM), BF16),
                pltpu.VMEM((HEAD_DIM, 2 * HEAD_DIM), F32),
                pltpu.VMEM((2 * HEAD_DIM, 1), F32),
            ],
        ),
        compiler_params=pltpu.CompilerParams(
            dimension_semantics=("arbitrary", "arbitrary"), vmem_limit_bytes=48 * 1024 * 1024
        ),
        cost_estimate=pl.CostEstimate(flops=1000, bytes_accessed=1000, transcendentals=0),
        name="attention_forward",
    )(marks, starts, qt, kvt, kvt, signed_maps(qmap), signed_maps(kmap))


def attention_backward(marks, starts, qt, kvt, qmap, kmap, dmt, mixt, inverse):
    length = qt.shape[1]
    padded = kvt.shape[1]
    groups = kmap.shape[0]
    ratio = qmap.shape[0] // groups
    rows = ratio * HEAD_DIM
    blocks = length // BLOCK
    back = lambda i: blocks - 1 - i
    query_spec = pl.BlockSpec((rows, BLOCK), lambda g, i, *_: (g, back(i)))
    local_spec = pl.BlockSpec((rows, BLOCK), lambda g, i, s: (g, local_block(back(i), s, blocks)))
    key_spec = pl.BlockSpec((HEAD_DIM, length), lambda g, i, *_: (g, 0))
    return pl.pallas_call(
        backward_kernel,
        out_shape=(
            jax.ShapeDtypeStruct(qt.shape, BF16),
            jax.ShapeDtypeStruct((groups * HEAD_DIM, length), BF16),
            jax.ShapeDtypeStruct((groups * HEAD_DIM, length), BF16),
            jax.ShapeDtypeStruct(qmap.shape, F32),
            jax.ShapeDtypeStruct(kmap.shape, F32),
        ),
        grid_spec=pltpu.PrefetchScalarGridSpec(
            num_scalar_prefetch=1,
            grid=(groups, blocks),
            in_specs=attention_specs(groups, ratio, padded, back)
            + [
                query_spec,
                local_spec,
                pl.BlockSpec((1, ratio, BLOCK), lambda g, i, *_: (g, 0, back(i))),
                pl.BlockSpec((ratio, HEAD_DIM, HEAD_DIM), lambda g, i, *_: (g, 0, 0)),
                pl.BlockSpec((1, HEAD_DIM, HEAD_DIM), lambda g, i, *_: (g, 0, 0)),
            ],
            out_specs=[
                local_spec,
                key_spec,
                key_spec,
                pl.BlockSpec((ratio, HEAD_DIM, HEAD_DIM), lambda g, i, *_: (g, 0, 0)),
                pl.BlockSpec((1, HEAD_DIM, HEAD_DIM), lambda g, i, *_: (g, 0, 0)),
            ],
            scratch_shapes=[
                pltpu.VMEM((2 * HEAD_DIM, padded), BF16),
                pltpu.VMEM((padded, 2 * HEAD_DIM), BF16),
                pltpu.VMEM((padded, HEAD_DIM), BF16),
                pltpu.VMEM((padded, HEAD_DIM), BF16),
                pltpu.VMEM((blocks, 2 * HEAD_DIM, HEAD_DIM), BF16),
                pltpu.VMEM((blocks, HEAD_DIM, 2 * HEAD_DIM), BF16),
                pltpu.VMEM((blocks, 2 * HEAD_DIM, 1), F32),
                pltpu.VMEM((HEAD_DIM, padded), F32),
                pltpu.VMEM((2 * HEAD_DIM, padded), F32),
                pltpu.VMEM((HEAD_DIM, padded), F32),
                pltpu.VMEM((2 * HEAD_DIM, HEAD_DIM), F32),
                pltpu.VMEM((HEAD_DIM, 2 * HEAD_DIM), F32),
                pltpu.VMEM((2 * HEAD_DIM, 1), F32),
            ],
        ),
        compiler_params=pltpu.CompilerParams(
            dimension_semantics=("arbitrary", "arbitrary"), vmem_limit_bytes=48 * 1024 * 1024
        ),
        cost_estimate=pl.CostEstimate(flops=1000, bytes_accessed=1000, transcendentals=0),
        name="attention_backward",
    )(
        marks, starts, qt, kvt, kvt, signed_maps(qmap), signed_maps(kmap), dmt, mixt, inverse, qmap, kmap
    )


FREE = pl.CostEstimate(flops=1000, bytes_accessed=1000, transcendentals=0)


def grid_call(kernel, name, grid, out_shape, in_specs, out_specs, scratch=(), aliases=None):
    return pl.pallas_call(
        kernel,
        out_shape=out_shape,
        grid_spec=pltpu.PrefetchScalarGridSpec(
            num_scalar_prefetch=1,
            grid=grid,
            in_specs=in_specs,
            out_specs=out_specs,
            scratch_shapes=list(scratch),
        ),
        input_output_aliases=aliases or {},
        compiler_params=pltpu.CompilerParams(
            dimension_semantics=("arbitrary",) * len(grid), vmem_limit_bytes=VMEM_LIMIT
        ),
        cost_estimate=FREE,
        name=name,
    )


MESH = pl.DeviceIdType.MESH


def exchange_kernel(query_cols, key_cols, *refs):
    inputs, grads, query, key, value, gate, up, down, output = refs[:9]
    thin = refs[9:11]
    near_other, grads_other, proj_got, gate_got, up_got, down_got, output_got = refs[11:18]
    thin_got = refs[18:20]
    proj_own, proj_both, output_both = refs[20:23]
    send_sem, recv_sem, local_sem, proj_all, output_all = refs[23:]
    col = lax.axis_index("col")

    barrier = pltpu.get_barrier_semaphore()
    pl.semaphore_signal(barrier, inc=1, device_id={"col": 1 - col}, device_id_type=MESH)
    pl.semaphore_wait(barrier, 1)

    copies = []

    def remote(source, target):
        n = len(copies)
        copy = pltpu.make_async_remote_copy(
            src_ref=source,
            dst_ref=target,
            send_sem=send_sem.at[n],
            recv_sem=recv_sem.at[n],
            device_id={"col": 1 - col},
            device_id_type=MESH,
        )
        copy.start()
        copies.append(copy)

    def columns(ref, index, width):
        return ref.at[:, pl.ds(pl.multiple_of(index * width, width), width)]

    def rows_of(ref, index, height):
        return ref.at[pl.ds(pl.multiple_of(index * height, height), height), :]

    remote(inputs, near_other)
    first = 0
    for weight, width in ((query, query_cols), (key, key_cols), (value, key_cols)):
        remote(columns(weight, 1 - col, width), proj_got.at[:, pl.ds(first, width)])
        first += width
    for source, target in zip(thin, thin_got):
        remote(source, target)
    remote(columns(gate, 1 - col, gate_got.shape[1]), gate_got)
    remote(columns(up, 1 - col, up_got.shape[1]), up_got)
    remote(rows_of(down, 1 - col, down_got.shape[0]), down_got)
    remote(rows_of(output, 1 - col, output_got.shape[0]), output_got)
    remote(grads, grads_other)

    def local(source, target, n):
        copy = pltpu.make_async_copy(source, target, local_sem.at[n])
        copy.start()
        return copy

    whole = proj_own.shape[1]
    height = output_got.shape[0]
    loads, first = [], 0
    for weight, width in ((query, query_cols), (key, key_cols), (value, key_cols)):
        for side in range(2):
            loads.append(
                local(
                    columns(weight, col ^ side, width),
                    proj_all.at[:, pl.ds(side * whole + first, width)],
                    len(loads),
                )
            )
        first += width
    for side in range(2):
        loads.append(
            local(
                rows_of(output, col ^ side, height),
                output_all.at[pl.ds(side * height, height), :],
                len(loads),
            )
        )
    for copy in loads:
        copy.wait()
    stores = [
        local(proj_all.at[:, pl.ds(0, whole)], proj_own, 8),
        local(proj_all, proj_both, 9),
        local(output_all, output_both, 10),
    ]

    for copy in stores:
        copy.wait()
    for copy in copies:
        copy.wait()


def exchange(inputs, grads, projections, gate, up, down, output, thin):
    query, key, value = projections
    rows, half = inputs.shape
    query_cols, key_cols = query.shape[1] // 2, key.shape[1] // 2
    columns = query_cols + 2 * key_cols
    like = lambda *shape: jax.ShapeDtypeStruct(shape, BF16)
    outs = [
        like(rows, half),
        like(rows, half),
        like(half, columns),
        like(half, gate.shape[1] // 2),
        like(half, up.shape[1] // 2),
        like(down.shape[0] // 2, half),
        like(output.shape[0] // 2, half),
    ]
    outs += [jax.ShapeDtypeStruct(values.shape, values.dtype) for values in thin]
    outs += [like(half, columns), like(half, 2 * columns), like(output.shape[0], half)]
    copies = 1 + 3 + len(thin) + 5
    return pl.pallas_call(
        functools.partial(exchange_kernel, query_cols, key_cols),
        out_shape=tuple(outs),
        in_specs=[pl.BlockSpec(memory_space=pl.ANY)] * (9 + len(thin)),
        out_specs=tuple([pl.BlockSpec(memory_space=pl.ANY)] * len(outs)),
        scratch_shapes=[
            pltpu.SemaphoreType.DMA((copies,)),
            pltpu.SemaphoreType.DMA((copies,)),
            pltpu.SemaphoreType.DMA((11,)),
            pltpu.VMEM((half, 2 * columns), BF16),
            pltpu.VMEM(output.shape, BF16),
        ],
        compiler_params=pltpu.CompilerParams(
            collective_id=0, has_side_effects=True, vmem_limit_bytes=VMEM_LIMIT
        ),
        cost_estimate=FREE,
        name="exchange",
    )(inputs, grads, query, key, value, gate, up, down, output, *thin)


def hidden_grad_kernel(place_ref, gm_own, go_own, gm_far, go_far, down_own, down_got, out_ref):
    half = gm_own.shape[0]
    out_ref[:half] = (
        dot_nt(gm_own[...], down_own[...]) + dot_nt(go_own[...], down_got[...])
    ).astype(BF16)
    out_ref[half:] = (
        dot_nt(gm_far[...], down_own[...]) + dot_nt(go_far[...], down_got[...])
    ).astype(BF16)


def hidden_grad(place, grads, down_weight, down_got):
    half, width = grads[0].shape
    hidden_cols = down_got.shape[0]
    tiles = hidden_cols // MLP_TILE
    whole = pl.BlockSpec((half, width), lambda i, s: (0, 0))
    return grid_call(
        hidden_grad_kernel,
        "hidden_grad",
        (tiles,),
        jax.ShapeDtypeStruct((2 * half, hidden_cols), BF16),
        [whole] * 4
        + [
            pl.BlockSpec((MLP_TILE, width), lambda i, s: (s[0] * tiles + i, 0)),
            pl.BlockSpec((MLP_TILE, width), lambda i, s: (i, 0)),
        ],
        pl.BlockSpec((2 * half, MLP_TILE), lambda i, s: (0, i)),
    )(place, *grads, down_weight, down_got)


def project_kernel(
    place_ref,
    mine_ref,
    other_ref,
    gain_ref,
    gain_got_ref,
    proj_own,
    proj_got,
    thin_ref,
    thin_got_ref,
    up_ref,
    *refs,
):
    normed_ref, queries_ref, keys_ref, adapters_ref, scale_ref = refs[-5:]
    half = mine_ref.shape[1]
    mine, other = mine_ref[...].astype(F32), other_ref[...].astype(F32)
    squares = jnp.sum(mine * mine, axis=1, keepdims=True) + jnp.sum(
        other * other, axis=1, keepdims=True
    )
    scale = lax.rsqrt(squares / (2 * half) + norm_eps)
    left = (mine * scale * gain_ref[:1, :]).astype(BF16)
    right = (other * scale * gain_got_ref[:1, :]).astype(BF16)
    normed_ref[:, :half] = left
    normed_ref[:, half:] = right
    scale_ref[...] = scale
    adapters = (dot_nt(left, thin_ref[...]) + dot_nt(right, thin_got_ref[...])).astype(BF16)
    adapters_ref[...] = adapters
    sums = dot_nn(left, proj_own[...]) + dot_nn(right, proj_got[...]) + dot_nn(adapters, up_ref[...])
    turned = jnp.transpose(sums.astype(BF16))
    rows = queries_ref.shape[0]
    queries_ref[...] = turned[:rows]
    keys_ref[...] = turned[rows:]


def global_block(local, flip, half_blocks):
    return ((local // half_blocks) ^ flip) * half_blocks + local % half_blocks


def project_block(index, place, mine, other, gains, projections, thin, up, query_part, kept):
    proj_own, proj_got = projections
    rows, half = mine.shape
    length = 2 * half_rows_of(kept, rows)
    blocks, half_blocks = length // BLOCK, length // BLOCK // 2
    columns = proj_own.shape[1]
    whole = lambda values: pl.BlockSpec(values.shape, lambda i, s: (0, 0))
    lanes = lambda i, s: (0, global_block(index + i, s[1], half_blocks))
    local = lambda i, s: (index + i, 0)
    shapes = (
        jax.ShapeDtypeStruct((length, 2 * half), BF16),
        jax.ShapeDtypeStruct((query_part, length), BF16),
        jax.ShapeDtypeStruct((columns - query_part, length), BF16),
        jax.ShapeDtypeStruct((length, up.shape[0]), BF16),
        jax.ShapeDtypeStruct((length, 1), F32),
    )
    operands = (mine, other, *gains, proj_own, proj_got, *thin, up)
    return grid_call(
        project_kernel,
        "project_block",
        (rows // BLOCK,),
        shapes,
        [
            pl.BlockSpec((BLOCK, half), lambda i, s: (i, 0)),
            pl.BlockSpec((BLOCK, half), lambda i, s: (i, 0)),
        ]
        + [whole(values) for values in operands[2:]]
        + [pl.BlockSpec(memory_space=pl.ANY)] * len(kept),
        [
            pl.BlockSpec((BLOCK, 2 * half), local),
            pl.BlockSpec((query_part, BLOCK), lanes),
            pl.BlockSpec((columns - query_part, BLOCK), lanes),
            pl.BlockSpec((BLOCK, up.shape[0]), local),
            pl.BlockSpec((BLOCK, 1), local),
        ],
        aliases={1 + len(operands) + i: i for i in range(len(kept))},
    )(place, *operands, *kept)


def half_rows_of(kept, rows):
    return kept[0].shape[0] // 2 if kept else rows


def mlp_kernel(
    count,
    place_ref,
    in_mine,
    in_other,
    at_mine,
    at_other,
    far_mine,
    far_other,
    adapter_ref,
    up_ref,
    gain_ref,
    gate_own,
    gate_got,
    up_own,
    up_got,
    dh_ref,
    *refs,
):
    hidden_ref, dgate_ref, dup_ref, normed_ref, scale_ref = refs[-1 - count : -1][:5]
    left_ref = refs[-1]
    half = in_mine.shape[1]

    @pl.when(pl.program_id(0) == 0)
    def _():
        def state(inputs, own, far, adapted):
            return inputs[...].astype(F32) + (
                own[...].astype(F32) + far[...].astype(F32) + adapted
            )

        adapter = adapter_ref[...]
        mine = state(in_mine, at_mine, far_mine, dot_nn(adapter, up_ref[:, :half]))
        other = state(in_other, at_other, far_other, dot_nn(adapter, up_ref[:, half:]))
        squares = jnp.sum(mine * mine, axis=1, keepdims=True) + jnp.sum(
            other * other, axis=1, keepdims=True
        )
        scale = lax.rsqrt(squares / (2 * half) + norm_eps)
        scale_ref[...] = scale
        if count == 6:
            refs[-2][...] = mine
        left_ref[:, :half] = (mine * scale * gain_ref[:, :half]).astype(BF16)
        left_ref[:, half:] = (other * scale * gain_ref[:, half:]).astype(BF16)
        normed_ref[...] = left_ref[...]

    left, right = left_ref[:, :half], left_ref[:, half:]
    gate = dot_nn(left, gate_own[...]) + dot_nn(right, gate_got[...])
    up = dot_nn(left, up_own[...]) + dot_nn(right, up_got[...])
    d_hidden = dh_ref[...].astype(F32)
    sig = 1.0 / (1.0 + jnp.exp(-gate))
    silu = gate * sig
    hidden_ref[...] = (silu * up).astype(BF16)
    dup_ref[...] = (d_hidden * silu).astype(BF16)
    dgate_ref[...] = (d_hidden * up * (sig * (1.0 + gate * (1.0 - sig)))).astype(BF16)


def mlp_block(
    index,
    place,
    inputs,
    input_block,
    attended,
    adapter,
    output_up,
    gain,
    gate_weight,
    gate_got,
    up_weight,
    up_got,
    d_hidden,
    kept,
    state_kept,
    with_state,
):
    half, hidden_cols = gate_got.shape
    width = 2 * half
    length = d_hidden.shape[0]
    tiles = hidden_cols // MLP_TILE
    own_spec = pl.BlockSpec((half, MLP_TILE), lambda i, s: (0, s[0] * tiles + i))
    got_spec = pl.BlockSpec((half, MLP_TILE), lambda i, s: (0, i))
    kept_spec = pl.BlockSpec((BLOCK, MLP_TILE), lambda i, s: (index, i))
    here = lambda columns: pl.BlockSpec((BLOCK, columns), lambda i, s: (index, 0))
    whole = lambda values: pl.BlockSpec(values.shape, lambda i, s: (0, 0))
    input_spec = pl.BlockSpec((BLOCK, half), lambda i, s: (input_block, 0))
    block_spec = pl.BlockSpec((BLOCK, half), lambda i, s: (0, 0))
    shapes = (jax.ShapeDtypeStruct((length, hidden_cols), BF16),) * 3 + (
        jax.ShapeDtypeStruct((length, width), BF16),
        jax.ShapeDtypeStruct((length, 1), F32),
    )
    out_specs = [kept_spec] * 3 + [here(width), here(1)]
    aliases = {15 + i: i for i in range(len(kept))}
    passed = tuple(kept)
    if with_state:
        shapes += (jax.ShapeDtypeStruct((length // 2, half), F32),)
        out_specs.append(here(half))
        if state_kept is not None:
            aliases[15 + len(passed)] = 5
            passed += (state_kept,)
    return grid_call(
        functools.partial(mlp_kernel, len(shapes)),
        "mlp_block",
        (tiles,),
        shapes,
        [input_spec, input_spec]
        + [block_spec] * 4
        + [here(adapter.shape[1]), whole(output_up), whole(gain)]
        + [own_spec, got_spec, own_spec, got_spec, kept_spec]
        + [pl.BlockSpec(memory_space=pl.ANY)] * len(passed),
        out_specs,
        [pltpu.VMEM((BLOCK, width), BF16)],
        aliases,
    )(
        place,
        *inputs,
        *attended,
        adapter,
        output_up,
        gain,
        gate_weight,
        gate_got,
        up_weight,
        up_got,
        d_hidden,
        *passed,
    )


def norm_back_kernel(
    count,
    place_ref,
    total_mine,
    total_other,
    normed_ref,
    scale_ref,
    grad_mine,
    grad_other,
    gain_ref,
    out_own,
    out_got,
    up_ref,
    down_ref,
    *refs,
):
    mixed_ref, mine_ref, adapter_ref, gain_sum = refs[-count:][:4]
    half = total_mine.shape[1]
    gain_left, gain_right = gain_ref[:, :half], gain_ref[:, half:]
    d_left, d_right = total_mine[...].astype(F32), total_other[...].astype(F32)
    hat_left = normed_ref[:, :half].astype(F32) * (1.0 / gain_left)
    hat_right = normed_ref[:, half:].astype(F32) * (1.0 / gain_right)
    term = jnp.sum(d_left * hat_left, axis=0, keepdims=True)
    g_left, g_right = d_left * gain_left, d_right * gain_right
    inner = (
        jnp.sum(g_left * hat_left, axis=1, keepdims=True)
        + jnp.sum(g_right * hat_right, axis=1, keepdims=True)
    ) / (2 * half)
    scale = scale_ref[...]
    left = grad_mine[...].astype(F32) + scale * (g_left - hat_left * inner)
    right = grad_other[...].astype(F32) + scale * (g_right - hat_right * inner)
    if count == 5:
        refs[-1][...] = left
    left, right = left.astype(BF16), right.astype(BF16)
    mine_ref[...] = left
    adapter = (dot_nt(left, up_ref[:, :half]) + dot_nt(right, up_ref[:, half:])).astype(BF16)
    adapter_ref[...] = adapter
    mixed_ref[...] = (
        dot_nt(out_own[...], left) + dot_nt(out_got[...], right) + dot_nt(down_ref[...], adapter)
    ).astype(BF16)

    @pl.when(pl.program_id(0) == 0)
    def _():
        gain_sum[...] = term

    @pl.when(pl.program_id(0) > 0)
    def _():
        gain_sum[...] += term


def norm_back(
    index, place, totals, normed, scale, grads, gain, out_own, out_got, up, down, kept, with_state
):
    half_rows, half = totals[0].shape
    length = 2 * half_rows
    half_blocks = half_rows // BLOCK
    heads = out_own.shape[0]
    base = index * half_blocks
    whole = lambda values: pl.BlockSpec(values.shape, lambda i, s: (0, 0))
    near = pl.BlockSpec((BLOCK, half), lambda i, s: (i, 0))
    here = lambda columns: pl.BlockSpec((BLOCK, columns), lambda i, s: (base + i, 0))
    shapes = (
        jax.ShapeDtypeStruct((heads, length), BF16),
        jax.ShapeDtypeStruct((length, half), BF16),
        jax.ShapeDtypeStruct((length, LANES), BF16),
        jax.ShapeDtypeStruct((1, half), F32),
    )
    out_specs = [
        pl.BlockSpec((heads, BLOCK), lambda i, s: (0, global_block(base + i, s[1], half_blocks))),
        here(half),
        here(LANES),
        pl.BlockSpec((1, half), lambda i, s: (0, 0)),
    ]
    if with_state:
        shapes += (jax.ShapeDtypeStruct((half_rows, half), F32),)
        out_specs.append(near)
    return grid_call(
        functools.partial(norm_back_kernel, len(shapes)),
        "norm_back",
        (half_blocks,),
        shapes,
        [near, near, here(2 * half), here(1), near, near]
        + [whole(values) for values in (gain, out_own, out_got, up, down)]
        + [pl.BlockSpec(memory_space=pl.ANY)] * len(kept),
        out_specs,
        aliases={12 + i: i for i in range(len(kept))},
    )(place, *totals, normed, scale, *grads, gain, out_own, out_got, up, down, *kept)


def pair_sum_kernel(products, *refs):
    operands = refs[:-5]
    out_ref, send_buf, recv_buf, send_sem, recv_sem = refs[-5:]
    step = pl.program_id(0)
    tiles = send_buf.shape[0]
    col = lax.axis_index("col")

    def copy(tile):
        return pltpu.make_async_remote_copy(
            src_ref=send_buf.at[tile],
            dst_ref=recv_buf.at[tile],
            send_sem=send_sem.at[tile],
            recv_sem=recv_sem.at[tile],
            device_id={"col": 1 - col},
            device_id_type=MESH,
        )

    @pl.when(step == 0)
    def _():
        barrier = pltpu.get_barrier_semaphore()
        pl.semaphore_signal(barrier, inc=1, device_id={"col": 1 - col}, device_id_type=MESH)
        pl.semaphore_wait(barrier, 1)

    @pl.when(step < tiles)
    def _():
        send_buf[step] = products(operands, False).astype(BF16)
        copy(step).start()

    @pl.when(step >= tiles)
    def _():
        tile = step - tiles
        sums = products(operands, True)
        copy(tile).wait_recv()
        out_ref[...] = (sums + recv_buf[tile].astype(F32)).astype(BF16)

    @pl.when(step == 2 * tiles - 1)
    def _():
        for tile in range(tiles):
            copy(tile).wait_send()


def pair_sum(products, name, collective, rows, half, in_specs, operands):
    tile = min(SUM_TILE, half)
    tiles = half // tile
    return pl.pallas_call(
        functools.partial(pair_sum_kernel, products),
        grid=(2 * tiles,),
        out_shape=jax.ShapeDtypeStruct((rows, half), BF16),
        in_specs=in_specs,
        out_specs=pl.BlockSpec((rows, tile), lambda i: (0, jnp.maximum(i - tiles, 0))),
        scratch_shapes=[
            pltpu.VMEM((tiles, rows, tile), BF16),
            pltpu.VMEM((tiles, rows, tile), BF16),
            pltpu.SemaphoreType.DMA((tiles,)),
            pltpu.SemaphoreType.DMA((tiles,)),
        ],
        compiler_params=pltpu.CompilerParams(
            dimension_semantics=("arbitrary",),
            collective_id=collective,
            has_side_effects=True,
            vmem_limit_bytes=VMEM_LIMIT,
        ),
        cost_estimate=FREE,
        name=name,
    )(*operands)


def second_products(refs, own):
    d_gate, d_up, gate_own, gate_got, up_own, up_got = refs
    if own:
        return dot_nt(d_gate[...], gate_own[...]) + dot_nt(d_up[...], up_own[...])
    return dot_nt(d_gate[...], gate_got[...]) + dot_nt(d_up[...], up_got[...])


def second_grad(index, d_gate, d_up, gate_weight, gate_got, up_weight, up_got):
    half, hidden_cols = gate_got.shape
    rows = d_gate.shape[0] // 2
    tile = min(SUM_TILE, half)
    tiles = half // tile
    left = pl.BlockSpec((rows, hidden_cols), lambda i: (index, 0))
    own = pl.BlockSpec(
        (tile, hidden_cols), lambda i: (jnp.maximum(i - tiles, 0), lax.axis_index("col"))
    )
    got = pl.BlockSpec((tile, hidden_cols), lambda i: (jnp.minimum(i, tiles - 1), 0))
    return pair_sum(
        second_products,
        "second_grad",
        1 + index,
        rows,
        half,
        [left, left, own, got, own, got],
        (d_gate, d_up, gate_weight, gate_got, up_weight, up_got),
    )


def down_products(refs, own):
    hidden, down_own, down_got = refs
    return dot_nn(hidden[...], (down_own if own else down_got)[...])


def down_product(hidden, down_weight, down_got):
    rows, hidden_cols = hidden.shape
    half = down_got.shape[1]
    tile = min(SUM_TILE, half)
    tiles = half // tile
    return pair_sum(
        down_products,
        "down_product",
        3,
        rows,
        half,
        [
            pl.BlockSpec((rows, hidden_cols), lambda i: (0, 0)),
            pl.BlockSpec(
                (hidden_cols, tile), lambda i: (lax.axis_index("col"), jnp.maximum(i - tiles, 0))
            ),
            pl.BlockSpec((hidden_cols, tile), lambda i: (0, jnp.minimum(i, tiles - 1))),
        ],
        (hidden, down_weight, down_got),
    )


def finish_kernel(orders, size, *refs):
    count = len(orders)
    far_ref, small_ref = refs[:2]
    grads = refs[2 : 2 + count]
    far_out, small_out = refs[2 + count : 4 + count]
    outs = refs[4 + count : 4 + 2 * count]
    small_got, small_sum, send_sem, recv_sem = refs[4 + 2 * count : 8 + 2 * count]
    buffers = refs[8 + 2 * count :]
    bits = len(orders[0])
    row, place = lax.axis_index("row"), lax.axis_index("dp")

    barrier = pltpu.get_barrier_semaphore()
    partners = [{"row": 1 - row}] + [{"dp": place ^ (1 << k)} for k in range(bits)]
    for partner in partners:
        pl.semaphore_signal(barrier, inc=1, device_id=partner, device_id_type=MESH)
    pl.semaphore_wait(barrier, len(partners))

    def send(source, target, n, partner):
        copy = pltpu.make_async_remote_copy(
            src_ref=source,
            dst_ref=target,
            send_sem=send_sem.at[n],
            recv_sem=recv_sem.at[n],
            device_id=partner,
            device_id_type=MESH,
        )
        copy.start()
        return copy

    waiting = [send(far_ref, far_out, 0, partners[0])]
    current = list(grads)
    small_sum[0] = small_ref[...]
    for step in range(bits):
        first = 1 + step * (count + 1)
        bit = (step + bits - 1) % bits
        small = send(small_sum.at[step], small_got.at[step], first, partners[1 + bit])
        moving = []
        for n in range(count):
            rows = current[n].shape[0] // 2
            got = buffers[n * (2 * bits - 1) + step]
            moving.append(
                send(
                    current[n].at[pl.ds(rows, rows), :],
                    got,
                    first + 1 + n,
                    partners[1 + orders[n][step]],
                )
            )
        small.wait_recv()
        if step + 1 < bits:
            small_sum[step + 1] = small_sum[step] + small_got[step]
        else:
            small_out[...] = small_sum[step] + small_got[step]
        for n in range(count):
            rows = current[n].shape[0] // 2
            got = buffers[n * (2 * bits - 1) + step]
            moving[n].wait_recv()
            sums = current[n][:rows].astype(F32) + got[...].astype(F32)
            if step + 1 < bits:
                target = buffers[n * (2 * bits - 1) + bits + step]
                target[...] = sums.astype(BF16)
                current[n] = target
            else:
                outs[n][...] = sums
        waiting += [small] + moving
    waiting[0].wait_recv()
    for copy in waiting:
        copy.wait_send()


def finish(far, small, grads, orders, size):
    bits = len(orders[0])
    count = len(grads)
    vmem = pl.BlockSpec(memory_space=pltpu.VMEM)
    anywhere = pl.BlockSpec(memory_space=pl.ANY)
    copies = 1 + bits * (count + 1)
    scratch = [
        pltpu.VMEM((bits,) + small.shape, F32),
        pltpu.VMEM((bits,) + small.shape, F32),
        pltpu.SemaphoreType.DMA((copies,)),
        pltpu.SemaphoreType.DMA((copies,)),
    ]
    for grad in grads:
        rows, columns = grad.shape
        scratch += [pltpu.VMEM((rows >> (k + 1), columns), BF16) for k in range(bits)]
        scratch += [pltpu.VMEM((rows >> (k + 1), columns), BF16) for k in range(bits - 1)]
    return pl.pallas_call(
        functools.partial(finish_kernel, orders, size),
        out_shape=(
            jax.ShapeDtypeStruct(far.shape, far.dtype),
            jax.ShapeDtypeStruct(small.shape, F32),
        )
        + tuple(jax.ShapeDtypeStruct((g.shape[0] // size, g.shape[1]), F32) for g in grads),
        in_specs=[anywhere, vmem] + [vmem] * count,
        out_specs=(anywhere, vmem) + (vmem,) * count,
        scratch_shapes=scratch,
        compiler_params=pltpu.CompilerParams(
            collective_id=4, has_side_effects=True, vmem_limit_bytes=VMEM_LIMIT
        ),
        cost_estimate=FREE,
        name="finish",
    )(far, small, *grads)


def weight_grad_kernel(sets, chunks, pieces, turned, right_turned, place_ref, *refs):
    outs = refs[-1 - pieces * sets : -1]
    right_ref, left_ref = refs[-2 - pieces * sets], refs[-1]
    lefts = refs[: -2 - pieces * sets]
    length = left_ref.shape[1]
    rows = left_ref.shape[0] // sets
    count = rows // LANES

    @pl.when(pl.program_id(0) == 0)
    def _():
        for p in range(sets * count):
            lanes = slice(p * LANES, (p + 1) * LANES)
            if turned:
                left_ref[lanes, :] = lefts[p][...]
            else:
                size = length // chunks
                for i in range(chunks):
                    left_ref[lanes, i * size : (i + 1) * size] = jnp.transpose(
                        lefts[p * chunks + i][...]
                    )

    for which in range(sets):
        left = left_ref[which * rows : (which + 1) * rows, :]
        sums = (dot_nt if right_turned else dot_nn)(left, right_ref[...])
        size = rows // pieces
        for i in range(pieces):
            outs[pieces * which + i][...] = sums[i * size : (i + 1) * size].astype(BF16)


def weight_grad(places, sets, right, pieces=2, turned=False, right_turned=False, cut=(0, 1)):
    chunks = len(sets[0][0])
    length = sets[0][0][0].shape[1] if turned else sum(c.shape[0] for c in sets[0][0])
    count = (places.shape[0] - 2) // len(sets)
    columns = (right.shape[0] if right_turned else right.shape[1]) // cut[1]
    tile = next(size for size in (GRAD_TILE, 384, 256, 128) if columns % size == 0)
    skip = cut[0] * (columns // tile)
    in_specs, operands = [], []
    for n, (lefts, base) in enumerate(sets):
        for p in range(count):
            at = 2 + n * count + p
            for left in lefts:
                if turned:
                    spec = pl.BlockSpec((LANES, length), lambda j, s, at=at: (s[at], 0))
                else:
                    spec = pl.BlockSpec(
                        (left.shape[0], LANES), lambda j, s, at=at, base=base: (0, base + s[at])
                    )
                in_specs.append(spec)
                operands.append(left)
    if right_turned:
        in_specs.append(pl.BlockSpec((tile, length), lambda j, s: (skip + j, 0)))
    else:
        in_specs.append(pl.BlockSpec((length, tile), lambda j, s: (0, skip + j)))
    size = count * LANES // pieces
    out_spec = pl.BlockSpec((size, tile), lambda j, s: (0, j))
    return grid_call(
        functools.partial(weight_grad_kernel, len(sets), chunks, pieces, turned, right_turned),
        "weight_grad",
        (columns // tile,),
        (jax.ShapeDtypeStruct((size, columns), BF16),) * (pieces * len(sets)),
        in_specs,
        [out_spec] * (pieces * len(sets)),
        [pltpu.VMEM((len(sets) * count * LANES, length), BF16)],
    )(places, *operands, right)


def first_back_kernel(place_ref, *refs):
    parts, (proj_ref, up_ref, normed_ref) = refs[:6], refs[6:9]
    far_ref, own_ref, turned_ref, adapter_ref, gain_ref = refs[9:]
    step = pl.program_id(0)
    first = 0
    for source in parts:
        turned_ref[:, first : first + source.shape[0]] = jnp.transpose(source[...])
        first += source.shape[0]
    turned = turned_ref[...]
    adapter_ref[...] = dot_nt(turned, up_ref[...])
    sums = dot_nt(turned, proj_ref[...])
    term = jnp.sum(sums * normed_ref[...].astype(F32), axis=0, keepdims=True)

    @pl.when(step < pl.num_programs(0) // 2)
    def _():
        far_ref[...] = sums.astype(BF16)

    @pl.when(step >= pl.num_programs(0) // 2)
    def _():
        own_ref[...] = sums

    @pl.when(step == 0)
    def _():
        gain_ref[...] = term

    @pl.when(step > 0)
    def _():
        gain_ref[...] += term


def first_back(place, parts, proj_native, up_native, normed):
    length = parts[0].shape[1]
    half, columns = proj_native.shape
    blocks = length // BLOCK
    middle = blocks // 2
    at = lambda i: (i + middle) % blocks
    whole = lambda values: pl.BlockSpec(values.shape, lambda i, s: (0, 0))
    return grid_call(
        first_back_kernel,
        "first_back",
        (blocks,),
        (
            jax.ShapeDtypeStruct((length // 2, half), BF16),
            jax.ShapeDtypeStruct((length // 2, half), F32),
            jax.ShapeDtypeStruct((length, columns), BF16),
            jax.ShapeDtypeStruct((length, up_native.shape[0]), F32),
            jax.ShapeDtypeStruct((1, half), F32),
        ),
        [pl.BlockSpec((values.shape[0], BLOCK), lambda i, s: (0, at(i))) for values in parts]
        + [whole(proj_native), whole(up_native)]
        + [pl.BlockSpec((BLOCK, half), lambda i, s: (at(i), 0))],
        [
            pl.BlockSpec((BLOCK, half), lambda i, s: (jnp.minimum(i, middle - 1), 0)),
            pl.BlockSpec((BLOCK, half), lambda i, s: (jnp.maximum(i - middle, 0), 0)),
            pl.BlockSpec((BLOCK, columns), lambda i, s: (at(i), 0)),
            pl.BlockSpec((BLOCK, up_native.shape[0]), lambda i, s: (at(i), 0)),
            whole(jnp.zeros((1, half))),
        ],
    )(place, *parts, proj_native, up_native, normed)


def after(value, *others):
    return lax.optimization_barrier((value,) + others)[0]


def swap(values, axis):
    return lax.ppermute(values, axis, [(0, 1), (1, 0)])


def part(values, index, count, axis):
    width = values.shape[axis] // count
    return lax.dynamic_slice_in_dim(values, index * width, width, axis)


def contract(left, right, left_dim, right_dim):
    return lax.dot_general(
        left, right, (((left_dim,), (right_dim,)), ((), ())), preferred_element_type=F32
    )


def exchange_order(bits, first):
    return [(first + k) % bits for k in range(bits)]


def relative_index(position, order):
    bits = len(order)
    return sum(((position >> (bits - 1 - k)) & 1) << order[k] for k in range(bits))


def relative_blocks(values, axis, device, order):
    count = 1 << len(order)
    return jnp.concatenate(
        [part(values, device ^ relative_index(p, order), count, axis) for p in range(count)],
        axis=axis,
    )


class Reduction:
    def __init__(self, keep, send, size, order):
        self.keep, self.size, self.order, self.step = keep, size, order, 0
        self.launch(send)

    def launch(self, send):
        bit = 1 << self.order[self.step]
        self.got = lax.ppermute(send, "dp", [(i, i ^ bit) for i in range(self.size)])

    def combine(self):
        got = self.got
        self.step += 1
        if self.step == len(self.order):
            self.keep = self.keep.astype(F32) + got.astype(F32)
            return self.keep
        half = self.keep.shape[0] // 2
        sums = (
            (self.keep[rows].astype(F32) + got[rows].astype(F32)).astype(BF16)
            for rows in (slice(0, half), slice(half, 2 * half))
        )
        self.keep, send = sums
        self.launch(send)
        return self.keep

    @property
    def done(self):
        return self.step == len(self.order)


def total_over(values, size, bits):
    for k in range(bits):
        values = values + lax.ppermute(values, "dp", [(i, i ^ (1 << k)) for i in range(size)])
    return values


def ordered(own, other, index, axis):
    return jnp.where(
        index == 0,
        jnp.concatenate([own, other], axis=axis),
        jnp.concatenate([other, own], axis=axis),
    )


def on_device(
    activations,
    grad_out,
    segments,
    first_gain,
    query_weight,
    key_weight,
    value_weight,
    query_down,
    query_up,
    key_down,
    key_up,
    value_down,
    value_up,
    query_map,
    key_map,
    output_weight,
    output_down,
    output_up,
    second_gain,
    gate_weight,
    up_weight,
    down_weight,
):
    size = lax.axis_size("dp")
    bits = size.bit_length() - 1
    device = lax.axis_index("dp")
    row = lax.axis_index("row")
    col = lax.axis_index("col")
    seq_rows = segments.shape[1]
    half_rows, feature_cols = activations.shape
    width = 2 * feature_cols
    blocks = seq_rows // BLOCK
    half_blocks = blocks // 2
    rank = query_down.shape[1]
    query_part = query_weight.shape[1] // 2
    key_part = key_weight.shape[1] // 2
    part_cols = query_part + 2 * key_part
    order = exchange_order(bits, 0)
    turned_order = exchange_order(bits, 1)

    def other_half(values, axis):
        return jnp.roll(values, values.shape[axis] // 2, axis)

    def sequence_order(values, axis):
        return jnp.where(row == 0, values, other_half(values, axis))

    def rows_of(index):
        return slice(index * BLOCK, (index + 1) * BLOCK)

    lane_blocks = feature_cols // LANES
    direct = lane_blocks == size

    def block_order(which, rows_of_pair=False):
        if not direct:
            return [jnp.int32(p) for p in range(lane_blocks)]
        blocks_of = [device ^ relative_index(p, which) for p in range(size)]
        if rows_of_pair:
            return [((b // (size // 2)) ^ col) * (size // 2) + b % (size // 2) for b in blocks_of]
        return blocks_of

    def places(*orders, rows_of_pair=False):
        entries = [col, row]
        for which in orders:
            entries += block_order(which, rows_of_pair)
        return jnp.stack([jnp.asarray(v, jnp.int32) for v in entries])

    place = places(order)

    def grads_of(sets, right, orders, right_turned=False, cut=(0, 1), pieces=2):
        if not direct:
            sets = [
                (
                    [
                        relative_blocks(
                            left[:, base * LANES : base * LANES + feature_cols], 1, device, which
                        )
                        for left in lefts
                    ],
                    0,
                )
                for (lefts, base), which in zip(sets, orders)
            ]
        outs = weight_grad(places(*orders), sets, right, pieces, False, right_turned, cut)
        return [outs[pieces * n : pieces * (n + 1)] for n in range(len(sets))]

    def ups(index):
        zeros_key = jnp.zeros((rank, key_part), BF16)
        zeros_query = jnp.zeros((rank, query_part), BF16)
        return jnp.concatenate(
            [
                jnp.concatenate([part(query_up, index, 2, 1), zeros_key, zeros_key], axis=1),
                jnp.concatenate([zeros_query, part(key_up, index, 2, 1), zeros_key], axis=1),
                jnp.concatenate([zeros_query, zeros_key, part(value_up, index, 2, 1)], axis=1),
                jnp.zeros((rank, part_cols), BF16),
            ],
            axis=0,
        )

    thin = jnp.concatenate(
        [jnp.transpose(v) for v in (query_down, key_down, value_down)] + [output_up], axis=0
    )
    gains = jnp.stack([first_gain, second_gain])
    inputs_far = swap(activations, "row")
    (
        inputs_other,
        grads_other,
        proj_got,
        gate_got,
        up_got,
        mlp_down_got,
        output_got,
        thin_got,
        gains_got,
        proj_own,
        proj_native,
        output_native,
    ) = exchange(
        activations,
        grad_out,
        (query_weight, key_weight, value_weight),
        gate_weight,
        up_weight,
        down_weight,
        output_weight,
        (thin, gains),
    )
    grads_far = swap(after(grad_out, inputs_far), "row")
    up_own = ups(col)
    up_native = jnp.concatenate([up_own, ups(1 - col)], axis=1)
    second_gain_full = jnp.concatenate([gains[1:], gains_got[1:]], axis=1)
    output_up_full = jnp.concatenate([output_up, thin_got[3 * rank :]], axis=1)
    output_up_full = jnp.pad(output_up_full, ((0, LANES - rank), (0, 0)))
    output_rows_own = part(output_weight, col, 2, 0)
    output_down_own = part(output_down, col, 2, 0)
    output_down_native = jnp.concatenate(
        [output_down_own, part(output_down, 1 - col, 2, 0)], axis=0
    )
    output_down_padded = jnp.pad(output_down_own, ((0, 0), (0, LANES - rank)))
    query_map_own = part(query_map, col, 2, 0)
    key_map_own = part(key_map, col, 2, 0)

    documents = segments[0]
    starts = jnp.sum((documents[None, :] < documents[:, None]).astype(jnp.int32), axis=1)
    marks = jnp.concatenate(
        [
            jnp.full((1,), seq_rows, jnp.int32),
            starts[BLOCK - WINDOW - 1 :: BLOCK],
            jnp.asarray(row, jnp.int32)[None],
        ]
    )
    starts = starts.reshape(1, 1, seq_rows)

    def project(index, mine, other, kept):
        return project_block(
            index,
            place,
            mine,
            other,
            (gains, gains_got),
            (proj_own, proj_got),
            (thin, thin_got),
            up_own,
            query_part,
            kept,
        )

    kept = project(0, activations, inputs_other, ())
    inputs_far = after(inputs_far, kept[0])
    inputs_far_other = swap(inputs_far, "col")
    kept = project(half_blocks, inputs_far, inputs_far_other, kept)
    normed_first, queries, keys_values, adapters, first_scale = kept
    keys_values = jnp.pad(keys_values, ((0, 0), (WINDOW, WINDOW)))
    mixed, inverse = attention_forward(
        marks, starts, queries, keys_values, query_map_own, key_map_own
    )

    mixed, grads_far = lax.optimization_barrier((mixed, grads_far))
    mixed_pair = jnp.concatenate([mixed, swap(mixed, "col")], axis=0)
    adapter_sum = contract(mixed_pair, output_down_native, 0, 0)
    adapter_far = swap(other_half(adapter_sum, 0), "row")
    grads_far_other = swap(after(grads_far, mixed), "col")
    send_order = [(b + half_blocks) % blocks for b in range(blocks)]
    attended, attended_far = [None] * blocks, [None] * blocks
    pair = after(mixed_pair, grads_far)
    for b in send_order:
        attended[b] = contract(pair[:, rows_of(b)], output_native, 0, 0).astype(BF16)
        attended_far[send_order[b]] = swap(after(attended[b], adapter_far), "row")
        pair = after(pair, attended[b])
    out_adapter = (adapter_sum + adapter_far).astype(BF16)
    adapter_padded = jnp.pad(out_adapter, ((0, 0), (0, LANES - rank)))
    attended_other = [swap(attended[0], "col")] + [None] * (blocks - 1)
    d_hidden = hidden_grad(
        place,
        [after(grad_out, *attended, adapter_padded), grads_other, grads_far, grads_far_other],
        down_weight,
        mlp_down_got,
    )

    clock = (d_hidden,)
    kept, state = (), None
    for b in range(blocks):
        far = after(attended_far[b], *clock)
        far_other = swap(far, "col")
        if b + 1 < blocks:
            attended_other[b + 1] = swap(after(attended[b + 1], far), "col")
        inputs = (
            (activations, inputs_other)
            if b < half_blocks
            else (inputs_far, inputs_far_other)
        )
        outs = mlp_block(
            b,
            place,
            inputs,
            b % half_blocks,
            (attended[b], attended_other[b], far, far_other),
            adapter_padded,
            output_up_full,
            second_gain_full,
            gate_weight,
            gate_got,
            up_weight,
            up_got,
            d_hidden,
            kept,
            state,
            b < half_blocks,
        )
        kept = outs[:5]
        state = outs[5] if b < half_blocks else state
        clock = (kept[0],)
    hidden, d_gate, d_up, second_normed, second_scale = kept

    sums = {}

    def reduction(name, pair, which):
        sums[name] = Reduction(*pair, size, which)

    def given(pair, clock):
        return [swap(after(values, *clock), "col") for values in pair]

    def settle(clock, *names):
        for name in names:
            sums[name].got = after(sums[name].got, *clock)
            clock = (sums[name].combine(),)
        return clock

    def scattered(values):
        return lax.psum_scatter(values, "dp", scatter_dimension=0, tiled=True).astype(F32)

    natural = jnp.stack(
        [jnp.asarray(v, jnp.int32) for v in [col, row] + 2 * list(range(lane_blocks))]
    )
    both = [([second_normed], 0), ([second_normed], lane_blocks)]

    def up_grads(right):
        own, other = both
        if not direct:
            columns = second_normed[:, feature_cols:]
            other = ([jnp.concatenate(
                [second_normed[:, :feature_cols], relative_blocks(columns, 1, device, order)], axis=1
            )], lane_blocks)
        entries = [col, row] + list(range(lane_blocks)) + block_order(order)
        table = jnp.stack([jnp.asarray(v, jnp.int32) for v in entries])
        outs = weight_grad(table, [own, other], right, 1)
        half = feature_cols // 2
        return outs[0], (outs[1][:half], outs[1][half:])

    own_gate, other_gate = weight_grad(natural, both, d_gate, 1)
    grad_gate_own = scattered(own_gate)
    got_gate = swap(other_gate, "col")
    own_down, other_down = grads_of(
        [([grad_out, grads_far], 0), ([grads_other, grads_far_other], 0)],
        after(hidden, own_gate),
        (order, turned_order),
    )
    reduction("down_own", own_down, order)
    down_given = given(other_down, ())

    reduction("down_got", down_given, turned_order)
    chip_far = second_grad(
        1, after(d_gate, own_down[0]), d_up, gate_weight, gate_got, up_weight, up_got
    )
    far_got_own = swap(chip_far, "row")
    chip_own = second_grad(
        0, after(d_gate, chip_far), d_up, gate_weight, gate_got, up_weight, up_got
    )
    far_got_far = swap(chip_own, "row")
    grad_gate_got = scattered(after(got_gate, chip_own))
    own_up, other_up = up_grads(after(d_up, chip_own))
    got_up = given(other_up, ())
    y_chip = down_product(after(hidden, own_up), down_weight, mlp_down_got)
    reduction("up_got", [after(v, y_chip) for v in got_up], order)
    clock = settle((y_chip,), "down_own", "down_got")

    totals = []
    for chip, got in ((chip_own, far_got_own), (chip_far, far_got_far)):
        total = (chip.astype(F32) + after(got, *clock).astype(F32)).astype(BF16)
        totals.append(total)
        clock = (total,)
    totals = [(total, swap(after(total, *clock), "col")) for total in totals]

    def back(index, grads, kept):
        return norm_back(
            index,
            place,
            totals[index],
            second_normed,
            second_scale,
            grads,
            second_gain_full,
            output_rows_own,
            output_got,
            output_up_full,
            output_down_padded,
            kept,
            index == 0,
        )

    outs = back(0, (grad_out, grads_other), ())
    kept, gain_sum, grad_state = outs[:3], outs[3], outs[4]
    grad_up_own = scattered(after(own_up, kept[0]))
    outs = back(1, (grads_far, grads_far_other), kept)
    kept = outs[:3]
    d_mixed, d_mine, d_out_padded = kept
    grad_second_gain = (gain_sum + outs[3])[0]
    d_out_adapter = d_out_padded[:, :rank]
    y_far = swap(after(y_chip, kept[0])[half_rows:], "row")
    grad_output_up = contract(out_adapter, d_mine, 0, 0)
    grad_output_down = contract(d_out_adapter, mixed, 0, 1)
    lefts = mixed_pair
    if not direct:
        lefts = relative_blocks(ordered(mixed, mixed_pair[query_part:], col, 0), 0, device, order)
    output_pair = weight_grad(
        places(order, rows_of_pair=True),
        [([lefts], 0)],
        after(d_mine, grad_output_up, grad_output_down),
        2,
        True,
    )
    reduction("output", output_pair, order)
    clock = settle((output_pair[0],), "down_own", "down_got", "up_got")

    d_queries, d_keys, d_values, grad_query_map, grad_key_map = attention_backward(
        marks,
        starts,
        queries,
        keys_values,
        query_map_own,
        key_map_own,
        after(d_mixed, *clock),
        mixed,
        inverse,
    )

    d_parts = (d_queries, d_keys, d_values)
    d_parts += tuple(swap(values, "col") for values in d_parts)
    clock = settle((d_queries,), "down_own", "down_got", "up_got", "output")
    d_first_far, d_first, d_turned, adapter_sum, gain_term = first_back(
        place, (after(d_queries, y_far, *clock),) + d_parts[1:], proj_native, up_native, normed_first
    )
    adapter_far = swap(other_half(adapter_sum, 0), "row")
    gain_far = swap(gain_term, "row")
    (proj_a,) = grads_of([([normed_first], 0)], d_turned, (order,), False, (0, 2), 1)
    (proj_b,) = grads_of(
        [([normed_first], 0)], after(d_turned, proj_a[0]), (turned_order,), False, (1, 2), 1
    )
    adapter_far, gain_far, _ = lax.optimization_barrier((adapter_far, gain_far, proj_b[0]))
    gain_term = (gain_term + gain_far)[0]
    d_adapter = (adapter_sum + adapter_far).astype(BF16)
    grad_down = contract(d_adapter, normed_first[:, :feature_cols], 0, 0)
    grad_up = contract(adapters, d_turned[:, :part_cols], 0, 0)
    down_term = jnp.sum(thin[: 3 * rank].astype(F32) * grad_down[: 3 * rank], axis=0)
    grad_first_gain = (gain_term + down_term) / first_gain
    grad_down = grad_down[: 3 * rank]
    small = (
        grad_first_gain,
        grad_second_gain,
        grad_output_up,
        grad_down,
        grad_output_down,
        grad_up[:rank, :query_part],
        grad_up[rank : 2 * rank, query_part : query_part + key_part],
        grad_up[2 * rank : 3 * rank, query_part + key_part :],
        grad_query_map,
        grad_key_map,
    )
    flat = [values.reshape(-1, LANES) for values in small]
    result = (
        state + y_chip[:half_rows].astype(F32) + y_far.astype(F32)
    ).astype(BF16)
    d_first = d_first + contract(d_adapter[:half_rows], thin, 1, 0)
    packed = after(jnp.concatenate(flat, axis=0), result, d_first)
    clock = settle((packed,), "up_got", "output")
    d_first_far, packed, grad_proj_a, grad_proj_b = finish(
        after(d_first_far, *clock), packed, (proj_a[0], proj_b[0]), (order, turned_order), size
    )
    shared_rows = sum(values.shape[0] for values in flat[:4])
    packed_other = swap(packed[shared_rows:], "col")
    d_first = d_first + d_first_far.astype(F32)
    first_scale = first_scale[:half_rows]
    hat_own = activations.astype(F32) * first_scale
    grad_hat = d_first * first_gain
    inner = jnp.sum(grad_hat * hat_own, axis=1)
    inner = ((inner + swap(inner, "col")) / width)[:, None]
    grad_activations = grad_state + first_scale * (grad_hat - hat_own * inner)
    clock = (packed,)
    while any(not sums[name].done for name in FINISH_ORDER):
        clock = settle(clock, *(name for name in FINISH_ORDER if not sums[name].done))

    def unpacked(index, source, base):
        first = sum(values.shape[0] for values in flat[:index]) - base
        return source[first : first + flat[index].shape[0]].reshape(small[index].shape)

    def joined(index, axis):
        return ordered(
            unpacked(index, packed, 0), unpacked(index, packed_other, shared_rows), col, axis
        )

    down_total = jnp.transpose(unpacked(3, packed, 0))
    proj_grads = [
        ordered(
            grad_proj_a[:, first : first + count],
            grad_proj_b[:, first : first + count],
            col,
            1,
        )
        for first, count in (
            (0, query_part),
            (query_part, key_part),
            (query_part + key_part, key_part),
        )
    ]

    grad_gate = ordered(grad_gate_own, grad_gate_got, col, 1)
    grad_up_weight = ordered(grad_up_own, sums["up_got"].keep, col, 1)
    grad_down_weight = ordered(sums["down_own"].keep, sums["down_got"].keep, col, 1)
    return (
        result,
        grad_activations,
        unpacked(0, packed, 0),
        proj_grads[0],
        proj_grads[1],
        proj_grads[2],
        down_total[:, :rank],
        joined(5, 1),
        down_total[:, rank : 2 * rank],
        joined(6, 1),
        down_total[:, 2 * rank :],
        joined(7, 1),
        joined(8, 0),
        joined(9, 0),
        sums["output"].keep,
        jnp.transpose(joined(4, 1)),
        unpacked(2, packed, 0),
        unpacked(1, packed, 0),
        grad_gate,
        grad_up_weight,
        jnp.transpose(grad_down_weight),
    )


def solution(mesh):
    placed = (
        P(("dp", "row"), "col"),
        P(("dp", "row"), "col"),
        P("dp", None),
        P("col"),
        P("col", "row"),
        P("col", "row"),
        P("col", "row"),
        P("col", None),
        P(None, "row"),
        P("col", None),
        P(None, "row"),
        P("col", None),
        P(None, "row"),
        P("row", None, None),
        P("row", None, None),
        P("row", "col"),
        P("row", None),
        P(None, "col"),
        P("col"),
        P("col", "row"),
        P("col", "row"),
        P("row", "col"),
    )
    return jax.shard_map(
        on_device,
        mesh=mesh,
        in_specs=placed,
        out_specs=(
            P(("dp", "row"), "col"),
            P(("dp", "row"), "col"),
            P("col"),
            P(("col", "dp"), "row"),
            P(("col", "dp"), "row"),
            P(("col", "dp"), "row"),
            P("col", None),
            P(None, "row"),
            P("col", None),
            P(None, "row"),
            P("col", None),
            P(None, "row"),
            P("row", None, None),
            P("row", None, None),
            P(("row", "dp"), "col"),
            P("row", None),
            P(None, "col"),
            P("col"),
            P(("col", "dp"), "row"),
            P(("col", "dp"), "row"),
            P("row", ("col", "dp")),
        ),
        check_vma=False,
    )
```

```python
import functools
import jax
import jax.numpy as jnp
from jax import lax
from jax.experimental import pallas as pl
from jax.experimental.pallas import tpu as pltpu
from jax.sharding import PartitionSpec as P

HEAD_DIM = 64
WINDOW = 64
BLOCK = 512
SUB = 128
SCALE = 0.125
NSUB = BLOCK // SUB
LANES = 128
MLP_TILE = 512
SUM_TILE = 256
GRAD_TILE = 512
VMEM_LIMIT = 56 * 1024 * 1024
norm_eps = 1e-05
F32 = jnp.float32
BF16 = jnp.bfloat16


def dot_nn(left, right):
    return lax.dot_general(left, right, (((1,), (0,)), ((), ())), preferred_element_type=F32)


def dot_nt(left, right):
    return lax.dot_general(left, right, (((1,), (1,)), ((), ())), preferred_element_type=F32)


def softmax_halves(before):
    def soft(values):
        powers = jnp.exp(values - jnp.max(values, axis=0, keepdims=True))
        return powers * (1.0 / jnp.sum(powers, axis=0, keepdims=True))

    return jnp.concatenate([soft(before[:HEAD_DIM]), soft(before[HEAD_DIM:])], axis=0)


def halves_backward(probs, grads):
    def half(p, g):
        return p * (g - jnp.sum(p * g, axis=0, keepdims=True))

    return half(probs[:HEAD_DIM], grads[:HEAD_DIM]) - half(probs[HEAD_DIM:], grads[HEAD_DIM:])


def side_by_side(parts, sub):
    return jnp.concatenate([part[:, sub * SUB : (sub + 1) * SUB] for part in parts], axis=1)


def key_side(kt_ref, vt_ref, kmap_ref, kft_ref, kfr_ref, kr_ref, vr_ref):
    features = softmax_halves(dot_nn(kmap_ref[0], kt_ref[...])).astype(BF16)
    kft_ref[...] = features
    kfr_ref[...] = jnp.transpose(features)
    kr_ref[...] = jnp.transpose(kt_ref[...])
    if vr_ref is not None:
        vr_ref[...] = jnp.transpose(vt_ref[...])


def tile_rows(start_ref, base, sub, ratio):
    low_one = start_ref[0, :, sub * SUB : (sub + 1) * SUB] + (WINDOW - base)
    low = jnp.concatenate([low_one] * ratio, axis=1)
    width = ratio * SUB
    place = sub * SUB + (lax.broadcasted_iota(jnp.int32, (1, width), 1) & (SUB - 1))
    same = jnp.where(low <= -1, 1.0, 0.0)
    return low, place, same


def tile_weights(kfr_ref, kr_ref, base, sub, low, place, q_sub, qf_sub):
    width = q_sub.shape[1]
    first = sub * SUB
    lin_keys = first + SUB
    win_keys = SUB + WINDOW
    link = dot_nn(kfr_ref[pl.ds(base, lin_keys), :], qf_sub)
    score = dot_nn(kr_ref[pl.ds(base + first, win_keys), :], q_sub) * SCALE
    lin_at = lax.broadcasted_iota(jnp.int32, (lin_keys, width), 0)
    win_at = lax.broadcasted_iota(jnp.int32, (win_keys, width), 0) + first
    lin_mask = (lin_at >= low) & (lin_at <= place)
    win_mask = (win_at >= jnp.maximum(low, place + 1)) & (win_at <= place + WINDOW)
    lin = jnp.where(lin_mask, link, 0.0)
    win = jnp.where(win_mask, jnp.exp(score), 0.0)
    return lin, win, lin_mask, win_mask


def member_lanes(base, mark):
    at = lax.broadcasted_iota(jnp.int32, (1, BLOCK), 1) + (base - WINDOW)
    return at >= mark


def forward_kernel(
    mark_ref, start_ref, qt_ref, kt_ref, vt_ref, qmap_ref, kmap_ref, mix_ref, inv_ref,
    kft_ref, kfr_ref, kr_ref, state_ref, norm_ref,
):
    b = pl.program_id(1)
    ratio = qmap_ref.shape[0]
    base = pl.multiple_of(b * BLOCK, BLOCK)

    @pl.when(b == 0)
    def _():
        key_side(kt_ref, vt_ref, kmap_ref, kft_ref, kfr_ref, kr_ref, None)
        state_ref[...] = jnp.zeros_like(state_ref)
        norm_ref[...] = jnp.zeros_like(norm_ref)

    queries = [qt_ref[h * HEAD_DIM : (h + 1) * HEAD_DIM, :] for h in range(ratio)]
    features = [softmax_halves(dot_nn(qmap_ref[h], queries[h])).astype(BF16) for h in range(ratio)]
    state_low = state_ref[...].astype(BF16)
    norm = norm_ref[...]
    for sub in range(NSUB):
        first = sub * SUB
        q_sub = side_by_side(queries, sub)
        qf_sub = side_by_side(features, sub)
        low, place, same = tile_rows(start_ref, base, sub, ratio)
        lin, win, _, _ = tile_weights(kfr_ref, kr_ref, base, sub, low, place, q_sub, qf_sub)
        carried = dot_nn(state_low, qf_sub)
        normal = jnp.sum(qf_sub.astype(F32) * norm, axis=0, keepdims=True)
        total = (
            jnp.sum(lin, axis=0, keepdims=True) + jnp.sum(win, axis=0, keepdims=True) + same * normal
        )
        inverse = 1.0 / total
        mixed = dot_nn(vt_ref[:, pl.ds(base, first + SUB)], lin.astype(BF16))
        mixed += dot_nn(vt_ref[:, pl.ds(base + first, SUB + WINDOW)], win.astype(BF16))
        mixed = ((mixed + same * carried) * inverse).astype(BF16)
        for h in range(ratio):
            lanes = slice(h * SUB, (h + 1) * SUB)
            mix_ref[h * HEAD_DIM : (h + 1) * HEAD_DIM, first : first + SUB] = mixed[:, lanes]
            inv_ref[0, h : h + 1, first : first + SUB] = inverse[:, lanes]

    mark = mark_ref[b + 1]
    keep = jnp.where((mark <= b * BLOCK - WINDOW - 1), 1.0, 0.0)
    tile = kft_ref[:, pl.ds(base, BLOCK)]
    member = jnp.where(member_lanes(base, mark), tile, jnp.zeros_like(tile))
    state_ref[...] = keep * state_ref[...] + dot_nt(vt_ref[:, pl.ds(base, BLOCK)], member)
    norm_ref[...] = keep * norm + jnp.sum(member.astype(F32), axis=1, keepdims=True)


def packed_map(grad):
    half = grad.shape[0] // 2
    return jnp.concatenate([grad[:half], grad[half:]], axis=1)


def backward_kernel(
    mark_ref, start_ref, qt_ref, kt_ref, vt_ref, qmap_ref, kmap_ref, dmt_ref, mix_ref, inv_ref,
    qback_ref, kback_ref,
    dqt_ref, dkt_ref, dvt_ref, gqm_ref, gkm_ref,
    kft_ref, kfr_ref, kr_ref, vr_ref, states_ref, statet_ref, norms_ref,
    dk_acc, dkf_acc, dv_acc, dst_ref, dstt_ref, dnorm_ref,
):
    step = pl.program_id(1)
    blocks = pl.num_programs(1)
    count = states_ref.shape[0]
    b = blocks - 1 - step
    ratio = qmap_ref.shape[0]
    base = pl.multiple_of(b * BLOCK, BLOCK)

    @pl.when(step == 0)
    def _():
        key_side(kt_ref, vt_ref, kmap_ref, kft_ref, kfr_ref, kr_ref, vr_ref)
        state = jnp.zeros(statet_ref.shape[1:], F32)
        norm = jnp.zeros(norms_ref.shape[1:], F32)
        statet = jnp.zeros(states_ref.shape[1:], F32)
        for i in range(count):
            statet_ref[i] = state.astype(BF16)
            states_ref[i] = statet.astype(BF16)
            norms_ref[i] = norm
            if i + 1 < count:
                mark = mark_ref[i + 1]
                keep = jnp.where((mark <= i * BLOCK - WINDOW - 1), 1.0, 0.0)
                tile = kft_ref[:, i * BLOCK : (i + 1) * BLOCK]
                member = jnp.where(member_lanes(i * BLOCK, mark), tile, jnp.zeros_like(tile))
                values = vt_ref[:, i * BLOCK : (i + 1) * BLOCK]
                state = keep * state + dot_nt(values, member)
                statet = keep * statet + dot_nt(member, values)
                norm = keep * norm + jnp.sum(member.astype(F32), axis=1, keepdims=True)
        dk_acc[...] = jnp.zeros_like(dk_acc)
        dkf_acc[...] = jnp.zeros_like(dkf_acc)
        dv_acc[...] = jnp.zeros_like(dv_acc)
        dst_ref[...] = jnp.zeros_like(dst_ref)
        dstt_ref[...] = jnp.zeros_like(dstt_ref)
        dnorm_ref[...] = jnp.zeros_like(dnorm_ref)
        gqm_ref[...] = jnp.zeros_like(gqm_ref)

    mark = mark_ref[b + 1]
    keep = jnp.where((mark <= b * BLOCK - WINDOW - 1), 1.0, 0.0)
    tile_lanes = pl.ds(base, BLOCK)
    member = member_lanes(base, mark)
    dst_low = dst_ref[...].astype(BF16)
    dstt_low = dstt_ref[...].astype(BF16)
    dkf_acc[:, tile_lanes] += jnp.where(
        member, dot_nn(dst_low, vt_ref[:, tile_lanes]) + dnorm_ref[...], 0.0
    )
    dv_acc[:, tile_lanes] += jnp.where(member, dot_nn(dstt_low, kft_ref[:, tile_lanes]), 0.0)

    queries = [qt_ref[h * HEAD_DIM : (h + 1) * HEAD_DIM, :] for h in range(ratio)]
    gradients = [dmt_ref[h * HEAD_DIM : (h + 1) * HEAD_DIM, :] for h in range(ratio)]
    mixes = [mix_ref[h * HEAD_DIM : (h + 1) * HEAD_DIM, :] for h in range(ratio)]
    inverses = [inv_ref[0, h : h + 1, :] for h in range(ratio)]
    probabilities = [softmax_halves(dot_nn(qmap_ref[h], queries[h])) for h in range(ratio)]
    features = [p.astype(BF16) for p in probabilities]
    norm = norms_ref[b]
    state_low = states_ref[b]
    dnorm = jnp.zeros((2 * HEAD_DIM, SUB), F32)
    dst = keep * dst_ref[...]
    dstt = keep * dstt_ref[...]
    dq_parts, dpre_parts = [], []
    for sub in range(NSUB):
        first = sub * SUB
        lin_lanes = pl.ds(base, first + SUB)
        win_lanes = pl.ds(base + first, SUB + WINDOW)
        q_sub = side_by_side(queries, sub)
        qf_sub = side_by_side(features, sub)
        dm_sub = side_by_side(gradients, sub)
        inverse = side_by_side(inverses, sub)
        dm_float = dm_sub.astype(F32)
        low, place, same = tile_rows(start_ref, base, sub, ratio)
        lin, win, lin_mask, win_mask = tile_weights(
            kfr_ref, kr_ref, base, sub, low, place, q_sub, qf_sub
        )
        delta = jnp.sum(dm_float * side_by_side(mixes, sub).astype(F32), axis=0, keepdims=True)
        dv_acc[:, lin_lanes] += dot_nt(dm_sub, (lin * inverse).astype(BF16))
        dv_acc[:, win_lanes] += dot_nt(dm_sub, (win * inverse).astype(BF16))
        dlin = (dot_nn(vr_ref[lin_lanes, :], dm_sub) - delta) * inverse
        dwin = (dot_nn(vr_ref[win_lanes, :], dm_sub) - delta) * inverse
        dlink = jnp.where(lin_mask, dlin, 0.0).astype(BF16)
        dscore = (win * dwin).astype(BF16)
        dcarried = (dm_float * (same * inverse)).astype(BF16)
        dtotal = -delta * (same * inverse)
        dk_acc[:, win_lanes] += dot_nt(q_sub, dscore)
        dkf_acc[:, lin_lanes] += dot_nt(qf_sub, dlink)
        dq_parts.append(dot_nn(kt_ref[:, win_lanes], dscore) * SCALE)
        dqf = dot_nn(kft_ref[:, lin_lanes], dlink) + dot_nn(state_low, dcarried) + norm * dtotal
        dst = dst + dot_nt(qf_sub, dcarried)
        dstt = dstt + dot_nt(dcarried, qf_sub)
        weighted = qf_sub.astype(F32) * dtotal
        for h in range(ratio):
            dnorm = dnorm + weighted[:, h * SUB : (h + 1) * SUB]
        dpre_parts.append(halves_backward(side_by_side(probabilities, sub), dqf).astype(BF16))
    dst_ref[...] = dst.astype(BF16).astype(F32)
    dstt_ref[...] = dstt.astype(BF16).astype(F32)
    dnorm_ref[...] = jnp.sum(dnorm, axis=1, keepdims=True) + keep * dnorm_ref[...]
    for h in range(ratio):
        lanes = slice(h * SUB, (h + 1) * SUB)
        dpre = jnp.concatenate([part[:, lanes] for part in dpre_parts], axis=1)
        dq = jnp.concatenate([part[:, lanes] for part in dq_parts], axis=1)
        dq = dq + dot_nn(qback_ref[h], dpre)
        dqt_ref[h * HEAD_DIM : (h + 1) * HEAD_DIM, :] = dq.astype(BF16)
        gqm_ref[h] += packed_map(dot_nt(queries[h], dpre))

    @pl.when(step == blocks - 1)
    def _():
        key_probs = softmax_halves(dot_nn(kmap_ref[0], kt_ref[...]))
        dpre = halves_backward(key_probs, dkf_acc[...]).astype(BF16)
        dk = (dk_acc[...] * SCALE + dot_nn(kback_ref[0], dpre)).astype(BF16)
        dv = dv_acc[...].astype(BF16)
        half = dkt_ref.shape[1] // 2
        flip = mark_ref[count + 1]
        for i in range(2):
            lanes = pl.ds(pl.multiple_of((i ^ flip) * half, half), half)
            dkt_ref[:, lanes] = dk[:, WINDOW + i * half : WINDOW + (i + 1) * half]
            dvt_ref[:, lanes] = dv[:, WINDOW + i * half : WINDOW + (i + 1) * half]
        gkm_ref[0] = packed_map(dot_nt(kt_ref[...], dpre))


def signed_maps(maps):
    turned = jnp.swapaxes(maps, 1, 2)
    return jnp.concatenate([turned, -turned], axis=1)


def local_block(block, marks, blocks):
    half = blocks // 2
    return ((block // half) ^ marks[blocks + 1]) * half + block % half


def attention_specs(groups, ratio, padded, block_of):
    rows = ratio * HEAD_DIM
    return [
        pl.BlockSpec((1, 1, BLOCK), lambda g, i, *_: (0, 0, block_of(i))),
        pl.BlockSpec((rows, BLOCK), lambda g, i, *_: (g, block_of(i))),
        pl.BlockSpec((HEAD_DIM, padded), lambda g, i, *_: (g, 0)),
        pl.BlockSpec((HEAD_DIM, padded), lambda g, i, *_: (groups + g, 0)),
        pl.BlockSpec((ratio, 2 * HEAD_DIM, HEAD_DIM), lambda g, i, *_: (g, 0, 0)),
        pl.BlockSpec((1, 2 * HEAD_DIM, HEAD_DIM), lambda g, i, *_: (g, 0, 0)),
    ]


def attention_forward(marks, starts, qt, kvt, qmap, kmap):
    length = qt.shape[1]
    padded = kvt.shape[1]
    groups = kmap.shape[0]
    ratio = qmap.shape[0] // groups
    rows = ratio * HEAD_DIM
    blocks = length // BLOCK
    return pl.pallas_call(
        forward_kernel,
        out_shape=(
            jax.ShapeDtypeStruct(qt.shape, BF16),
            jax.ShapeDtypeStruct((groups, ratio, length), F32),
        ),
        grid_spec=pltpu.PrefetchScalarGridSpec(
            num_scalar_prefetch=1,
            grid=(groups, blocks),
            in_specs=attention_specs(groups, ratio, padded, lambda i: i),
            out_specs=[
                pl.BlockSpec((rows, BLOCK), lambda g, i, s: (g, local_block(i, s, blocks))),
                pl.BlockSpec((1, ratio, BLOCK), lambda g, i, *_: (g, 0, i)),
            ],
            scratch_shapes=[
                pltpu.VMEM((2 * HEAD_DIM, padded), BF16),
                pltpu.VMEM((padded, 2 * HEAD_DIM), BF16),
                pltpu.VMEM((padded, HEAD_DIM), BF16),
                pltpu.VMEM((HEAD_DIM, 2 * HEAD_DIM), F32),
                pltpu.VMEM((2 * HEAD_DIM, 1), F32),
            ],
        ),
        compiler_params=pltpu.CompilerParams(
            dimension_semantics=("arbitrary", "arbitrary"), vmem_limit_bytes=48 * 1024 * 1024
        ),
        cost_estimate=pl.CostEstimate(flops=1000, bytes_accessed=1000, transcendentals=0),
        name="attention_forward",
    )(marks, starts, qt, kvt, kvt, signed_maps(qmap), signed_maps(kmap))


def attention_backward(marks, starts, qt, kvt, qmap, kmap, dmt, mixt, inverse):
    length = qt.shape[1]
    padded = kvt.shape[1]
    groups = kmap.shape[0]
    ratio = qmap.shape[0] // groups
    rows = ratio * HEAD_DIM
    blocks = length // BLOCK
    back = lambda i: blocks - 1 - i
    query_spec = pl.BlockSpec((rows, BLOCK), lambda g, i, *_: (g, back(i)))
    local_spec = pl.BlockSpec((rows, BLOCK), lambda g, i, s: (g, local_block(back(i), s, blocks)))
    key_spec = pl.BlockSpec((HEAD_DIM, length), lambda g, i, *_: (g, 0))
    return pl.pallas_call(
        backward_kernel,
        out_shape=(
            jax.ShapeDtypeStruct(qt.shape, BF16),
            jax.ShapeDtypeStruct((groups * HEAD_DIM, length), BF16),
            jax.ShapeDtypeStruct((groups * HEAD_DIM, length), BF16),
            jax.ShapeDtypeStruct((qmap.shape[0], HEAD_DIM // 2, 2 * HEAD_DIM), F32),
            jax.ShapeDtypeStruct((kmap.shape[0], HEAD_DIM // 2, 2 * HEAD_DIM), F32),
        ),
        grid_spec=pltpu.PrefetchScalarGridSpec(
            num_scalar_prefetch=1,
            grid=(groups, blocks),
            in_specs=attention_specs(groups, ratio, padded, back)
            + [
                query_spec,
                local_spec,
                pl.BlockSpec((1, ratio, BLOCK), lambda g, i, *_: (g, 0, back(i))),
                pl.BlockSpec((ratio, HEAD_DIM, HEAD_DIM), lambda g, i, *_: (g, 0, 0)),
                pl.BlockSpec((1, HEAD_DIM, HEAD_DIM), lambda g, i, *_: (g, 0, 0)),
            ],
            out_specs=[
                local_spec,
                key_spec,
                key_spec,
                pl.BlockSpec((ratio, HEAD_DIM // 2, 2 * HEAD_DIM), lambda g, i, *_: (g, 0, 0)),
                pl.BlockSpec((1, HEAD_DIM // 2, 2 * HEAD_DIM), lambda g, i, *_: (g, 0, 0)),
            ],
            scratch_shapes=[
                pltpu.VMEM((2 * HEAD_DIM, padded), BF16),
                pltpu.VMEM((padded, 2 * HEAD_DIM), BF16),
                pltpu.VMEM((padded, HEAD_DIM), BF16),
                pltpu.VMEM((padded, HEAD_DIM), BF16),
                pltpu.VMEM((blocks, 2 * HEAD_DIM, HEAD_DIM), BF16),
                pltpu.VMEM((blocks, HEAD_DIM, 2 * HEAD_DIM), BF16),
                pltpu.VMEM((blocks, 2 * HEAD_DIM, 1), F32),
                pltpu.VMEM((HEAD_DIM, padded), F32),
                pltpu.VMEM((2 * HEAD_DIM, padded), F32),
                pltpu.VMEM((HEAD_DIM, padded), F32),
                pltpu.VMEM((2 * HEAD_DIM, HEAD_DIM), F32),
                pltpu.VMEM((HEAD_DIM, 2 * HEAD_DIM), F32),
                pltpu.VMEM((2 * HEAD_DIM, 1), F32),
            ],
        ),
        compiler_params=pltpu.CompilerParams(
            dimension_semantics=("arbitrary", "arbitrary"), vmem_limit_bytes=48 * 1024 * 1024
        ),
        cost_estimate=pl.CostEstimate(flops=1000, bytes_accessed=1000, transcendentals=0),
        name="attention_backward",
    )(
        marks, starts, qt, kvt, kvt, signed_maps(qmap), signed_maps(kmap), dmt, mixt, inverse, qmap, kmap
    )


FREE = pl.CostEstimate(flops=1000, bytes_accessed=1000, transcendentals=0)


def grid_call(kernel, name, grid, out_shape, in_specs, out_specs, scratch=(), aliases=None):
    return pl.pallas_call(
        kernel,
        out_shape=out_shape,
        grid_spec=pltpu.PrefetchScalarGridSpec(
            num_scalar_prefetch=1,
            grid=grid,
            in_specs=in_specs,
            out_specs=out_specs,
            scratch_shapes=list(scratch),
        ),
        input_output_aliases=aliases or {},
        compiler_params=pltpu.CompilerParams(
            dimension_semantics=("arbitrary",) * len(grid), vmem_limit_bytes=VMEM_LIMIT
        ),
        cost_estimate=FREE,
        name=name,
    )


MESH = pl.DeviceIdType.MESH


def exchange_kernel(query_cols, key_cols, *refs):
    inputs, grads, query, key, value, gate, up, down, output = refs[:9]
    thin = refs[9:11]
    near_other, grads_other, proj_got, gate_got, up_got, down_got, output_got = refs[11:18]
    thin_got = refs[18:20]
    proj_own, proj_both, output_both = refs[20:23]
    send_sem, recv_sem, local_sem, proj_all, output_all = refs[23:]
    col = lax.axis_index("col")

    barrier = pltpu.get_barrier_semaphore()
    pl.semaphore_signal(barrier, inc=1, device_id={"col": 1 - col}, device_id_type=MESH)
    pl.semaphore_wait(barrier, 1)

    copies = []

    def remote(source, target):
        n = len(copies)
        copy = pltpu.make_async_remote_copy(
            src_ref=source,
            dst_ref=target,
            send_sem=send_sem.at[n],
            recv_sem=recv_sem.at[n],
            device_id={"col": 1 - col},
            device_id_type=MESH,
        )
        copy.start()
        copies.append(copy)

    def columns(ref, index, width):
        return ref.at[:, pl.ds(pl.multiple_of(index * width, width), width)]

    def rows_of(ref, index, height):
        return ref.at[pl.ds(pl.multiple_of(index * height, height), height), :]

    remote(inputs, near_other)
    first = 0
    for weight, width in ((query, query_cols), (key, key_cols), (value, key_cols)):
        remote(columns(weight, 1 - col, width), proj_got.at[:, pl.ds(first, width)])
        first += width
    for source, target in zip(thin, thin_got):
        remote(source, target)
    remote(columns(gate, 1 - col, gate_got.shape[1]), gate_got)
    remote(columns(up, 1 - col, up_got.shape[1]), up_got)
    remote(rows_of(down, 1 - col, down_got.shape[0]), down_got)
    remote(rows_of(output, 1 - col, output_got.shape[0]), output_got)
    remote(grads, grads_other)

    def local(source, target, n):
        copy = pltpu.make_async_copy(source, target, local_sem.at[n])
        copy.start()
        return copy

    whole = proj_own.shape[1]
    height = output_got.shape[0]
    loads, first = [], 0
    for weight, width in ((query, query_cols), (key, key_cols), (value, key_cols)):
        for side in range(2):
            loads.append(
                local(
                    columns(weight, col ^ side, width),
                    proj_all.at[:, pl.ds(side * whole + first, width)],
                    len(loads),
                )
            )
        first += width
    for side in range(2):
        loads.append(
            local(
                rows_of(output, col ^ side, height),
                output_all.at[pl.ds(side * height, height), :],
                len(loads),
            )
        )
    for copy in loads:
        copy.wait()
    stores = [
        local(proj_all.at[:, pl.ds(0, whole)], proj_own, 8),
        local(proj_all, proj_both, 9),
        local(output_all, output_both, 10),
    ]

    for copy in stores:
        copy.wait()
    for copy in copies:
        copy.wait()


def exchange(inputs, grads, projections, gate, up, down, output, thin):
    query, key, value = projections
    rows, half = inputs.shape
    query_cols, key_cols = query.shape[1] // 2, key.shape[1] // 2
    columns = query_cols + 2 * key_cols
    like = lambda *shape: jax.ShapeDtypeStruct(shape, BF16)
    outs = [
        like(rows, half),
        like(rows, half),
        like(half, columns),
        like(half, gate.shape[1] // 2),
        like(half, up.shape[1] // 2),
        like(down.shape[0] // 2, half),
        like(output.shape[0] // 2, half),
    ]
    outs += [jax.ShapeDtypeStruct(values.shape, values.dtype) for values in thin]
    outs += [like(half, columns), like(half, 2 * columns), like(output.shape[0], half)]
    copies = 1 + 3 + len(thin) + 5
    return pl.pallas_call(
        functools.partial(exchange_kernel, query_cols, key_cols),
        out_shape=tuple(outs),
        in_specs=[pl.BlockSpec(memory_space=pl.ANY)] * (9 + len(thin)),
        out_specs=tuple([pl.BlockSpec(memory_space=pl.ANY)] * len(outs)),
        scratch_shapes=[
            pltpu.SemaphoreType.DMA((copies,)),
            pltpu.SemaphoreType.DMA((copies,)),
            pltpu.SemaphoreType.DMA((11,)),
            pltpu.VMEM((half, 2 * columns), BF16),
            pltpu.VMEM(output.shape, BF16),
        ],
        compiler_params=pltpu.CompilerParams(
            collective_id=0, has_side_effects=True, vmem_limit_bytes=VMEM_LIMIT
        ),
        cost_estimate=FREE,
        name="exchange",
    )(inputs, grads, query, key, value, gate, up, down, output, *thin)


def hidden_grad_kernel(place_ref, mine, other, down_own, down_got, *refs):
    refs[-1][...] = (
        dot_nt(mine[...], down_own[...]) + dot_nt(other[...], down_got[...])
    ).astype(BF16)


def hidden_grad(index, place, grads, down_weight, down_got, kept):
    half, width = grads[0].shape
    hidden_cols = down_got.shape[0]
    tiles = hidden_cols // MLP_TILE
    whole = pl.BlockSpec((half, width), lambda i, s: (0, 0))
    return grid_call(
        hidden_grad_kernel,
        "hidden_grad",
        (tiles,),
        jax.ShapeDtypeStruct((2 * half, hidden_cols), BF16),
        [whole] * 2
        + [
            pl.BlockSpec((MLP_TILE, width), lambda i, s: (s[0] * tiles + i, 0)),
            pl.BlockSpec((MLP_TILE, width), lambda i, s: (i, 0)),
        ]
        + [pl.BlockSpec(memory_space=pl.ANY)] * len(kept),
        pl.BlockSpec((half, MLP_TILE), lambda i, s: (index, i)),
        aliases={5 + i: i for i in range(len(kept))},
    )(place, *grads, down_weight, down_got, *kept)


def project_kernel(
    place_ref,
    mine_ref,
    other_ref,
    gain_ref,
    gain_got_ref,
    proj_own,
    proj_got,
    thin_ref,
    thin_got_ref,
    up_ref,
    *refs,
):
    normed_ref, queries_ref, keys_ref, adapters_ref, scale_ref = refs[-5:]
    half = mine_ref.shape[1]
    mine, other = mine_ref[...].astype(F32), other_ref[...].astype(F32)
    squares = jnp.sum(mine * mine, axis=1, keepdims=True) + jnp.sum(
        other * other, axis=1, keepdims=True
    )
    scale = lax.rsqrt(squares / (2 * half) + norm_eps)
    left = (mine * scale * gain_ref[:1, :]).astype(BF16)
    right = (other * scale * gain_got_ref[:1, :]).astype(BF16)
    normed_ref[:, :half] = left
    normed_ref[:, half:] = right
    scale_ref[...] = scale
    adapters = (dot_nt(left, thin_ref[...]) + dot_nt(right, thin_got_ref[...])).astype(BF16)
    adapters_ref[...] = adapters
    sums = dot_nn(left, proj_own[...]) + dot_nn(right, proj_got[...]) + dot_nn(adapters, up_ref[...])
    turned = jnp.transpose(sums.astype(BF16))
    rows = queries_ref.shape[0]
    queries_ref[...] = turned[:rows]
    keys_ref[...] = turned[rows:]


def global_block(local, flip, half_blocks):
    return ((local // half_blocks) ^ flip) * half_blocks + local % half_blocks


def project_block(index, place, mine, other, gains, projections, thin, up, query_part, kept):
    proj_own, proj_got = projections
    rows, half = mine.shape
    length = 2 * half_rows_of(kept, rows)
    blocks, half_blocks = length // BLOCK, length // BLOCK // 2
    columns = proj_own.shape[1]
    whole = lambda values: pl.BlockSpec(values.shape, lambda i, s: (0, 0))
    lanes = lambda i, s: (0, global_block(index + i, s[1], half_blocks))
    local = lambda i, s: (index + i, 0)
    shapes = (
        jax.ShapeDtypeStruct((length, 2 * half), BF16),
        jax.ShapeDtypeStruct((query_part, length), BF16),
        jax.ShapeDtypeStruct((columns - query_part, length), BF16),
        jax.ShapeDtypeStruct((length, up.shape[0]), BF16),
        jax.ShapeDtypeStruct((length, 1), F32),
    )
    operands = (mine, other, *gains, proj_own, proj_got, *thin, up)
    return grid_call(
        project_kernel,
        "project_block",
        (rows // BLOCK,),
        shapes,
        [
            pl.BlockSpec((BLOCK, half), lambda i, s: (i, 0)),
            pl.BlockSpec((BLOCK, half), lambda i, s: (i, 0)),
        ]
        + [whole(values) for values in operands[2:]]
        + [pl.BlockSpec(memory_space=pl.ANY)] * len(kept),
        [
            pl.BlockSpec((BLOCK, 2 * half), local),
            pl.BlockSpec((query_part, BLOCK), lanes),
            pl.BlockSpec((columns - query_part, BLOCK), lanes),
            pl.BlockSpec((BLOCK, up.shape[0]), local),
            pl.BlockSpec((BLOCK, 1), local),
        ],
        aliases={1 + len(operands) + i: i for i in range(len(kept))},
    )(place, *operands, *kept)


def half_rows_of(kept, rows):
    return kept[0].shape[0] // 2 if kept else rows


def mlp_kernel(
    count,
    place_ref,
    in_mine,
    in_other,
    at_mine,
    at_other,
    far_mine,
    far_other,
    adapter_ref,
    up_ref,
    gain_ref,
    gate_own,
    gate_got,
    up_own,
    up_got,
    dh_ref,
    *refs,
):
    hidden_ref, dgate_ref, dup_ref, normed_ref, scale_ref = refs[-1 - count : -1][:5]
    left_ref = refs[-1]
    half = in_mine.shape[1]

    @pl.when(pl.program_id(0) == 0)
    def _():
        def state(inputs, own, far, adapted):
            return inputs[...].astype(F32) + (
                own[...].astype(F32) + far[...].astype(F32) + adapted
            )

        adapter = adapter_ref[...]
        mine = state(in_mine, at_mine, far_mine, dot_nn(adapter, up_ref[:, :half]))
        other = state(in_other, at_other, far_other, dot_nn(adapter, up_ref[:, half:]))
        squares = jnp.sum(mine * mine, axis=1, keepdims=True) + jnp.sum(
            other * other, axis=1, keepdims=True
        )
        scale = lax.rsqrt(squares / (2 * half) + norm_eps)
        scale_ref[...] = scale
        if count == 6:
            refs[-2][...] = mine
        left_ref[:, :half] = (mine * scale * gain_ref[:, :half]).astype(BF16)
        left_ref[:, half:] = (other * scale * gain_ref[:, half:]).astype(BF16)
        normed_ref[...] = left_ref[...]

    left, right = left_ref[:, :half], left_ref[:, half:]
    gate = dot_nn(left, gate_own[...]) + dot_nn(right, gate_got[...])
    up = dot_nn(left, up_own[...]) + dot_nn(right, up_got[...])
    d_hidden = dh_ref[...].astype(F32)
    sig = 1.0 / (1.0 + jnp.exp(-gate))
    silu = gate * sig
    hidden_ref[...] = (silu * up).astype(BF16)
    dup_ref[...] = (d_hidden * silu).astype(BF16)
    dgate_ref[...] = (d_hidden * up * (sig * (1.0 + gate * (1.0 - sig)))).astype(BF16)


def mlp_block(
    index,
    place,
    inputs,
    input_block,
    attended,
    adapter,
    output_up,
    gain,
    gate_weight,
    gate_got,
    up_weight,
    up_got,
    d_hidden,
    kept,
    state_kept,
    with_state,
):
    half, hidden_cols = gate_got.shape
    width = 2 * half
    length = d_hidden.shape[0]
    tiles = hidden_cols // MLP_TILE
    own_spec = pl.BlockSpec((half, MLP_TILE), lambda i, s: (0, s[0] * tiles + i))
    got_spec = pl.BlockSpec((half, MLP_TILE), lambda i, s: (0, i))
    kept_spec = pl.BlockSpec((BLOCK, MLP_TILE), lambda i, s: (index, i))
    here = lambda columns: pl.BlockSpec((BLOCK, columns), lambda i, s: (index, 0))
    whole = lambda values: pl.BlockSpec(values.shape, lambda i, s: (0, 0))
    input_spec = pl.BlockSpec((BLOCK, half), lambda i, s: (input_block, 0))
    block_spec = pl.BlockSpec((BLOCK, half), lambda i, s: (0, 0))
    shapes = (jax.ShapeDtypeStruct((length, hidden_cols), BF16),) * 3 + (
        jax.ShapeDtypeStruct((length, width), BF16),
        jax.ShapeDtypeStruct((length, 1), F32),
    )
    out_specs = [kept_spec] * 3 + [here(width), here(1)]
    aliases = {15 + i: i for i in range(len(kept))}
    passed = tuple(kept)
    if with_state:
        shapes += (jax.ShapeDtypeStruct((length // 2, half), F32),)
        out_specs.append(here(half))
        if state_kept is not None:
            aliases[15 + len(passed)] = 5
            passed += (state_kept,)
    return grid_call(
        functools.partial(mlp_kernel, len(shapes)),
        "mlp_block",
        (tiles,),
        shapes,
        [input_spec, input_spec]
        + [block_spec] * 4
        + [here(adapter.shape[1]), whole(output_up), whole(gain)]
        + [own_spec, got_spec, own_spec, got_spec, kept_spec]
        + [pl.BlockSpec(memory_space=pl.ANY)] * len(passed),
        out_specs,
        [pltpu.VMEM((BLOCK, width), BF16)],
        aliases,
    )(
        place,
        *inputs,
        *attended,
        adapter,
        output_up,
        gain,
        gate_weight,
        gate_got,
        up_weight,
        up_got,
        d_hidden,
        *passed,
    )


def norm_back_kernel(
    count,
    place_ref,
    total_mine,
    total_other,
    normed_ref,
    scale_ref,
    grad_mine,
    grad_other,
    gain_ref,
    out_own,
    out_got,
    up_ref,
    down_ref,
    *refs,
):
    mixed_ref, mine_ref, adapter_ref, gain_sum = refs[-count:][:4]
    half = total_mine.shape[1]
    gain_left, gain_right = gain_ref[:, :half], gain_ref[:, half:]
    d_left, d_right = total_mine[...].astype(F32), total_other[...].astype(F32)
    hat_left = normed_ref[:, :half].astype(F32) * (1.0 / gain_left)
    hat_right = normed_ref[:, half:].astype(F32) * (1.0 / gain_right)
    term = jnp.sum(d_left * hat_left, axis=0, keepdims=True)
    g_left, g_right = d_left * gain_left, d_right * gain_right
    inner = (
        jnp.sum(g_left * hat_left, axis=1, keepdims=True)
        + jnp.sum(g_right * hat_right, axis=1, keepdims=True)
    ) / (2 * half)
    scale = scale_ref[...]
    left = grad_mine[...].astype(F32) + scale * (g_left - hat_left * inner)
    right = grad_other[...].astype(F32) + scale * (g_right - hat_right * inner)
    if count == 5:
        refs[-1][...] = left
    left, right = left.astype(BF16), right.astype(BF16)
    mine_ref[...] = left
    adapter = (dot_nt(left, up_ref[:, :half]) + dot_nt(right, up_ref[:, half:])).astype(BF16)
    adapter_ref[...] = adapter
    mixed_ref[...] = (
        dot_nt(out_own[...], left) + dot_nt(out_got[...], right) + dot_nt(down_ref[...], adapter)
    ).astype(BF16)

    @pl.when(pl.program_id(0) == 0)
    def _():
        gain_sum[...] = term

    @pl.when(pl.program_id(0) > 0)
    def _():
        gain_sum[...] += term


def norm_back(
    index, place, totals, normed, scale, grads, gain, out_own, out_got, up, down, kept, with_state
):
    half_rows, half = totals[0].shape
    length = 2 * half_rows
    half_blocks = half_rows // BLOCK
    heads = out_own.shape[0]
    base = index * half_blocks
    whole = lambda values: pl.BlockSpec(values.shape, lambda i, s: (0, 0))
    near = pl.BlockSpec((BLOCK, half), lambda i, s: (i, 0))
    here = lambda columns: pl.BlockSpec((BLOCK, columns), lambda i, s: (base + i, 0))
    shapes = (
        jax.ShapeDtypeStruct((heads, length), BF16),
        jax.ShapeDtypeStruct((length, half), BF16),
        jax.ShapeDtypeStruct((length, LANES), BF16),
        jax.ShapeDtypeStruct((1, half), F32),
    )
    out_specs = [
        pl.BlockSpec((heads, BLOCK), lambda i, s: (0, global_block(base + i, s[1], half_blocks))),
        here(half),
        here(LANES),
        pl.BlockSpec((1, half), lambda i, s: (0, 0)),
    ]
    if with_state:
        shapes += (jax.ShapeDtypeStruct((half_rows, half), F32),)
        out_specs.append(near)
    return grid_call(
        functools.partial(norm_back_kernel, len(shapes)),
        "norm_back",
        (half_blocks,),
        shapes,
        [near, near, here(2 * half), here(1), near, near]
        + [whole(values) for values in (gain, out_own, out_got, up, down)]
        + [pl.BlockSpec(memory_space=pl.ANY)] * len(kept),
        out_specs,
        aliases={12 + i: i for i in range(len(kept))},
    )(place, *totals, normed, scale, *grads, gain, out_own, out_got, up, down, *kept)


def pair_sum_kernel(products, *refs):
    operands = refs[:-5]
    out_ref, send_buf, recv_buf, send_sem, recv_sem = refs[-5:]
    step = pl.program_id(0)
    tiles = send_buf.shape[0]
    col = lax.axis_index("col")

    def copy(tile):
        return pltpu.make_async_remote_copy(
            src_ref=send_buf.at[tile],
            dst_ref=recv_buf.at[tile],
            send_sem=send_sem.at[tile],
            recv_sem=recv_sem.at[tile],
            device_id={"col": 1 - col},
            device_id_type=MESH,
        )

    @pl.when(step == 0)
    def _():
        barrier = pltpu.get_barrier_semaphore()
        pl.semaphore_signal(barrier, inc=1, device_id={"col": 1 - col}, device_id_type=MESH)
        pl.semaphore_wait(barrier, 1)

    @pl.when(step < tiles)
    def _():
        send_buf[step] = products(operands, False).astype(BF16)
        copy(step).start()

    @pl.when(step >= tiles)
    def _():
        tile = step - tiles
        sums = products(operands, True)
        copy(tile).wait_recv()
        out_ref[...] = (sums + recv_buf[tile].astype(F32)).astype(BF16)

    @pl.when(step == 2 * tiles - 1)
    def _():
        for tile in range(tiles):
            copy(tile).wait_send()


def pair_sum(products, name, collective, rows, half, in_specs, operands):
    tile = min(SUM_TILE, half)
    tiles = half // tile
    return pl.pallas_call(
        functools.partial(pair_sum_kernel, products),
        grid=(2 * tiles,),
        out_shape=jax.ShapeDtypeStruct((rows, half), BF16),
        in_specs=in_specs,
        out_specs=pl.BlockSpec((rows, tile), lambda i: (0, jnp.maximum(i - tiles, 0))),
        scratch_shapes=[
            pltpu.VMEM((tiles, rows, tile), BF16),
            pltpu.VMEM((tiles, rows, tile), BF16),
            pltpu.SemaphoreType.DMA((tiles,)),
            pltpu.SemaphoreType.DMA((tiles,)),
        ],
        compiler_params=pltpu.CompilerParams(
            dimension_semantics=("arbitrary",),
            collective_id=collective,
            has_side_effects=True,
            vmem_limit_bytes=VMEM_LIMIT,
        ),
        cost_estimate=FREE,
        name=name,
    )(*operands)


def second_products(refs, own):
    d_gate, d_up, gate_own, gate_got, up_own, up_got = refs
    if own:
        return dot_nt(d_gate[...], gate_own[...]) + dot_nt(d_up[...], up_own[...])
    return dot_nt(d_gate[...], gate_got[...]) + dot_nt(d_up[...], up_got[...])


def second_grad(index, d_gate, d_up, gate_weight, gate_got, up_weight, up_got):
    half, hidden_cols = gate_got.shape
    rows = d_gate.shape[0] // 2
    tile = min(SUM_TILE, half)
    tiles = half // tile
    left = pl.BlockSpec((rows, hidden_cols), lambda i: (index, 0))
    own = pl.BlockSpec(
        (tile, hidden_cols), lambda i: (jnp.maximum(i - tiles, 0), lax.axis_index("col"))
    )
    got = pl.BlockSpec((tile, hidden_cols), lambda i: (jnp.minimum(i, tiles - 1), 0))
    return pair_sum(
        second_products,
        "second_grad",
        1 + index,
        rows,
        half,
        [left, left, own, got, own, got],
        (d_gate, d_up, gate_weight, gate_got, up_weight, up_got),
    )


def down_products(refs, own):
    hidden, down_own, down_got = refs
    return dot_nn(hidden[...], (down_own if own else down_got)[...])


def down_product(hidden, down_weight, down_got):
    rows, hidden_cols = hidden.shape
    half = down_got.shape[1]
    tile = min(SUM_TILE, half)
    tiles = half // tile
    return pair_sum(
        down_products,
        "down_product",
        3,
        rows,
        half,
        [
            pl.BlockSpec((rows, hidden_cols), lambda i: (0, 0)),
            pl.BlockSpec(
                (hidden_cols, tile), lambda i: (lax.axis_index("col"), jnp.maximum(i - tiles, 0))
            ),
            pl.BlockSpec((hidden_cols, tile), lambda i: (0, jnp.minimum(i, tiles - 1))),
        ],
        (hidden, down_weight, down_got),
    )


def finish_kernel(orders, small_count, joins, *refs):
    count = len(orders)
    far_ref, refs = refs[0], refs[1:]
    smalls, refs = refs[:small_count], refs[small_count:]
    grads, refs = refs[:count], refs[count:]
    far_out, refs = refs[0], refs[1:]
    totals, refs = refs[:small_count], refs[small_count:]
    joined, refs = refs[: len(joins)], refs[len(joins) :]
    outs, refs = refs[:count], refs[count:]
    send_sem, recv_sem = refs[:2]
    refs = refs[2:]
    place, col = lax.axis_index("dp"), lax.axis_index("col")
    bits = max(len(order) for order in orders)
    small_sums, refs = refs[: small_count * (bits - 1)], refs[small_count * (bits - 1) :]
    small_gots, buffers = refs[: small_count * bits], refs[small_count * bits :]

    barrier = pltpu.get_barrier_semaphore()
    partners = [{"col": 1 - col}]
    partners += [{"dp": place ^ (1 << k)} for k in range(bits)]
    partners.append({"row": 1 - lax.axis_index("row")})
    for partner in partners:
        pl.semaphore_signal(barrier, inc=1, device_id=partner, device_id_type=MESH)
    pl.semaphore_wait(barrier, len(partners))

    started = []

    def send(source, target, partner):
        copy = pltpu.make_async_remote_copy(
            src_ref=source,
            dst_ref=target,
            send_sem=send_sem.at[len(started)],
            recv_sem=recv_sem.at[len(started)],
            device_id=partner,
            device_id_type=MESH,
        )
        copy.start()
        started.append(copy)
        return copy

    far_copy = send(far_ref, far_out, partners[-1])
    current = list(grads)
    small_now = list(smalls)
    used = 0
    for step in range(bits):
        moving = []
        for n in range(small_count):
            got = small_gots[n * bits + step]
            bit = (step + n) % bits
            moving.append((send(small_now[n], got, partners[1 + bit]), got))
        halves = {}
        for n, order in enumerate(orders):
            if step < len(order):
                rows = current[n].shape[0] // 2
                got = buffers[used]
                used += 1
                copy = send(
                    current[n].at[pl.ds(rows, rows), :], got, partners[1 + order[step]]
                )
                halves[n] = (copy, got, rows)
        for n, (copy, got) in enumerate(moving):
            copy.wait_recv()
            target = totals[n] if step + 1 == bits else small_sums[n * (bits - 1) + step]
            target[...] = small_now[n][...] + got[...]
            small_now[n] = target
        if step + 1 == bits:
            joining = []
            for out, (source, first, size, columns, axis) in zip(joined, joins):
                total = totals[source]
                if axis == 0:
                    size = total.shape[0]
                    part, slot = total, out.at[pl.ds(col * size, size)]
                else:
                    part = total.at[pl.ds(first, size), pl.ds(*columns)]
                    slot = out.at[:, pl.ds(pl.multiple_of(col * columns[1], LANES), columns[1])]
                joining.append(send(part, slot, partners[0]))
                slot[...] = part[...]
        for n, (copy, got, rows) in halves.items():
            copy.wait_recv()
            sums = current[n][:rows].astype(F32) + got[...].astype(F32)
            if step + 1 == len(orders[n]):
                outs[n][...] = sums
            else:
                target = buffers[used]
                used += 1
                target[...] = sums.astype(BF16)
                current[n] = target
    for copy in joining + [far_copy]:
        copy.wait_recv()
    for copy in started:
        copy.wait_send()


def finish(far, smalls, joins, grads, orders):
    count = len(grads)
    bits = max(len(order) for order in orders)
    vmem = pl.BlockSpec(memory_space=pltpu.VMEM)
    copies = 1 + bits * len(smalls) + len(joins) + sum(len(order) for order in orders)
    scratch = [pltpu.SemaphoreType.DMA((copies,)), pltpu.SemaphoreType.DMA((copies,))]
    scratch += [pltpu.VMEM(s.shape, F32) for s in smalls for _ in range(bits - 1)]
    scratch += [pltpu.VMEM(s.shape, F32) for s in smalls for _ in range(bits)]
    for step in range(bits):
        for target in range(2):
            for grad, order in zip(grads, orders):
                if step + target < len(order):
                    rows = grad.shape[0] >> (step + 1)
                    scratch.append(pltpu.VMEM((rows, grad.shape[1]), BF16))
    joined = []
    for source, first, size, columns, axis in joins:
        shape = smalls[source].shape
        if axis == 0:
            joined.append(jax.ShapeDtypeStruct((2 * shape[0],) + shape[1:], F32))
        else:
            joined.append(jax.ShapeDtypeStruct((size, 2 * columns[1]), F32))
    outs = [
        jax.ShapeDtypeStruct((g.shape[0] >> len(order), g.shape[1]), F32)
        for g, order in zip(grads, orders)
    ]
    totals = [jax.ShapeDtypeStruct(s.shape, F32) for s in smalls]
    results = pl.pallas_call(
        functools.partial(finish_kernel, orders, len(smalls), joins),
        out_shape=(jax.ShapeDtypeStruct(far.shape, far.dtype), *totals, *joined, *outs),
        in_specs=[pl.BlockSpec(memory_space=pl.ANY)] + [vmem] * (len(smalls) + count),
        out_specs=(pl.BlockSpec(memory_space=pl.ANY),)
        + (vmem,) * (len(totals) + len(joined) + count),
        scratch_shapes=scratch,
        compiler_params=pltpu.CompilerParams(
            collective_id=4, has_side_effects=True, vmem_limit_bytes=VMEM_LIMIT
        ),
        cost_estimate=FREE,
        name="finish",
    )(far, *smalls, *grads)
    first, second = 1 + len(smalls), 1 + len(smalls) + len(joins)
    return results[0], results[1:first], results[first:second], results[second:]


def weight_grad_kernel(sets, chunks, pieces, turned, right_turned, place_ref, *refs):
    outs = refs[-1 - pieces * sets : -1]
    right_ref, left_ref = refs[-2 - pieces * sets], refs[-1]
    lefts = refs[: -2 - pieces * sets]
    length = left_ref.shape[1]
    rows = left_ref.shape[0] // sets
    count = rows // LANES

    @pl.when(pl.program_id(0) == 0)
    def _():
        for p in range(sets * count):
            lanes = slice(p * LANES, (p + 1) * LANES)
            if turned:
                left_ref[lanes, :] = lefts[p][...]
            else:
                size = length // chunks
                for i in range(chunks):
                    left_ref[lanes, i * size : (i + 1) * size] = jnp.transpose(
                        lefts[p * chunks + i][...]
                    )

    for which in range(sets):
        left = left_ref[which * rows : (which + 1) * rows, :]
        sums = (dot_nt if right_turned else dot_nn)(left, right_ref[...])
        size = rows // pieces
        for i in range(pieces):
            outs[pieces * which + i][...] = sums[i * size : (i + 1) * size].astype(BF16)


def weight_grad(places, sets, right, pieces=2, turned=False, right_turned=False, cut=(0, 1)):
    chunks = len(sets[0][0])
    length = sets[0][0][0].shape[1] if turned else sum(c.shape[0] for c in sets[0][0])
    count = (places.shape[0] - 2) // len(sets)
    columns = (right.shape[0] if right_turned else right.shape[1]) // cut[1]
    tile = next(size for size in (GRAD_TILE, 384, 256, 128) if columns % size == 0)
    skip = cut[0] * (columns // tile)
    in_specs, operands = [], []
    for n, (lefts, base) in enumerate(sets):
        for p in range(count):
            at = 2 + n * count + p
            for left in lefts:
                if turned:
                    spec = pl.BlockSpec((LANES, length), lambda j, s, at=at: (s[at], 0))
                else:
                    spec = pl.BlockSpec(
                        (left.shape[0], LANES), lambda j, s, at=at, base=base: (0, base + s[at])
                    )
                in_specs.append(spec)
                operands.append(left)
    if right_turned:
        in_specs.append(pl.BlockSpec((tile, length), lambda j, s: (skip + j, 0)))
    else:
        in_specs.append(pl.BlockSpec((length, tile), lambda j, s: (0, skip + j)))
    size = count * LANES // pieces
    out_spec = pl.BlockSpec((size, tile), lambda j, s: (0, j))
    return grid_call(
        functools.partial(weight_grad_kernel, len(sets), chunks, pieces, turned, right_turned),
        "weight_grad",
        (columns // tile,),
        (jax.ShapeDtypeStruct((size, columns), BF16),) * (pieces * len(sets)),
        in_specs,
        [out_spec] * (pieces * len(sets)),
        [pltpu.VMEM((len(sets) * count * LANES, length), BF16)],
    )(places, *operands, right)


def pair_grad_kernel(chunks, merged, *refs):
    send_buf, own_buf, left_ref, send_sem, recv_sem, local_sem = refs[-6:]
    outs = refs[-7:-6] if merged else refs[-10:-6]
    inputs = refs[: -7 if merged else -10]
    lefts, right_ref = inputs[:-1], inputs[-1]
    step = pl.program_id(0)
    tiles, rows, tile = send_buf.shape
    count = rows // LANES
    half = rows // 2
    col = lax.axis_index("col")

    def sent(source, target, n):
        return pltpu.make_async_remote_copy(
            src_ref=source,
            dst_ref=target,
            send_sem=send_sem.at[n],
            recv_sem=recv_sem.at[n],
            device_id={"col": 1 - col},
            device_id_type=MESH,
        )

    def columns(index, base):
        start = index * tile
        if not isinstance(start, int):
            start = pl.multiple_of(start, tile)
        return pl.ds(base + start, tile)

    def copies(index):
        if merged:
            (out,) = outs
            whole = tiles * tile
            return (
                [sent(send_buf.at[index], out.at[:, columns(index, whole)], index)],
                [
                    pltpu.make_async_copy(
                        own_buf.at[index], out.at[:, columns(index, 0)], local_sem.at[index]
                    )
                ],
            )
        got = outs[2:]
        return [
            sent(
                send_buf.at[index, pl.ds(n * half, half), :],
                got[n].at[:, columns(index, 0)],
                2 * index + n,
            )
            for n in range(2)
        ], []

    @pl.when(step == 0)
    def _():
        barrier = pltpu.get_barrier_semaphore()
        pl.semaphore_signal(barrier, inc=1, device_id={"col": 1 - col}, device_id_type=MESH)
        pl.semaphore_wait(barrier, 1)
        size = left_ref.shape[1] // chunks
        for p in range(2 * count):
            for i in range(chunks):
                left_ref[p * LANES : (p + 1) * LANES, i * size : (i + 1) * size] = jnp.transpose(
                    lefts[p * chunks + i][...]
                )

    send_buf[step] = dot_nn(left_ref[rows:, :], right_ref[...]).astype(BF16)
    away, near = copies(step)
    for copy in away:
        copy.start()
    own = dot_nn(left_ref[:rows, :], right_ref[...]).astype(BF16)
    if merged:
        own_buf[step] = own
        near[0].start()
    else:
        outs[0][...] = own[:half]
        outs[1][...] = own[half:]

    @pl.when(step == tiles - 1)
    def _():
        for index in range(tiles):
            away, near = copies(index)
            for copy in away + near:
                copy.wait()


def pair_grad(name, collective, lefts, others, right, order, other_order, merged):
    chunks = len(lefts[0])
    length = sum(values.shape[0] for values in lefts[0])
    columns = right.shape[1]
    tile = min(GRAD_TILE, columns)
    tiles = columns // tile
    count = len(order)
    rows = count * LANES
    in_specs, operands = [], []
    for (parts, base), which in ((lefts, order), (others, other_order)):
        for p in range(count):
            for values in parts:

                def at(j, base=base, entry=which[p]):
                    if isinstance(entry, tuple):
                        return (0, base + (lax.axis_index("dp") ^ entry[0]))
                    return (0, base + entry)

                in_specs.append(pl.BlockSpec((values.shape[0], LANES), at))
                operands.append(values)
    in_specs.append(pl.BlockSpec((length, tile), lambda j: (0, j)))
    anywhere = pl.BlockSpec(memory_space=pl.ANY)
    like = lambda *shape: jax.ShapeDtypeStruct(shape, BF16)
    if merged:
        out_shape, out_specs = (like(rows, 2 * columns),), (anywhere,)
    else:
        out_shape = (like(rows // 2, columns),) * 4
        near = pl.BlockSpec((rows // 2, tile), lambda j: (0, j))
        out_specs = (near, near, anywhere, anywhere)
    transfers = tiles if merged else 2 * tiles
    return pl.pallas_call(
        functools.partial(pair_grad_kernel, chunks, merged),
        grid=(tiles,),
        out_shape=out_shape,
        in_specs=in_specs,
        out_specs=out_specs,
        scratch_shapes=[
            pltpu.VMEM((tiles, rows, tile), BF16),
            pltpu.VMEM((tiles if merged else 1, rows, tile), BF16),
            pltpu.VMEM((2 * rows, length), BF16),
            pltpu.SemaphoreType.DMA((transfers,)),
            pltpu.SemaphoreType.DMA((transfers,)),
            pltpu.SemaphoreType.DMA((tiles,)),
        ],
        compiler_params=pltpu.CompilerParams(
            dimension_semantics=("arbitrary",),
            collective_id=collective,
            has_side_effects=True,
            vmem_limit_bytes=VMEM_LIMIT,
        ),
        cost_estimate=FREE,
        name=name,
    )(*operands, right)


def first_back_kernel(place_ref, *refs):
    parts, (proj_ref, up_ref, normed_ref) = refs[:6], refs[6:9]
    far_ref, own_ref, turned_ref, adapter_ref, gain_ref = refs[9:]
    step = pl.program_id(0)
    first = 0
    for source in parts:
        turned_ref[:, first : first + source.shape[0]] = jnp.transpose(source[...])
        first += source.shape[0]
    turned = turned_ref[...]
    adapter_ref[...] = dot_nt(up_ref[...], turned)
    sums = dot_nt(turned, proj_ref[...])
    term = jnp.sum(sums * normed_ref[...].astype(F32), axis=0, keepdims=True)

    @pl.when(step < pl.num_programs(0) // 2)
    def _():
        far_ref[...] = sums.astype(BF16)

    @pl.when(step >= pl.num_programs(0) // 2)
    def _():
        own_ref[...] = sums

    @pl.when(step == 0)
    def _():
        gain_ref[...] = term

    @pl.when(step > 0)
    def _():
        gain_ref[...] += term


def first_back(place, parts, proj_native, up_native, normed):
    length = parts[0].shape[1]
    half, columns = proj_native.shape
    blocks = length // BLOCK
    middle = blocks // 2
    at = lambda i: (i + middle) % blocks
    whole = lambda values: pl.BlockSpec(values.shape, lambda i, s: (0, 0))
    return grid_call(
        first_back_kernel,
        "first_back",
        (blocks,),
        (
            jax.ShapeDtypeStruct((length // 2, half), BF16),
            jax.ShapeDtypeStruct((length // 2, half), F32),
            jax.ShapeDtypeStruct((length, columns), BF16),
            jax.ShapeDtypeStruct((up_native.shape[0], length), F32),
            jax.ShapeDtypeStruct((1, half), F32),
        ),
        [pl.BlockSpec((values.shape[0], BLOCK), lambda i, s: (0, at(i))) for values in parts]
        + [whole(proj_native), whole(up_native)]
        + [pl.BlockSpec((BLOCK, half), lambda i, s: (at(i), 0))],
        [
            pl.BlockSpec((BLOCK, half), lambda i, s: (jnp.minimum(i, middle - 1), 0)),
            pl.BlockSpec((BLOCK, half), lambda i, s: (jnp.maximum(i - middle, 0), 0)),
            pl.BlockSpec((BLOCK, columns), lambda i, s: (at(i), 0)),
            pl.BlockSpec((up_native.shape[0], BLOCK), lambda i, s: (0, at(i))),
            whole(jnp.zeros((1, half))),
        ],
    )(place, *parts, proj_native, up_native, normed)


def after(value, *others):
    return lax.optimization_barrier((value,) + others)[0]


def swap(values, axis):
    return lax.ppermute(values, axis, [(0, 1), (1, 0)])


def part(values, index, count, axis):
    width = values.shape[axis] // count
    return lax.dynamic_slice_in_dim(values, index * width, width, axis)


def contract(left, right, left_dim, right_dim):
    return lax.dot_general(
        left, right, (((left_dim,), (right_dim,)), ((), ())), preferred_element_type=F32
    )


def exchange_order(bits, first):
    return [(first + k) % bits for k in range(bits)]


def relative_index(position, order):
    bits = len(order)
    return sum(((position >> (bits - 1 - k)) & 1) << order[k] for k in range(bits))


def relative_blocks(values, axis, device, order):
    count = 1 << len(order)
    return jnp.concatenate(
        [part(values, device ^ relative_index(p, order), count, axis) for p in range(count)],
        axis=axis,
    )


class Reduction:
    def __init__(self, keep, send, size, order):
        self.keep, self.size, self.order, self.step = keep, size, order, 0
        self.launch(send)

    def launch(self, send):
        bit = 1 << self.order[self.step]
        self.got = lax.ppermute(send, "dp", [(i, i ^ bit) for i in range(self.size)])

    def combine(self):
        got = self.got
        self.step += 1
        if self.step == len(self.order):
            self.keep = self.keep.astype(F32) + got.astype(F32)
            return self.keep
        half = self.keep.shape[0] // 2
        sums = (
            (self.keep[rows].astype(F32) + got[rows].astype(F32)).astype(BF16)
            for rows in (slice(0, half), slice(half, 2 * half))
        )
        self.keep, send = sums
        self.launch(send)
        return self.keep

    @property
    def done(self):
        return self.step == len(self.order)


def total_over(values, size, bits):
    for k in range(bits):
        values = values + lax.ppermute(values, "dp", [(i, i ^ (1 << k)) for i in range(size)])
    return values


def ordered(own, other, index, axis):
    return jnp.where(
        index == 0,
        jnp.concatenate([own, other], axis=axis),
        jnp.concatenate([other, own], axis=axis),
    )


def on_device(
    activations,
    grad_out,
    segments,
    first_gain,
    query_weight,
    key_weight,
    value_weight,
    query_down,
    query_up,
    key_down,
    key_up,
    value_down,
    value_up,
    query_map,
    key_map,
    output_weight,
    output_down,
    output_up,
    second_gain,
    gate_weight,
    up_weight,
    down_weight,
):
    size = lax.axis_size("dp")
    bits = size.bit_length() - 1
    device = lax.axis_index("dp")
    row = lax.axis_index("row")
    col = lax.axis_index("col")
    seq_rows = segments.shape[1]
    half_rows, feature_cols = activations.shape
    width = 2 * feature_cols
    blocks = seq_rows // BLOCK
    half_blocks = blocks // 2
    rank = query_down.shape[1]
    query_part = query_weight.shape[1] // 2
    key_part = key_weight.shape[1] // 2
    part_cols = query_part + 2 * key_part
    order = exchange_order(bits, 0)
    turned_order = exchange_order(bits, 1)
    mixed_order = [1, 0] + order[2:]

    def other_half(values, axis):
        return jnp.roll(values, values.shape[axis] // 2, axis)

    def sequence_order(values, axis):
        return jnp.where(row == 0, values, other_half(values, axis))

    def rows_of(index):
        return slice(index * BLOCK, (index + 1) * BLOCK)

    lane_blocks = feature_cols // LANES
    direct = lane_blocks == size

    def block_order(which, rows_of_pair=False):
        if not direct:
            return [jnp.int32(p) for p in range(lane_blocks)]
        blocks_of = [device ^ relative_index(p, which) for p in range(size)]
        if rows_of_pair:
            return [((b // (size // 2)) ^ col) * (size // 2) + b % (size // 2) for b in blocks_of]
        return blocks_of

    def places(*orders, rows_of_pair=False):
        entries = [col, row]
        for which in orders:
            entries += block_order(which, rows_of_pair)
        return jnp.stack([jnp.asarray(v, jnp.int32) for v in entries])

    place = places(order)

    def grads_of(sets, right, orders, right_turned=False, cut=(0, 1), pieces=2):
        if not direct:
            sets = [
                (
                    [
                        relative_blocks(
                            left[:, base * LANES : base * LANES + feature_cols], 1, device, which
                        )
                        for left in lefts
                    ],
                    0,
                )
                for (lefts, base), which in zip(sets, orders)
            ]
        outs = weight_grad(places(*orders), sets, right, pieces, False, right_turned, cut)
        return [outs[pieces * n : pieces * (n + 1)] for n in range(len(sets))]

    def ups(index):
        zeros_key = jnp.zeros((rank, key_part), BF16)
        zeros_query = jnp.zeros((rank, query_part), BF16)
        return jnp.concatenate(
            [
                jnp.concatenate([part(query_up, index, 2, 1), zeros_key, zeros_key], axis=1),
                jnp.concatenate([zeros_query, part(key_up, index, 2, 1), zeros_key], axis=1),
                jnp.concatenate([zeros_query, zeros_key, part(value_up, index, 2, 1)], axis=1),
                jnp.zeros((rank, part_cols), BF16),
            ],
            axis=0,
        )

    thin = jnp.concatenate(
        [jnp.transpose(v) for v in (query_down, key_down, value_down)] + [output_up], axis=0
    )
    gains = jnp.stack([first_gain, second_gain])
    inputs_far = swap(activations, "row")
    (
        inputs_other,
        grads_other,
        proj_got,
        gate_got,
        up_got,
        mlp_down_got,
        output_got,
        thin_got,
        gains_got,
        proj_own,
        proj_native,
        output_native,
    ) = exchange(
        activations,
        grad_out,
        (query_weight, key_weight, value_weight),
        gate_weight,
        up_weight,
        down_weight,
        output_weight,
        (thin, gains),
    )
    grads_far = swap(after(grad_out, inputs_far), "row")
    up_own = ups(col)
    up_native = jnp.concatenate([up_own, ups(1 - col)], axis=1)
    second_gain_full = jnp.concatenate([gains[1:], gains_got[1:]], axis=1)
    output_up_full = jnp.concatenate([output_up, thin_got[3 * rank :]], axis=1)
    output_up_full = jnp.pad(output_up_full, ((0, LANES - rank), (0, 0)))
    output_rows_own = part(output_weight, col, 2, 0)
    output_down_own = part(output_down, col, 2, 0)
    output_down_native = jnp.concatenate(
        [output_down_own, part(output_down, 1 - col, 2, 0)], axis=0
    )
    output_down_padded = jnp.pad(output_down_own, ((0, 0), (0, LANES - rank)))
    query_map_own = part(query_map, col, 2, 0)
    key_map_own = part(key_map, col, 2, 0)

    documents = segments[0]
    starts = jnp.sum((documents[None, :] < documents[:, None]).astype(jnp.int32), axis=1)
    marks = jnp.concatenate(
        [
            jnp.full((1,), seq_rows, jnp.int32),
            starts[BLOCK - WINDOW - 1 :: BLOCK],
            jnp.asarray(row, jnp.int32)[None],
        ]
    )
    starts = starts.reshape(1, 1, seq_rows)

    def project(index, mine, other, kept):
        return project_block(
            index,
            place,
            mine,
            other,
            (gains, gains_got),
            (proj_own, proj_got),
            (thin, thin_got),
            up_own,
            query_part,
            kept,
        )

    kept = project(0, activations, inputs_other, ())
    inputs_far = after(inputs_far, kept[0])
    inputs_far_other = swap(inputs_far, "col")
    kept = project(half_blocks, inputs_far, inputs_far_other, kept)
    normed_first, queries, keys_values, adapters, first_scale = kept
    keys_values = jnp.pad(keys_values, ((0, 0), (WINDOW, WINDOW)))
    mixed, inverse = attention_forward(
        marks, starts, queries, keys_values, query_map_own, key_map_own
    )

    d_hidden = hidden_grad(
        0, place, (after(grad_out, mixed), grads_other), down_weight, mlp_down_got, ()
    )
    mixed, grads_far, _ = lax.optimization_barrier((mixed, grads_far, d_hidden))
    mixed_pair = jnp.concatenate([mixed, swap(mixed, "col")], axis=0)
    adapter_sum = contract(mixed_pair, output_down_native, 0, 0)
    adapter_far = swap(other_half(adapter_sum, 0), "row")
    grads_far_other = swap(after(grads_far, mixed), "col")
    send_order = [(b + half_blocks) % blocks for b in range(blocks)]
    attended, attended_far = [None] * blocks, [None] * blocks
    pair = after(mixed_pair, grads_far)
    for b in send_order:
        attended[b] = contract(pair[:, rows_of(b)], output_native, 0, 0).astype(BF16)
        attended_far[send_order[b]] = swap(after(attended[b], adapter_far), "row")
        pair = after(pair, attended[b])
    out_adapter = (adapter_sum + adapter_far).astype(BF16)
    adapter_padded = jnp.pad(out_adapter, ((0, 0), (0, LANES - rank)))
    attended_other = [swap(attended[0], "col")] + [None] * (blocks - 1)
    d_hidden = hidden_grad(
        1,
        place,
        (after(grads_far, *attended, adapter_padded), grads_far_other),
        down_weight,
        mlp_down_got,
        (d_hidden,),
    )

    clock = (d_hidden,)
    kept, state = (), None
    for b in range(blocks):
        far = after(attended_far[b], *clock)
        far_other = swap(far, "col")
        if b + 1 < blocks:
            attended_other[b + 1] = swap(after(attended[b + 1], far), "col")
        inputs = (
            (activations, inputs_other)
            if b < half_blocks
            else (inputs_far, inputs_far_other)
        )
        outs = mlp_block(
            b,
            place,
            inputs,
            b % half_blocks,
            (attended[b], attended_other[b], far, far_other),
            adapter_padded,
            output_up_full,
            second_gain_full,
            gate_weight,
            gate_got,
            up_weight,
            up_got,
            d_hidden,
            kept,
            state,
            b < half_blocks,
        )
        kept = outs[:5]
        state = outs[5] if b < half_blocks else state
        clock = (kept[0],)
    hidden, d_gate, d_up, second_normed, second_scale = kept

    sums = {}

    def reduction(name, pair, which):
        sums[name] = Reduction(*pair, size, which)

    def settle(clock, *names):
        for name in names:
            sums[name].got = after(sums[name].got, *clock)
            clock = (sums[name].combine(),)
        return clock

    def arrived(values, *names):
        tied = lax.optimization_barrier((values,) + tuple(sums[name].got for name in names))
        for name, got in zip(names, tied[1:]):
            sums[name].got = got
        return tied[0]

    def scattered(values):
        return lax.psum_scatter(values, "dp", scatter_dimension=0, tiled=True).astype(F32)

    in_order = list(range(lane_blocks))

    def relative(which):
        return [(relative_index(p, which),) for p in range(size)] if direct else in_order

    def arranged(parts, which):
        if direct:
            return parts
        return [relative_blocks(values, 1, device, which) for values in parts]

    (gate_pair,) = pair_grad(
        "gate_grad",
        5,
        ([second_normed], 0),
        ([second_normed], lane_blocks),
        d_gate,
        in_order,
        in_order,
        True,
    )
    grad_gate_pair = scattered(gate_pair)
    down_outs = pair_grad(
        "down_grad",
        6,
        (arranged([grad_out, grads_far], order), 0),
        (arranged([grads_other, grads_far_other], turned_order), 0),
        after(hidden, gate_pair),
        relative(order),
        relative(turned_order),
        False,
    )
    own_down = down_outs[:2]
    reduction("down_own", own_down, order)
    reduction("down_got", down_outs[2:], turned_order)
    chip_far = second_grad(
        1, after(d_gate, own_down[0]), d_up, gate_weight, gate_got, up_weight, up_got
    )
    far_got_own = swap(chip_far, "row")
    chip_own = second_grad(
        0, after(d_gate, chip_far), d_up, gate_weight, gate_got, up_weight, up_got
    )
    far_got_far = swap(chip_own, "row")
    (up_pair,) = pair_grad(
        "up_grad",
        7,
        ([second_normed], 0),
        ([second_normed], lane_blocks),
        after(d_up, chip_own),
        in_order,
        in_order,
        True,
    )
    y_chip = down_product(after(hidden, up_pair), down_weight, mlp_down_got)
    clock = settle((y_chip,), "down_own", "down_got")

    totals = []
    for chip, got in ((chip_own, far_got_own), (chip_far, far_got_far)):
        total = (chip.astype(F32) + after(got, *clock).astype(F32)).astype(BF16)
        totals.append(total)
        clock = (total,)
    totals = [(total, swap(after(total, *clock), "col")) for total in totals]

    def back(index, grads, kept):
        return norm_back(
            index,
            place,
            totals[index],
            second_normed,
            second_scale,
            grads,
            second_gain_full,
            output_rows_own,
            output_got,
            output_up_full,
            output_down_padded,
            kept,
            index == 0,
        )

    outs = back(0, (grad_out, grads_other), ())
    kept, gain_sum, grad_state = outs[:3], outs[3], outs[4]
    grad_up_pair = scattered(after(up_pair, kept[0]))
    outs = back(1, (grads_far, grads_far_other), kept)
    kept = outs[:3]
    d_mixed, d_mine, d_out_padded = kept
    grad_second_gain = gain_sum + outs[3]
    d_out_adapter = d_out_padded[:, :rank]
    y_far = swap(after(y_chip, kept[0])[half_rows:], "row")
    grad_output_up = contract(out_adapter, d_mine, 0, 0)
    grad_output_down = contract(d_out_adapter, mixed, 0, 1)
    lefts = mixed_pair
    if not direct:
        lefts = relative_blocks(ordered(mixed, mixed_pair[query_part:], col, 0), 0, device, order)
    output_pair = weight_grad(
        places(order, rows_of_pair=True),
        [([lefts], 0)],
        after(d_mine, grad_output_up, grad_output_down),
        2,
        True,
    )
    reduction("output", output_pair, order)
    clock = (output_pair[0],)

    d_queries, d_keys, d_values, grad_query_map, grad_key_map = attention_backward(
        marks,
        starts,
        queries,
        keys_values,
        query_map_own,
        key_map_own,
        after(d_mixed, *clock),
        mixed,
        inverse,
    )

    d_queries = arrived(d_queries, "output", "down_own", "down_got")
    d_keys, d_values, _ = lax.optimization_barrier((d_keys, d_values, d_queries))
    d_parts = (d_queries, d_keys, d_values)
    d_parts += tuple(swap(values, "col") for values in d_parts)
    clock = tuple(sums[name].combine() for name in ("output", "down_own", "down_got"))
    d_first_far, d_first, d_turned, adapter_sum, gain_term = first_back(
        place, (after(d_queries, y_far, *clock),) + d_parts[1:], proj_native, up_native, normed_first
    )
    adapter_far = swap(other_half(adapter_sum, 1), "row")
    gain_far = swap(gain_term, "row")
    (proj_a,) = grads_of([([normed_first], 0)], d_turned, (order,), False, (0, 2), 1)
    (proj_b,) = grads_of(
        [([normed_first], 0)], after(d_turned, proj_a[0]), (mixed_order,), False, (1, 2), 1
    )
    adapter_far, gain_far, _ = lax.optimization_barrier((adapter_far, gain_far, proj_b[0]))
    d_adapter = (adapter_sum + adapter_far).astype(BF16)
    grad_down = contract(d_adapter, normed_first[:, :feature_cols], 1, 0)[: 3 * rank]
    grad_up = contract(adapters, d_turned[:, :part_cols], 0, 0)
    grad_up = jnp.concatenate(
        [
            grad_up[n * rank : (n + 1) * rank, first : first + count]
            for n, (first, count) in enumerate(
                ((0, query_part), (query_part, key_part), (query_part + key_part, key_part))
            )
        ],
        axis=1,
    )
    down_term = jnp.sum(thin[: 3 * rank].astype(F32) * grad_down, axis=0, keepdims=True)
    grad_first_gain = (gain_term + gain_far + down_term) / first_gain[None]
    result = (state + y_chip[:half_rows].astype(F32) + y_far.astype(F32)).astype(BF16)

    def sides(pair):
        half = pair.shape[1] // 2
        return ordered(pair[:, :half], pair[:, half:], col, 1)

    grad_gate = sides(grad_gate_pair)
    clock = settle((grad_up, result, grad_gate), "output", "down_own", "down_got")
    d_first = d_first + contract(d_adapter[:, :half_rows], thin, 0, 0)
    d_first_far, totals, joined, reduced = finish(
        after(d_first_far, *clock),
        (
            after(grad_first_gain, d_first),
            grad_second_gain,
            grad_output_up,
            grad_down,
            grad_output_down,
            grad_up,
            grad_query_map,
            grad_key_map,
        ),
        (
            (5, 0, rank, (0, query_part), 1),
            (5, 0, rank, (query_part, key_part), 1),
            (5, 0, rank, (query_part + key_part, key_part), 1),
            (6, 0, 0, (), 0),
            (7, 0, 0, (), 0),
            (4, 0, rank, (0, query_part), 1),
        ),
        (proj_a[0], proj_b[0]),
        (order, mixed_order),
    )
    d_first = d_first + d_first_far.astype(F32)
    first_scale = first_scale[:half_rows]
    hat_own = activations.astype(F32) * first_scale
    grad_hat = d_first * first_gain
    inner = jnp.sum(grad_hat * hat_own, axis=1)
    inner = ((inner + swap(inner, "col")) / width)[:, None]
    grad_activations = grad_state + first_scale * (grad_hat - hat_own * inner)
    grad_proj_a, grad_proj_b = reduced
    clock = (totals[0],)
    while any(not item.done for item in sums.values()):
        clock = settle(clock, *(name for name, item in sums.items() if not item.done))
    down_total = jnp.transpose(totals[3])

    def unpacked_maps(maps):
        half = maps.shape[2] // 2
        return jnp.concatenate([maps[:, :, :half], maps[:, :, half:]], axis=1)

    proj_grads = [
        ordered(
            grad_proj_a[:, first : first + count],
            grad_proj_b[:, first : first + count],
            col,
            1,
        )
        for first, count in (
            (0, query_part),
            (query_part, key_part),
            (query_part + key_part, key_part),
        )
    ]

    grad_up_weight = sides(grad_up_pair)
    grad_down_weight = ordered(sums["down_own"].keep, sums["down_got"].keep, col, 1)
    return (
        result,
        grad_activations,
        totals[0][0],
        proj_grads[0],
        proj_grads[1],
        proj_grads[2],
        down_total[:, :rank],
        joined[0],
        down_total[:, rank : 2 * rank],
        joined[1],
        down_total[:, 2 * rank : 3 * rank],
        joined[2],
        unpacked_maps(joined[3]),
        unpacked_maps(joined[4]),
        sums["output"].keep,
        jnp.transpose(joined[5]),
        totals[2],
        totals[1][0],
        grad_gate,
        grad_up_weight,
        jnp.transpose(grad_down_weight),
    )


def solution(mesh):
    placed = (
        P(("dp", "row"), "col"),
        P(("dp", "row"), "col"),
        P("dp", None),
        P("col"),
        P("col", "row"),
        P("col", "row"),
        P("col", "row"),
        P("col", None),
        P(None, "row"),
        P("col", None),
        P(None, "row"),
        P("col", None),
        P(None, "row"),
        P("row", None, None),
        P("row", None, None),
        P("row", "col"),
        P("row", None),
        P(None, "col"),
        P("col"),
        P("col", "row"),
        P("col", "row"),
        P("row", "col"),
    )
    return jax.shard_map(
        on_device,
        mesh=mesh,
        in_specs=placed,
        out_specs=(
            P(("dp", "row"), "col"),
            P(("dp", "row"), "col"),
            P("col"),
            P(("col", "dp"), "row"),
            P(("col", "dp"), "row"),
            P(("col", "dp"), "row"),
            P("col", None),
            P(None, "row"),
            P("col", None),
            P(None, "row"),
            P("col", None),
            P(None, "row"),
            P("row", None, None),
            P("row", None, None),
            P(("row", "dp"), "col"),
            P("row", None),
            P(None, "col"),
            P("col"),
            P(("col", "dp"), "row"),
            P(("col", "dp"), "row"),
            P("row", ("col", "dp")),
        ),
        check_vma=False,
    )
```

```python
import functools
import jax
import jax.numpy as jnp
from jax import lax
from jax.experimental import pallas as pl
from jax.experimental.pallas import tpu as pltpu
from jax.sharding import PartitionSpec as P

HEAD_DIM = 64
WINDOW = 64
BLOCK = 512
SUB = 128
SCALE = 0.125
NSUB = BLOCK // SUB
LANES = 128
MLP_TILE = 512
SUM_TILE = 256
GRAD_TILE = 512
VMEM_LIMIT = 56 * 1024 * 1024
norm_eps = 1e-05
F32 = jnp.float32
BF16 = jnp.bfloat16


def dot_nn(left, right):
    return lax.dot_general(left, right, (((1,), (0,)), ((), ())), preferred_element_type=F32)


def dot_nt(left, right):
    return lax.dot_general(left, right, (((1,), (1,)), ((), ())), preferred_element_type=F32)


def softmax_halves(before):
    def soft(values):
        powers = jnp.exp(values - jnp.max(values, axis=0, keepdims=True))
        return powers * (1.0 / jnp.sum(powers, axis=0, keepdims=True))

    return jnp.concatenate([soft(before[:HEAD_DIM]), soft(before[HEAD_DIM:])], axis=0)


def halves_backward(probs, grads):
    def half(p, g):
        return p * (g - jnp.sum(p * g, axis=0, keepdims=True))

    return half(probs[:HEAD_DIM], grads[:HEAD_DIM]) - half(probs[HEAD_DIM:], grads[HEAD_DIM:])


def side_by_side(parts, sub):
    return jnp.concatenate([part[:, sub * SUB : (sub + 1) * SUB] for part in parts], axis=1)


def key_side(kt_ref, vt_ref, kmap_ref, kft_ref, kfr_ref, kr_ref, vr_ref):
    features = softmax_halves(dot_nn(kmap_ref[0], kt_ref[...])).astype(BF16)
    kft_ref[...] = features
    kfr_ref[...] = jnp.transpose(features)
    kr_ref[...] = jnp.transpose(kt_ref[...])
    if vr_ref is not None:
        vr_ref[...] = jnp.transpose(vt_ref[...])


def tile_rows(start_ref, base, sub, ratio):
    low_one = start_ref[0, :, sub * SUB : (sub + 1) * SUB] + (WINDOW - base)
    low = jnp.concatenate([low_one] * ratio, axis=1)
    width = ratio * SUB
    place = sub * SUB + (lax.broadcasted_iota(jnp.int32, (1, width), 1) & (SUB - 1))
    same = jnp.where(low <= -1, 1.0, 0.0)
    return low, place, same


def tile_weights(kfr_ref, kr_ref, base, sub, low, place, q_sub, qf_sub):
    width = q_sub.shape[1]
    first = sub * SUB
    lin_keys = first + SUB
    win_keys = SUB + WINDOW
    link = dot_nn(kfr_ref[pl.ds(base, lin_keys), :], qf_sub)
    score = dot_nn(kr_ref[pl.ds(base + first, win_keys), :], q_sub) * SCALE
    lin_at = lax.broadcasted_iota(jnp.int32, (lin_keys, width), 0)
    win_at = lax.broadcasted_iota(jnp.int32, (win_keys, width), 0) + first
    lin_mask = (lin_at >= low) & (lin_at <= place)
    win_mask = (win_at >= jnp.maximum(low, place + 1)) & (win_at <= place + WINDOW)
    lin = jnp.where(lin_mask, link, 0.0)
    win = jnp.where(win_mask, jnp.exp(score), 0.0)
    return lin, win, lin_mask, win_mask


def member_lanes(base, mark):
    at = lax.broadcasted_iota(jnp.int32, (1, BLOCK), 1) + (base - WINDOW)
    return at >= mark


def forward_kernel(
    mark_ref, start_ref, qt_ref, kt_ref, vt_ref, qmap_ref, kmap_ref, mix_ref, inv_ref,
    kft_ref, kfr_ref, kr_ref, state_ref, norm_ref,
):
    b = pl.program_id(1)
    ratio = qmap_ref.shape[0]
    base = pl.multiple_of(b * BLOCK, BLOCK)

    @pl.when(b == 0)
    def _():
        key_side(kt_ref, vt_ref, kmap_ref, kft_ref, kfr_ref, kr_ref, None)
        state_ref[...] = jnp.zeros_like(state_ref)
        norm_ref[...] = jnp.zeros_like(norm_ref)

    queries = [qt_ref[h * HEAD_DIM : (h + 1) * HEAD_DIM, :] for h in range(ratio)]
    features = [softmax_halves(dot_nn(qmap_ref[h], queries[h])).astype(BF16) for h in range(ratio)]
    state_low = state_ref[...].astype(BF16)
    norm = norm_ref[...]
    for sub in range(NSUB):
        first = sub * SUB
        q_sub = side_by_side(queries, sub)
        qf_sub = side_by_side(features, sub)
        low, place, same = tile_rows(start_ref, base, sub, ratio)
        lin, win, _, _ = tile_weights(kfr_ref, kr_ref, base, sub, low, place, q_sub, qf_sub)
        carried = dot_nn(state_low, qf_sub)
        normal = jnp.sum(qf_sub.astype(F32) * norm, axis=0, keepdims=True)
        total = (
            jnp.sum(lin, axis=0, keepdims=True) + jnp.sum(win, axis=0, keepdims=True) + same * normal
        )
        inverse = 1.0 / total
        mixed = dot_nn(vt_ref[:, pl.ds(base, first + SUB)], lin.astype(BF16))
        mixed += dot_nn(vt_ref[:, pl.ds(base + first, SUB + WINDOW)], win.astype(BF16))
        mixed = ((mixed + same * carried) * inverse).astype(BF16)
        for h in range(ratio):
            lanes = slice(h * SUB, (h + 1) * SUB)
            mix_ref[h * HEAD_DIM : (h + 1) * HEAD_DIM, first : first + SUB] = mixed[:, lanes]
            inv_ref[0, h : h + 1, first : first + SUB] = inverse[:, lanes]

    mark = mark_ref[b + 1]
    keep = jnp.where((mark <= b * BLOCK - WINDOW - 1), 1.0, 0.0)
    tile = kft_ref[:, pl.ds(base, BLOCK)]
    member = jnp.where(member_lanes(base, mark), tile, jnp.zeros_like(tile))
    state_ref[...] = keep * state_ref[...] + dot_nt(vt_ref[:, pl.ds(base, BLOCK)], member)
    norm_ref[...] = keep * norm + jnp.sum(member.astype(F32), axis=1, keepdims=True)


def packed_map(grad):
    half = grad.shape[0] // 2
    return jnp.concatenate([grad[:half], grad[half:]], axis=1)


def backward_kernel(
    mark_ref, start_ref, qt_ref, kt_ref, vt_ref, qmap_ref, kmap_ref, dmt_ref, mix_ref, inv_ref,
    qback_ref, kback_ref,
    dqt_ref, dkt_ref, dvt_ref, gqm_ref, gkm_ref,
    kft_ref, kfr_ref, kr_ref, vr_ref, states_ref, statet_ref, norms_ref,
    dk_acc, dkf_acc, dv_acc, dst_ref, dstt_ref, dnorm_ref,
):
    step = pl.program_id(1)
    blocks = pl.num_programs(1)
    count = states_ref.shape[0]
    b = blocks - 1 - step
    ratio = qmap_ref.shape[0]
    base = pl.multiple_of(b * BLOCK, BLOCK)

    @pl.when(step == 0)
    def _():
        key_side(kt_ref, vt_ref, kmap_ref, kft_ref, kfr_ref, kr_ref, vr_ref)
        state = jnp.zeros(statet_ref.shape[1:], F32)
        norm = jnp.zeros(norms_ref.shape[1:], F32)
        statet = jnp.zeros(states_ref.shape[1:], F32)
        for i in range(count):
            statet_ref[i] = state.astype(BF16)
            states_ref[i] = statet.astype(BF16)
            norms_ref[i] = norm
            if i + 1 < count:
                mark = mark_ref[i + 1]
                keep = jnp.where((mark <= i * BLOCK - WINDOW - 1), 1.0, 0.0)
                tile = kft_ref[:, i * BLOCK : (i + 1) * BLOCK]
                member = jnp.where(member_lanes(i * BLOCK, mark), tile, jnp.zeros_like(tile))
                values = vt_ref[:, i * BLOCK : (i + 1) * BLOCK]
                state = keep * state + dot_nt(values, member)
                statet = keep * statet + dot_nt(member, values)
                norm = keep * norm + jnp.sum(member.astype(F32), axis=1, keepdims=True)
        dk_acc[...] = jnp.zeros_like(dk_acc)
        dkf_acc[...] = jnp.zeros_like(dkf_acc)
        dv_acc[...] = jnp.zeros_like(dv_acc)
        dst_ref[...] = jnp.zeros_like(dst_ref)
        dstt_ref[...] = jnp.zeros_like(dstt_ref)
        dnorm_ref[...] = jnp.zeros_like(dnorm_ref)
        gqm_ref[...] = jnp.zeros_like(gqm_ref)

    mark = mark_ref[b + 1]
    keep = jnp.where((mark <= b * BLOCK - WINDOW - 1), 1.0, 0.0)
    tile_lanes = pl.ds(base, BLOCK)
    member = member_lanes(base, mark)
    dst_low = dst_ref[...].astype(BF16)
    dstt_low = dstt_ref[...].astype(BF16)
    dkf_acc[:, tile_lanes] += jnp.where(
        member, dot_nn(dst_low, vt_ref[:, tile_lanes]) + dnorm_ref[...], 0.0
    )
    dv_acc[:, tile_lanes] += jnp.where(member, dot_nn(dstt_low, kft_ref[:, tile_lanes]), 0.0)

    queries = [qt_ref[h * HEAD_DIM : (h + 1) * HEAD_DIM, :] for h in range(ratio)]
    gradients = [dmt_ref[h * HEAD_DIM : (h + 1) * HEAD_DIM, :] for h in range(ratio)]
    mixes = [mix_ref[h * HEAD_DIM : (h + 1) * HEAD_DIM, :] for h in range(ratio)]
    inverses = [inv_ref[0, h : h + 1, :] for h in range(ratio)]
    probabilities = [softmax_halves(dot_nn(qmap_ref[h], queries[h])) for h in range(ratio)]
    features = [p.astype(BF16) for p in probabilities]
    norm = norms_ref[b]
    state_low = states_ref[b]
    dnorm = jnp.zeros((2 * HEAD_DIM, SUB), F32)
    dst = keep * dst_ref[...]
    dstt = keep * dstt_ref[...]
    dq_parts, dpre_parts = [], []
    for sub in range(NSUB):
        first = sub * SUB
        lin_lanes = pl.ds(base, first + SUB)
        win_lanes = pl.ds(base + first, SUB + WINDOW)
        q_sub = side_by_side(queries, sub)
        qf_sub = side_by_side(features, sub)
        dm_sub = side_by_side(gradients, sub)
        inverse = side_by_side(inverses, sub)
        dm_float = dm_sub.astype(F32)
        low, place, same = tile_rows(start_ref, base, sub, ratio)
        lin, win, lin_mask, win_mask = tile_weights(
            kfr_ref, kr_ref, base, sub, low, place, q_sub, qf_sub
        )
        delta = jnp.sum(dm_float * side_by_side(mixes, sub).astype(F32), axis=0, keepdims=True)
        dv_acc[:, lin_lanes] += dot_nt(dm_sub, (lin * inverse).astype(BF16))
        dv_acc[:, win_lanes] += dot_nt(dm_sub, (win * inverse).astype(BF16))
        dlin = (dot_nn(vr_ref[lin_lanes, :], dm_sub) - delta) * inverse
        dwin = (dot_nn(vr_ref[win_lanes, :], dm_sub) - delta) * inverse
        dlink = jnp.where(lin_mask, dlin, 0.0).astype(BF16)
        dscore = (win * dwin).astype(BF16)
        dcarried = (dm_float * (same * inverse)).astype(BF16)
        dtotal = -delta * (same * inverse)
        dk_acc[:, win_lanes] += dot_nt(q_sub, dscore)
        dkf_acc[:, lin_lanes] += dot_nt(qf_sub, dlink)
        dq_parts.append(dot_nn(kt_ref[:, win_lanes], dscore) * SCALE)
        dqf = dot_nn(kft_ref[:, lin_lanes], dlink) + dot_nn(state_low, dcarried) + norm * dtotal
        dst = dst + dot_nt(qf_sub, dcarried)
        dstt = dstt + dot_nt(dcarried, qf_sub)
        weighted = qf_sub.astype(F32) * dtotal
        for h in range(ratio):
            dnorm = dnorm + weighted[:, h * SUB : (h + 1) * SUB]
        dpre_parts.append(halves_backward(side_by_side(probabilities, sub), dqf).astype(BF16))
    dst_ref[...] = dst.astype(BF16).astype(F32)
    dstt_ref[...] = dstt.astype(BF16).astype(F32)
    dnorm_ref[...] = jnp.sum(dnorm, axis=1, keepdims=True) + keep * dnorm_ref[...]
    for h in range(ratio):
        lanes = slice(h * SUB, (h + 1) * SUB)
        dpre = jnp.concatenate([part[:, lanes] for part in dpre_parts], axis=1)
        dq = jnp.concatenate([part[:, lanes] for part in dq_parts], axis=1)
        dq = dq + dot_nn(qback_ref[h], dpre)
        dqt_ref[h * HEAD_DIM : (h + 1) * HEAD_DIM, :] = dq.astype(BF16)
        gqm_ref[h] += packed_map(dot_nt(queries[h], dpre))

    @pl.when(step == blocks - 1)
    def _():
        key_probs = softmax_halves(dot_nn(kmap_ref[0], kt_ref[...]))
        dpre = halves_backward(key_probs, dkf_acc[...]).astype(BF16)
        dk = (dk_acc[...] * SCALE + dot_nn(kback_ref[0], dpre)).astype(BF16)
        dv = dv_acc[...].astype(BF16)
        half = dkt_ref.shape[1] // 2
        flip = mark_ref[count + 1]
        for i in range(2):
            lanes = pl.ds(pl.multiple_of((i ^ flip) * half, half), half)
            dkt_ref[:, lanes] = dk[:, WINDOW + i * half : WINDOW + (i + 1) * half]
            dvt_ref[:, lanes] = dv[:, WINDOW + i * half : WINDOW + (i + 1) * half]
        gkm_ref[0] = packed_map(dot_nt(kt_ref[...], dpre))


def signed_maps(maps):
    turned = jnp.swapaxes(maps, 1, 2)
    return jnp.concatenate([turned, -turned], axis=1)


def local_block(block, marks, blocks):
    half = blocks // 2
    return ((block // half) ^ marks[blocks + 1]) * half + block % half


def attention_specs(groups, ratio, padded, block_of):
    rows = ratio * HEAD_DIM
    return [
        pl.BlockSpec((1, 1, BLOCK), lambda g, i, *_: (0, 0, block_of(i))),
        pl.BlockSpec((rows, BLOCK), lambda g, i, *_: (g, block_of(i))),
        pl.BlockSpec((HEAD_DIM, padded), lambda g, i, *_: (g, 0)),
        pl.BlockSpec((HEAD_DIM, padded), lambda g, i, *_: (groups + g, 0)),
        pl.BlockSpec((ratio, 2 * HEAD_DIM, HEAD_DIM), lambda g, i, *_: (g, 0, 0)),
        pl.BlockSpec((1, 2 * HEAD_DIM, HEAD_DIM), lambda g, i, *_: (g, 0, 0)),
    ]


def attention_forward(marks, starts, qt, kvt, qmap, kmap):
    length = qt.shape[1]
    padded = kvt.shape[1]
    groups = kmap.shape[0]
    ratio = qmap.shape[0] // groups
    rows = ratio * HEAD_DIM
    blocks = length // BLOCK
    return pl.pallas_call(
        forward_kernel,
        out_shape=(
            jax.ShapeDtypeStruct(qt.shape, BF16),
            jax.ShapeDtypeStruct((groups, ratio, length), F32),
        ),
        grid_spec=pltpu.PrefetchScalarGridSpec(
            num_scalar_prefetch=1,
            grid=(groups, blocks),
            in_specs=attention_specs(groups, ratio, padded, lambda i: i),
            out_specs=[
                pl.BlockSpec((rows, BLOCK), lambda g, i, s: (g, local_block(i, s, blocks))),
                pl.BlockSpec((1, ratio, BLOCK), lambda g, i, *_: (g, 0, i)),
            ],
            scratch_shapes=[
                pltpu.VMEM((2 * HEAD_DIM, padded), BF16),
                pltpu.VMEM((padded, 2 * HEAD_DIM), BF16),
                pltpu.VMEM((padded, HEAD_DIM), BF16),
                pltpu.VMEM((HEAD_DIM, 2 * HEAD_DIM), F32),
                pltpu.VMEM((2 * HEAD_DIM, 1), F32),
            ],
        ),
        compiler_params=pltpu.CompilerParams(
            dimension_semantics=("arbitrary", "arbitrary"), vmem_limit_bytes=48 * 1024 * 1024
        ),
        cost_estimate=pl.CostEstimate(flops=1000, bytes_accessed=1000, transcendentals=0),
        name="attention_forward",
    )(marks, starts, qt, kvt, kvt, signed_maps(qmap), signed_maps(kmap))


def attention_backward(marks, starts, qt, kvt, qmap, kmap, dmt, mixt, inverse):
    length = qt.shape[1]
    padded = kvt.shape[1]
    groups = kmap.shape[0]
    ratio = qmap.shape[0] // groups
    rows = ratio * HEAD_DIM
    blocks = length // BLOCK
    back = lambda i: blocks - 1 - i
    query_spec = pl.BlockSpec((rows, BLOCK), lambda g, i, *_: (g, back(i)))
    local_spec = pl.BlockSpec((rows, BLOCK), lambda g, i, s: (g, local_block(back(i), s, blocks)))
    key_spec = pl.BlockSpec((HEAD_DIM, length), lambda g, i, *_: (g, 0))
    return pl.pallas_call(
        backward_kernel,
        out_shape=(
            jax.ShapeDtypeStruct(qt.shape, BF16),
            jax.ShapeDtypeStruct((groups * HEAD_DIM, length), BF16),
            jax.ShapeDtypeStruct((groups * HEAD_DIM, length), BF16),
            jax.ShapeDtypeStruct((qmap.shape[0], HEAD_DIM // 2, 2 * HEAD_DIM), F32),
            jax.ShapeDtypeStruct((kmap.shape[0], HEAD_DIM // 2, 2 * HEAD_DIM), F32),
        ),
        grid_spec=pltpu.PrefetchScalarGridSpec(
            num_scalar_prefetch=1,
            grid=(groups, blocks),
            in_specs=attention_specs(groups, ratio, padded, back)
            + [
                query_spec,
                local_spec,
                pl.BlockSpec((1, ratio, BLOCK), lambda g, i, *_: (g, 0, back(i))),
                pl.BlockSpec((ratio, HEAD_DIM, HEAD_DIM), lambda g, i, *_: (g, 0, 0)),
                pl.BlockSpec((1, HEAD_DIM, HEAD_DIM), lambda g, i, *_: (g, 0, 0)),
            ],
            out_specs=[
                local_spec,
                key_spec,
                key_spec,
                pl.BlockSpec((ratio, HEAD_DIM // 2, 2 * HEAD_DIM), lambda g, i, *_: (g, 0, 0)),
                pl.BlockSpec((1, HEAD_DIM // 2, 2 * HEAD_DIM), lambda g, i, *_: (g, 0, 0)),
            ],
            scratch_shapes=[
                pltpu.VMEM((2 * HEAD_DIM, padded), BF16),
                pltpu.VMEM((padded, 2 * HEAD_DIM), BF16),
                pltpu.VMEM((padded, HEAD_DIM), BF16),
                pltpu.VMEM((padded, HEAD_DIM), BF16),
                pltpu.VMEM((blocks, 2 * HEAD_DIM, HEAD_DIM), BF16),
                pltpu.VMEM((blocks, HEAD_DIM, 2 * HEAD_DIM), BF16),
                pltpu.VMEM((blocks, 2 * HEAD_DIM, 1), F32),
                pltpu.VMEM((HEAD_DIM, padded), F32),
                pltpu.VMEM((2 * HEAD_DIM, padded), F32),
                pltpu.VMEM((HEAD_DIM, padded), F32),
                pltpu.VMEM((2 * HEAD_DIM, HEAD_DIM), F32),
                pltpu.VMEM((HEAD_DIM, 2 * HEAD_DIM), F32),
                pltpu.VMEM((2 * HEAD_DIM, 1), F32),
            ],
        ),
        compiler_params=pltpu.CompilerParams(
            dimension_semantics=("arbitrary", "arbitrary"), vmem_limit_bytes=48 * 1024 * 1024
        ),
        cost_estimate=pl.CostEstimate(flops=1000, bytes_accessed=1000, transcendentals=0),
        name="attention_backward",
    )(
        marks, starts, qt, kvt, kvt, signed_maps(qmap), signed_maps(kmap), dmt, mixt, inverse, qmap, kmap
    )


FREE = pl.CostEstimate(flops=1000, bytes_accessed=1000, transcendentals=0)


def grid_call(kernel, name, grid, out_shape, in_specs, out_specs, scratch=(), aliases=None):
    return pl.pallas_call(
        kernel,
        out_shape=out_shape,
        grid_spec=pltpu.PrefetchScalarGridSpec(
            num_scalar_prefetch=1,
            grid=grid,
            in_specs=in_specs,
            out_specs=out_specs,
            scratch_shapes=list(scratch),
        ),
        input_output_aliases=aliases or {},
        compiler_params=pltpu.CompilerParams(
            dimension_semantics=("arbitrary",) * len(grid), vmem_limit_bytes=VMEM_LIMIT
        ),
        cost_estimate=FREE,
        name=name,
    )


MESH = pl.DeviceIdType.MESH


def exchange_kernel(query_cols, key_cols, *refs):
    inputs, grads, query, key, value, gate, up, down, output = refs[:9]
    thin = refs[9:11]
    near_other, grads_other, proj_got, gate_got, up_got, down_got, output_got = refs[11:18]
    thin_got = refs[18:20]
    proj_own, proj_both, output_both = refs[20:23]
    send_sem, recv_sem, local_sem, proj_all, output_all = refs[23:]
    col = lax.axis_index("col")

    barrier = pltpu.get_barrier_semaphore()
    pl.semaphore_signal(barrier, inc=1, device_id={"col": 1 - col}, device_id_type=MESH)
    pl.semaphore_wait(barrier, 1)

    copies = []

    def remote(source, target):
        n = len(copies)
        copy = pltpu.make_async_remote_copy(
            src_ref=source,
            dst_ref=target,
            send_sem=send_sem.at[n],
            recv_sem=recv_sem.at[n],
            device_id={"col": 1 - col},
            device_id_type=MESH,
        )
        copy.start()
        copies.append(copy)

    def columns(ref, index, width):
        return ref.at[:, pl.ds(pl.multiple_of(index * width, width), width)]

    def rows_of(ref, index, height):
        return ref.at[pl.ds(pl.multiple_of(index * height, height), height), :]

    remote(inputs, near_other)
    first = 0
    for weight, width in ((query, query_cols), (key, key_cols), (value, key_cols)):
        remote(columns(weight, 1 - col, width), proj_got.at[:, pl.ds(first, width)])
        first += width
    for source, target in zip(thin, thin_got):
        remote(source, target)
    remote(columns(gate, 1 - col, gate_got.shape[1]), gate_got)
    remote(columns(up, 1 - col, up_got.shape[1]), up_got)
    remote(rows_of(down, 1 - col, down_got.shape[0]), down_got)
    remote(rows_of(output, 1 - col, output_got.shape[0]), output_got)
    remote(grads, grads_other)

    def local(source, target, n):
        copy = pltpu.make_async_copy(source, target, local_sem.at[n])
        copy.start()
        return copy

    whole = proj_own.shape[1]
    height = output_got.shape[0]
    loads, first = [], 0
    for weight, width in ((query, query_cols), (key, key_cols), (value, key_cols)):
        for side in range(2):
            loads.append(
                local(
                    columns(weight, col ^ side, width),
                    proj_all.at[:, pl.ds(side * whole + first, width)],
                    len(loads),
                )
            )
        first += width
    for side in range(2):
        loads.append(
            local(
                rows_of(output, col ^ side, height),
                output_all.at[pl.ds(side * height, height), :],
                len(loads),
            )
        )
    for copy in loads:
        copy.wait()
    stores = [
        local(proj_all.at[:, pl.ds(0, whole)], proj_own, 8),
        local(proj_all, proj_both, 9),
        local(output_all, output_both, 10),
    ]

    for copy in stores:
        copy.wait()
    for copy in copies:
        copy.wait()


def exchange(inputs, grads, projections, gate, up, down, output, thin):
    query, key, value = projections
    rows, half = inputs.shape
    query_cols, key_cols = query.shape[1] // 2, key.shape[1] // 2
    columns = query_cols + 2 * key_cols
    like = lambda *shape: jax.ShapeDtypeStruct(shape, BF16)
    outs = [
        like(rows, half),
        like(rows, half),
        like(half, columns),
        like(half, gate.shape[1] // 2),
        like(half, up.shape[1] // 2),
        like(down.shape[0] // 2, half),
        like(output.shape[0] // 2, half),
    ]
    outs += [jax.ShapeDtypeStruct(values.shape, values.dtype) for values in thin]
    outs += [like(half, columns), like(half, 2 * columns), like(output.shape[0], half)]
    copies = 1 + 3 + len(thin) + 5
    return pl.pallas_call(
        functools.partial(exchange_kernel, query_cols, key_cols),
        out_shape=tuple(outs),
        in_specs=[pl.BlockSpec(memory_space=pl.ANY)] * (9 + len(thin)),
        out_specs=tuple([pl.BlockSpec(memory_space=pl.ANY)] * len(outs)),
        scratch_shapes=[
            pltpu.SemaphoreType.DMA((copies,)),
            pltpu.SemaphoreType.DMA((copies,)),
            pltpu.SemaphoreType.DMA((11,)),
            pltpu.VMEM((half, 2 * columns), BF16),
            pltpu.VMEM(output.shape, BF16),
        ],
        compiler_params=pltpu.CompilerParams(
            collective_id=0, has_side_effects=True, vmem_limit_bytes=VMEM_LIMIT
        ),
        cost_estimate=FREE,
        name="exchange",
    )(inputs, grads, query, key, value, gate, up, down, output, *thin)


def hidden_grad_kernel(place_ref, mine, other, down_own, down_got, *refs):
    refs[-1][...] = (
        dot_nt(mine[...], down_own[...]) + dot_nt(other[...], down_got[...])
    ).astype(BF16)


def hidden_grad(index, place, grads, down_weight, down_got, kept):
    half, width = grads[0].shape
    hidden_cols = down_got.shape[0]
    tiles = hidden_cols // MLP_TILE
    whole = pl.BlockSpec((half, width), lambda i, s: (0, 0))
    return grid_call(
        hidden_grad_kernel,
        "hidden_grad",
        (tiles,),
        jax.ShapeDtypeStruct((2 * half, hidden_cols), BF16),
        [whole] * 2
        + [
            pl.BlockSpec((MLP_TILE, width), lambda i, s: (s[0] * tiles + i, 0)),
            pl.BlockSpec((MLP_TILE, width), lambda i, s: (i, 0)),
        ]
        + [pl.BlockSpec(memory_space=pl.ANY)] * len(kept),
        pl.BlockSpec((half, MLP_TILE), lambda i, s: (index, i)),
        aliases={5 + i: i for i in range(len(kept))},
    )(place, *grads, down_weight, down_got, *kept)


def project_kernel(
    place_ref,
    mine_ref,
    other_ref,
    gain_ref,
    gain_got_ref,
    proj_own,
    proj_got,
    thin_ref,
    thin_got_ref,
    up_ref,
    *refs,
):
    normed_ref, queries_ref, keys_ref, adapters_ref, scale_ref = refs[-5:]
    half = mine_ref.shape[1]
    mine, other = mine_ref[...].astype(F32), other_ref[...].astype(F32)
    squares = jnp.sum(mine * mine, axis=1, keepdims=True) + jnp.sum(
        other * other, axis=1, keepdims=True
    )
    scale = lax.rsqrt(squares / (2 * half) + norm_eps)
    left = (mine * scale * gain_ref[:1, :]).astype(BF16)
    right = (other * scale * gain_got_ref[:1, :]).astype(BF16)
    normed_ref[:, :half] = left
    normed_ref[:, half:] = right
    scale_ref[...] = scale
    adapters = (dot_nt(left, thin_ref[...]) + dot_nt(right, thin_got_ref[...])).astype(BF16)
    adapters_ref[...] = adapters
    sums = dot_nn(left, proj_own[...]) + dot_nn(right, proj_got[...]) + dot_nn(adapters, up_ref[...])
    turned = jnp.transpose(sums.astype(BF16))
    rows = queries_ref.shape[0]
    queries_ref[...] = turned[:rows]
    keys_ref[...] = turned[rows:]


def global_block(local, flip, half_blocks):
    return ((local // half_blocks) ^ flip) * half_blocks + local % half_blocks


def project_block(index, place, mine, other, gains, projections, thin, up, query_part, kept):
    proj_own, proj_got = projections
    rows, half = mine.shape
    length = 2 * half_rows_of(kept, rows)
    blocks, half_blocks = length // BLOCK, length // BLOCK // 2
    columns = proj_own.shape[1]
    whole = lambda values: pl.BlockSpec(values.shape, lambda i, s: (0, 0))
    lanes = lambda i, s: (0, global_block(index + i, s[1], half_blocks))
    local = lambda i, s: (index + i, 0)
    shapes = (
        jax.ShapeDtypeStruct((length, 2 * half), BF16),
        jax.ShapeDtypeStruct((query_part, length), BF16),
        jax.ShapeDtypeStruct((columns - query_part, length), BF16),
        jax.ShapeDtypeStruct((length, up.shape[0]), BF16),
        jax.ShapeDtypeStruct((length, 1), F32),
    )
    operands = (mine, other, *gains, proj_own, proj_got, *thin, up)
    return grid_call(
        project_kernel,
        "project_block",
        (rows // BLOCK,),
        shapes,
        [
            pl.BlockSpec((BLOCK, half), lambda i, s: (i, 0)),
            pl.BlockSpec((BLOCK, half), lambda i, s: (i, 0)),
        ]
        + [whole(values) for values in operands[2:]]
        + [pl.BlockSpec(memory_space=pl.ANY)] * len(kept),
        [
            pl.BlockSpec((BLOCK, 2 * half), local),
            pl.BlockSpec((query_part, BLOCK), lanes),
            pl.BlockSpec((columns - query_part, BLOCK), lanes),
            pl.BlockSpec((BLOCK, up.shape[0]), local),
            pl.BlockSpec((BLOCK, 1), local),
        ],
        aliases={1 + len(operands) + i: i for i in range(len(kept))},
    )(place, *operands, *kept)


def half_rows_of(kept, rows):
    return kept[0].shape[0] // 2 if kept else rows


def mlp_kernel(
    count,
    place_ref,
    in_mine,
    in_other,
    at_mine,
    at_other,
    far_mine,
    far_other,
    adapter_ref,
    up_ref,
    gain_ref,
    gate_own,
    gate_got,
    up_own,
    up_got,
    dh_ref,
    *refs,
):
    hidden_ref, dgate_ref, dup_ref, normed_ref, scale_ref = refs[-1 - count : -1][:5]
    left_ref = refs[-1]
    half = in_mine.shape[1]

    @pl.when(pl.program_id(0) == 0)
    def _():
        def state(inputs, own, far, adapted):
            return inputs[...].astype(F32) + (
                own[...].astype(F32) + far[...].astype(F32) + adapted
            )

        adapter = adapter_ref[...]
        mine = state(in_mine, at_mine, far_mine, dot_nn(adapter, up_ref[:, :half]))
        other = state(in_other, at_other, far_other, dot_nn(adapter, up_ref[:, half:]))
        squares = jnp.sum(mine * mine, axis=1, keepdims=True) + jnp.sum(
            other * other, axis=1, keepdims=True
        )
        scale = lax.rsqrt(squares / (2 * half) + norm_eps)
        scale_ref[...] = scale
        if count == 6:
            refs[-2][...] = mine
        left_ref[:, :half] = (mine * scale * gain_ref[:, :half]).astype(BF16)
        left_ref[:, half:] = (other * scale * gain_ref[:, half:]).astype(BF16)
        normed_ref[...] = left_ref[...]

    left, right = left_ref[:, :half], left_ref[:, half:]
    gate = dot_nn(left, gate_own[...]) + dot_nn(right, gate_got[...])
    up = dot_nn(left, up_own[...]) + dot_nn(right, up_got[...])
    d_hidden = dh_ref[...].astype(F32)
    sig = 1.0 / (1.0 + jnp.exp(-gate))
    silu = gate * sig
    hidden_ref[...] = (silu * up).astype(BF16)
    dup_ref[...] = (d_hidden * silu).astype(BF16)
    dgate_ref[...] = (d_hidden * up * (sig * (1.0 + gate * (1.0 - sig)))).astype(BF16)


def mlp_block(
    index,
    place,
    inputs,
    input_block,
    attended,
    adapter,
    output_up,
    gain,
    gate_weight,
    gate_got,
    up_weight,
    up_got,
    d_hidden,
    kept,
    state_kept,
    with_state,
):
    half, hidden_cols = gate_got.shape
    width = 2 * half
    length = d_hidden.shape[0]
    tiles = hidden_cols // MLP_TILE
    own_spec = pl.BlockSpec((half, MLP_TILE), lambda i, s: (0, s[0] * tiles + i))
    got_spec = pl.BlockSpec((half, MLP_TILE), lambda i, s: (0, i))
    kept_spec = pl.BlockSpec((BLOCK, MLP_TILE), lambda i, s: (index, i))
    here = lambda columns: pl.BlockSpec((BLOCK, columns), lambda i, s: (index, 0))
    whole = lambda values: pl.BlockSpec(values.shape, lambda i, s: (0, 0))
    input_spec = pl.BlockSpec((BLOCK, half), lambda i, s: (input_block, 0))
    block_spec = pl.BlockSpec((BLOCK, half), lambda i, s: (0, 0))
    shapes = (jax.ShapeDtypeStruct((length, hidden_cols), BF16),) * 3 + (
        jax.ShapeDtypeStruct((length, width), BF16),
        jax.ShapeDtypeStruct((length, 1), F32),
    )
    out_specs = [kept_spec] * 3 + [here(width), here(1)]
    aliases = {15 + i: i for i in range(len(kept))}
    passed = tuple(kept)
    if with_state:
        shapes += (jax.ShapeDtypeStruct((length // 2, half), F32),)
        out_specs.append(here(half))
        if state_kept is not None:
            aliases[15 + len(passed)] = 5
            passed += (state_kept,)
    return grid_call(
        functools.partial(mlp_kernel, len(shapes)),
        "mlp_block",
        (tiles,),
        shapes,
        [input_spec, input_spec]
        + [block_spec] * 4
        + [here(adapter.shape[1]), whole(output_up), whole(gain)]
        + [own_spec, got_spec, own_spec, got_spec, kept_spec]
        + [pl.BlockSpec(memory_space=pl.ANY)] * len(passed),
        out_specs,
        [pltpu.VMEM((BLOCK, width), BF16)],
        aliases,
    )(
        place,
        *inputs,
        *attended,
        adapter,
        output_up,
        gain,
        gate_weight,
        gate_got,
        up_weight,
        up_got,
        d_hidden,
        *passed,
    )


def norm_back_kernel(
    count,
    place_ref,
    total_mine,
    total_other,
    normed_ref,
    scale_ref,
    grad_mine,
    grad_other,
    gain_ref,
    out_own,
    out_got,
    up_ref,
    down_ref,
    *refs,
):
    mixed_ref, mine_ref, adapter_ref, gain_sum = refs[-count:][:4]
    half = total_mine.shape[1]
    gain_left, gain_right = gain_ref[:, :half], gain_ref[:, half:]
    d_left, d_right = total_mine[...].astype(F32), total_other[...].astype(F32)
    hat_left = normed_ref[:, :half].astype(F32) * (1.0 / gain_left)
    hat_right = normed_ref[:, half:].astype(F32) * (1.0 / gain_right)
    term = jnp.sum(d_left * hat_left, axis=0, keepdims=True)
    g_left, g_right = d_left * gain_left, d_right * gain_right
    inner = (
        jnp.sum(g_left * hat_left, axis=1, keepdims=True)
        + jnp.sum(g_right * hat_right, axis=1, keepdims=True)
    ) / (2 * half)
    scale = scale_ref[...]
    left = grad_mine[...].astype(F32) + scale * (g_left - hat_left * inner)
    right = grad_other[...].astype(F32) + scale * (g_right - hat_right * inner)
    if count == 5:
        refs[-1][...] = left
    left, right = left.astype(BF16), right.astype(BF16)
    mine_ref[...] = left
    adapter = (dot_nt(left, up_ref[:, :half]) + dot_nt(right, up_ref[:, half:])).astype(BF16)
    adapter_ref[...] = adapter
    mixed_ref[...] = (
        dot_nt(out_own[...], left) + dot_nt(out_got[...], right) + dot_nt(down_ref[...], adapter)
    ).astype(BF16)

    @pl.when(pl.program_id(0) == 0)
    def _():
        gain_sum[...] = term

    @pl.when(pl.program_id(0) > 0)
    def _():
        gain_sum[...] += term


def norm_back(
    index, place, totals, normed, scale, grads, gain, out_own, out_got, up, down, kept, with_state
):
    half_rows, half = totals[0].shape
    length = 2 * half_rows
    half_blocks = half_rows // BLOCK
    heads = out_own.shape[0]
    base = index * half_blocks
    whole = lambda values: pl.BlockSpec(values.shape, lambda i, s: (0, 0))
    near = pl.BlockSpec((BLOCK, half), lambda i, s: (i, 0))
    here = lambda columns: pl.BlockSpec((BLOCK, columns), lambda i, s: (base + i, 0))
    shapes = (
        jax.ShapeDtypeStruct((heads, length), BF16),
        jax.ShapeDtypeStruct((length, half), BF16),
        jax.ShapeDtypeStruct((length, LANES), BF16),
        jax.ShapeDtypeStruct((1, half), F32),
    )
    out_specs = [
        pl.BlockSpec((heads, BLOCK), lambda i, s: (0, global_block(base + i, s[1], half_blocks))),
        here(half),
        here(LANES),
        pl.BlockSpec((1, half), lambda i, s: (0, 0)),
    ]
    if with_state:
        shapes += (jax.ShapeDtypeStruct((half_rows, half), F32),)
        out_specs.append(near)
    return grid_call(
        functools.partial(norm_back_kernel, len(shapes)),
        "norm_back",
        (half_blocks,),
        shapes,
        [near, near, here(2 * half), here(1), near, near]
        + [whole(values) for values in (gain, out_own, out_got, up, down)]
        + [pl.BlockSpec(memory_space=pl.ANY)] * len(kept),
        out_specs,
        aliases={12 + i: i for i in range(len(kept))},
    )(place, *totals, normed, scale, *grads, gain, out_own, out_got, up, down, *kept)


def pair_sum_kernel(products, *refs):
    operands = refs[:-5]
    out_ref, send_buf, recv_buf, send_sem, recv_sem = refs[-5:]
    step = pl.program_id(0)
    tiles = send_buf.shape[0]
    col = lax.axis_index("col")

    def copy(tile):
        return pltpu.make_async_remote_copy(
            src_ref=send_buf.at[tile],
            dst_ref=recv_buf.at[tile],
            send_sem=send_sem.at[tile],
            recv_sem=recv_sem.at[tile],
            device_id={"col": 1 - col},
            device_id_type=MESH,
        )

    @pl.when(step == 0)
    def _():
        barrier = pltpu.get_barrier_semaphore()
        pl.semaphore_signal(barrier, inc=1, device_id={"col": 1 - col}, device_id_type=MESH)
        pl.semaphore_wait(barrier, 1)

    @pl.when(step < tiles)
    def _():
        send_buf[step] = products(operands, False).astype(BF16)
        copy(step).start()

    @pl.when(step >= tiles)
    def _():
        tile = step - tiles
        sums = products(operands, True)
        copy(tile).wait_recv()
        out_ref[...] = (sums + recv_buf[tile].astype(F32)).astype(BF16)

    @pl.when(step == 2 * tiles - 1)
    def _():
        for tile in range(tiles):
            copy(tile).wait_send()


def pair_sum(products, name, collective, rows, half, in_specs, operands):
    tile = min(SUM_TILE, half)
    tiles = half // tile
    return pl.pallas_call(
        functools.partial(pair_sum_kernel, products),
        grid=(2 * tiles,),
        out_shape=jax.ShapeDtypeStruct((rows, half), BF16),
        in_specs=in_specs,
        out_specs=pl.BlockSpec((rows, tile), lambda i: (0, jnp.maximum(i - tiles, 0))),
        scratch_shapes=[
            pltpu.VMEM((tiles, rows, tile), BF16),
            pltpu.VMEM((tiles, rows, tile), BF16),
            pltpu.SemaphoreType.DMA((tiles,)),
            pltpu.SemaphoreType.DMA((tiles,)),
        ],
        compiler_params=pltpu.CompilerParams(
            dimension_semantics=("arbitrary",),
            collective_id=collective,
            has_side_effects=True,
            vmem_limit_bytes=VMEM_LIMIT,
        ),
        cost_estimate=FREE,
        name=name,
    )(*operands)


def second_products(refs, own):
    d_gate, d_up, gate_own, gate_got, up_own, up_got = refs
    if own:
        return dot_nt(d_gate[...], gate_own[...]) + dot_nt(d_up[...], up_own[...])
    return dot_nt(d_gate[...], gate_got[...]) + dot_nt(d_up[...], up_got[...])


def second_grad(index, d_gate, d_up, gate_weight, gate_got, up_weight, up_got):
    half, hidden_cols = gate_got.shape
    rows = d_gate.shape[0] // 2
    tile = min(SUM_TILE, half)
    tiles = half // tile
    left = pl.BlockSpec((rows, hidden_cols), lambda i: (index, 0))
    own = pl.BlockSpec(
        (tile, hidden_cols), lambda i: (jnp.maximum(i - tiles, 0), lax.axis_index("col"))
    )
    got = pl.BlockSpec((tile, hidden_cols), lambda i: (jnp.minimum(i, tiles - 1), 0))
    return pair_sum(
        second_products,
        "second_grad",
        1 + index,
        rows,
        half,
        [left, left, own, got, own, got],
        (d_gate, d_up, gate_weight, gate_got, up_weight, up_got),
    )


def down_products(refs, own):
    hidden, down_own, down_got = refs
    return dot_nn(hidden[...], (down_own if own else down_got)[...])


def down_product(hidden, down_weight, down_got):
    rows, hidden_cols = hidden.shape
    half = down_got.shape[1]
    tile = min(SUM_TILE, half)
    tiles = half // tile
    return pair_sum(
        down_products,
        "down_product",
        3,
        rows,
        half,
        [
            pl.BlockSpec((rows, hidden_cols), lambda i: (0, 0)),
            pl.BlockSpec(
                (hidden_cols, tile), lambda i: (lax.axis_index("col"), jnp.maximum(i - tiles, 0))
            ),
            pl.BlockSpec((hidden_cols, tile), lambda i: (0, jnp.minimum(i, tiles - 1))),
        ],
        (hidden, down_weight, down_got),
    )


def finish_kernel(orders, small_count, joins, *refs):
    count = len(orders)
    far_ref, refs = refs[0], refs[1:]
    smalls, refs = refs[:small_count], refs[small_count:]
    grads, refs = refs[:count], refs[count:]
    far_out, refs = refs[0], refs[1:]
    totals, refs = refs[:small_count], refs[small_count:]
    joined, refs = refs[: len(joins)], refs[len(joins) :]
    outs, refs = refs[:count], refs[count:]
    send_sem, recv_sem = refs[:2]
    refs = refs[2:]
    place, col = lax.axis_index("dp"), lax.axis_index("col")
    bits = max(len(order) for order in orders)
    small_sums, refs = refs[: small_count * (bits - 1)], refs[small_count * (bits - 1) :]
    small_gots, buffers = refs[: small_count * bits], refs[small_count * bits :]

    barrier = pltpu.get_barrier_semaphore()
    partners = [{"col": 1 - col}]
    partners += [{"dp": place ^ (1 << k)} for k in range(bits)]
    partners.append({"row": 1 - lax.axis_index("row")})
    for partner in partners:
        pl.semaphore_signal(barrier, inc=1, device_id=partner, device_id_type=MESH)
    pl.semaphore_wait(barrier, len(partners))

    started = []

    def send(source, target, partner):
        copy = pltpu.make_async_remote_copy(
            src_ref=source,
            dst_ref=target,
            send_sem=send_sem.at[len(started)],
            recv_sem=recv_sem.at[len(started)],
            device_id=partner,
            device_id_type=MESH,
        )
        copy.start()
        started.append(copy)
        return copy

    far_copy = send(far_ref, far_out, partners[-1])
    current = list(grads)
    small_now = list(smalls)
    used = 0
    for step in range(bits):
        moving = []
        for n in range(small_count):
            got = small_gots[n * bits + step]
            bit = (step + n) % bits
            moving.append((send(small_now[n], got, partners[1 + bit]), got))
        halves = {}
        for n, order in enumerate(orders):
            if step < len(order):
                rows = current[n].shape[0] // 2
                got = buffers[used]
                used += 1
                copy = send(
                    current[n].at[pl.ds(rows, rows), :], got, partners[1 + order[step]]
                )
                halves[n] = (copy, got, rows)
        for n, (copy, got) in enumerate(moving):
            copy.wait_recv()
            target = totals[n] if step + 1 == bits else small_sums[n * (bits - 1) + step]
            target[...] = small_now[n][...] + got[...]
            small_now[n] = target
        if step + 1 == bits:
            joining = []
            for out, (source, first, size, columns, axis) in zip(joined, joins):
                total = totals[source]
                if axis == 0:
                    size = total.shape[0]
                    part, slot = total, out.at[pl.ds(col * size, size)]
                else:
                    part = total.at[pl.ds(first, size), pl.ds(*columns)]
                    slot = out.at[:, pl.ds(pl.multiple_of(col * columns[1], LANES), columns[1])]
                joining.append(send(part, slot, partners[0]))
                slot[...] = part[...]
        for n, (copy, got, rows) in halves.items():
            copy.wait_recv()
            sums = current[n][:rows].astype(F32) + got[...].astype(F32)
            if step + 1 == len(orders[n]):
                outs[n][...] = sums
            else:
                target = buffers[used]
                used += 1
                target[...] = sums.astype(BF16)
                current[n] = target
    for copy in joining + [far_copy]:
        copy.wait_recv()
    for copy in started:
        copy.wait_send()


def finish(far, smalls, joins, grads, orders):
    count = len(grads)
    bits = max(len(order) for order in orders)
    vmem = pl.BlockSpec(memory_space=pltpu.VMEM)
    copies = 1 + bits * len(smalls) + len(joins) + sum(len(order) for order in orders)
    scratch = [pltpu.SemaphoreType.DMA((copies,)), pltpu.SemaphoreType.DMA((copies,))]
    scratch += [pltpu.VMEM(s.shape, F32) for s in smalls for _ in range(bits - 1)]
    scratch += [pltpu.VMEM(s.shape, F32) for s in smalls for _ in range(bits)]
    for step in range(bits):
        for target in range(2):
            for grad, order in zip(grads, orders):
                if step + target < len(order):
                    rows = grad.shape[0] >> (step + 1)
                    scratch.append(pltpu.VMEM((rows, grad.shape[1]), BF16))
    joined = []
    for source, first, size, columns, axis in joins:
        shape = smalls[source].shape
        if axis == 0:
            joined.append(jax.ShapeDtypeStruct((2 * shape[0],) + shape[1:], F32))
        else:
            joined.append(jax.ShapeDtypeStruct((size, 2 * columns[1]), F32))
    outs = [
        jax.ShapeDtypeStruct((g.shape[0] >> len(order), g.shape[1]), F32)
        for g, order in zip(grads, orders)
    ]
    totals = [jax.ShapeDtypeStruct(s.shape, F32) for s in smalls]
    results = pl.pallas_call(
        functools.partial(finish_kernel, orders, len(smalls), joins),
        out_shape=(jax.ShapeDtypeStruct(far.shape, far.dtype), *totals, *joined, *outs),
        in_specs=[pl.BlockSpec(memory_space=pl.ANY)] + [vmem] * (len(smalls) + count),
        out_specs=(pl.BlockSpec(memory_space=pl.ANY),)
        + (vmem,) * (len(totals) + len(joined) + count),
        scratch_shapes=scratch,
        compiler_params=pltpu.CompilerParams(
            collective_id=4, has_side_effects=True, vmem_limit_bytes=VMEM_LIMIT
        ),
        cost_estimate=FREE,
        name="finish",
    )(far, *smalls, *grads)
    first, second = 1 + len(smalls), 1 + len(smalls) + len(joins)
    return results[0], results[1:first], results[first:second], results[second:]


def weight_grad_kernel(sets, chunks, pieces, turned, right_turned, place_ref, *refs):
    outs = refs[-1 - pieces * sets : -1]
    right_ref, left_ref = refs[-2 - pieces * sets], refs[-1]
    lefts = refs[: -2 - pieces * sets]
    length = left_ref.shape[1]
    rows = left_ref.shape[0] // sets
    count = rows // LANES

    @pl.when(pl.program_id(0) == 0)
    def _():
        for p in range(sets * count):
            lanes = slice(p * LANES, (p + 1) * LANES)
            if turned:
                left_ref[lanes, :] = lefts[p][...]
            else:
                size = length // chunks
                for i in range(chunks):
                    left_ref[lanes, i * size : (i + 1) * size] = jnp.transpose(
                        lefts[p * chunks + i][...]
                    )

    for which in range(sets):
        left = left_ref[which * rows : (which + 1) * rows, :]
        sums = (dot_nt if right_turned else dot_nn)(left, right_ref[...])
        size = rows // pieces
        for i in range(pieces):
            outs[pieces * which + i][...] = sums[i * size : (i + 1) * size].astype(BF16)


def weight_grad(places, sets, right, pieces=2, turned=False, right_turned=False, cut=(0, 1)):
    chunks = len(sets[0][0])
    length = sets[0][0][0].shape[1] if turned else sum(c.shape[0] for c in sets[0][0])
    count = (places.shape[0] - 2) // len(sets)
    columns = (right.shape[0] if right_turned else right.shape[1]) // cut[1]
    tile = next(size for size in (GRAD_TILE, 384, 256, 128) if columns % size == 0)
    skip = cut[0] * (columns // tile)
    in_specs, operands = [], []
    for n, (lefts, base) in enumerate(sets):
        for p in range(count):
            at = 2 + n * count + p
            for left in lefts:
                if turned:
                    spec = pl.BlockSpec((LANES, length), lambda j, s, at=at: (s[at], 0))
                else:
                    spec = pl.BlockSpec(
                        (left.shape[0], LANES), lambda j, s, at=at, base=base: (0, base + s[at])
                    )
                in_specs.append(spec)
                operands.append(left)
    if right_turned:
        in_specs.append(pl.BlockSpec((tile, length), lambda j, s: (skip + j, 0)))
    else:
        in_specs.append(pl.BlockSpec((length, tile), lambda j, s: (0, skip + j)))
    size = count * LANES // pieces
    out_spec = pl.BlockSpec((size, tile), lambda j, s: (0, j))
    return grid_call(
        functools.partial(weight_grad_kernel, len(sets), chunks, pieces, turned, right_turned),
        "weight_grad",
        (columns // tile,),
        (jax.ShapeDtypeStruct((size, columns), BF16),) * (pieces * len(sets)),
        in_specs,
        [out_spec] * (pieces * len(sets)),
        [pltpu.VMEM((len(sets) * count * LANES, length), BF16)],
    )(places, *operands, right)


def pair_grad_kernel(chunks, merged, *refs):
    send_buf, own_buf, left_ref, send_sem, recv_sem, local_sem = refs[-6:]
    outs = refs[-7:-6] if merged else refs[-10:-6]
    inputs = refs[: -7 if merged else -10]
    lefts, right_ref = inputs[:-1], inputs[-1]
    step = pl.program_id(0)
    tiles, rows, tile = send_buf.shape
    count = rows // LANES
    half = rows // 2
    col = lax.axis_index("col")

    def sent(source, target, n):
        return pltpu.make_async_remote_copy(
            src_ref=source,
            dst_ref=target,
            send_sem=send_sem.at[n],
            recv_sem=recv_sem.at[n],
            device_id={"col": 1 - col},
            device_id_type=MESH,
        )

    def columns(index, base):
        start = index * tile
        if not isinstance(start, int):
            start = pl.multiple_of(start, tile)
        return pl.ds(base + start, tile)

    def copies(index):
        if merged:
            (out,) = outs
            whole = tiles * tile
            return (
                [sent(send_buf.at[index], out.at[:, columns(index, whole)], index)],
                [
                    pltpu.make_async_copy(
                        own_buf.at[index], out.at[:, columns(index, 0)], local_sem.at[index]
                    )
                ],
            )
        got = outs[2:]
        return [
            sent(
                send_buf.at[index, pl.ds(n * half, half), :],
                got[n].at[:, columns(index, 0)],
                2 * index + n,
            )
            for n in range(2)
        ], []

    @pl.when(step == 0)
    def _():
        barrier = pltpu.get_barrier_semaphore()
        pl.semaphore_signal(barrier, inc=1, device_id={"col": 1 - col}, device_id_type=MESH)
        pl.semaphore_wait(barrier, 1)
        size = left_ref.shape[1] // chunks
        for p in range(2 * count):
            for i in range(chunks):
                left_ref[p * LANES : (p + 1) * LANES, i * size : (i + 1) * size] = jnp.transpose(
                    lefts[p * chunks + i][...]
                )

    send_buf[step] = dot_nn(left_ref[rows:, :], right_ref[...]).astype(BF16)
    away, near = copies(step)
    for copy in away:
        copy.start()
    own = dot_nn(left_ref[:rows, :], right_ref[...]).astype(BF16)
    if merged:
        own_buf[step] = own
        near[0].start()
    else:
        outs[0][...] = own[:half]
        outs[1][...] = own[half:]

    @pl.when(step == tiles - 1)
    def _():
        for index in range(tiles):
            away, near = copies(index)
            for copy in away + near:
                copy.wait()


def pair_grad(name, collective, lefts, others, right, order, other_order, merged):
    chunks = len(lefts[0])
    length = sum(values.shape[0] for values in lefts[0])
    columns = right.shape[1]
    tile = min(GRAD_TILE, columns)
    tiles = columns // tile
    count = len(order)
    rows = count * LANES
    in_specs, operands = [], []
    for (parts, base), which in ((lefts, order), (others, other_order)):
        for p in range(count):
            for values in parts:

                def at(j, base=base, entry=which[p]):
                    if isinstance(entry, tuple):
                        return (0, base + (lax.axis_index("dp") ^ entry[0]))
                    return (0, base + entry)

                in_specs.append(pl.BlockSpec((values.shape[0], LANES), at))
                operands.append(values)
    in_specs.append(pl.BlockSpec((length, tile), lambda j: (0, j)))
    anywhere = pl.BlockSpec(memory_space=pl.ANY)
    like = lambda *shape: jax.ShapeDtypeStruct(shape, BF16)
    if merged:
        out_shape, out_specs = (like(rows, 2 * columns),), (anywhere,)
    else:
        out_shape = (like(rows // 2, columns),) * 4
        near = pl.BlockSpec((rows // 2, tile), lambda j: (0, j))
        out_specs = (near, near, anywhere, anywhere)
    transfers = tiles if merged else 2 * tiles
    return pl.pallas_call(
        functools.partial(pair_grad_kernel, chunks, merged),
        grid=(tiles,),
        out_shape=out_shape,
        in_specs=in_specs,
        out_specs=out_specs,
        scratch_shapes=[
            pltpu.VMEM((tiles, rows, tile), BF16),
            pltpu.VMEM((tiles if merged else 1, rows, tile), BF16),
            pltpu.VMEM((2 * rows, length), BF16),
            pltpu.SemaphoreType.DMA((transfers,)),
            pltpu.SemaphoreType.DMA((transfers,)),
            pltpu.SemaphoreType.DMA((tiles,)),
        ],
        compiler_params=pltpu.CompilerParams(
            dimension_semantics=("arbitrary",),
            collective_id=collective,
            has_side_effects=True,
            vmem_limit_bytes=VMEM_LIMIT,
        ),
        cost_estimate=FREE,
        name=name,
    )(*operands, right)


def first_back_kernel(place_ref, *refs):
    parts, (proj_ref, up_ref, normed_ref) = refs[:6], refs[6:9]
    far_ref, own_ref, turned_ref, adapter_ref, gain_ref = refs[9:]
    step = pl.program_id(0)
    first = 0
    for source in parts:
        turned_ref[:, first : first + source.shape[0]] = jnp.transpose(source[...])
        first += source.shape[0]
    turned = turned_ref[...]
    adapter_ref[...] = dot_nt(up_ref[...], turned)
    sums = dot_nt(turned, proj_ref[...])
    term = jnp.sum(sums * normed_ref[...].astype(F32), axis=0, keepdims=True)

    @pl.when(step < pl.num_programs(0) // 2)
    def _():
        far_ref[...] = sums.astype(BF16)

    @pl.when(step >= pl.num_programs(0) // 2)
    def _():
        own_ref[...] = sums

    @pl.when(step == 0)
    def _():
        gain_ref[...] = term

    @pl.when(step > 0)
    def _():
        gain_ref[...] += term


def first_back(place, parts, proj_native, up_native, normed):
    length = parts[0].shape[1]
    half, columns = proj_native.shape
    blocks = length // BLOCK
    middle = blocks // 2
    at = lambda i: (i + middle) % blocks
    whole = lambda values: pl.BlockSpec(values.shape, lambda i, s: (0, 0))
    return grid_call(
        first_back_kernel,
        "first_back",
        (blocks,),
        (
            jax.ShapeDtypeStruct((length // 2, half), BF16),
            jax.ShapeDtypeStruct((length // 2, half), F32),
            jax.ShapeDtypeStruct((length, columns), BF16),
            jax.ShapeDtypeStruct((up_native.shape[0], length), F32),
            jax.ShapeDtypeStruct((1, half), F32),
        ),
        [pl.BlockSpec((values.shape[0], BLOCK), lambda i, s: (0, at(i))) for values in parts]
        + [whole(proj_native), whole(up_native)]
        + [pl.BlockSpec((BLOCK, half), lambda i, s: (at(i), 0))],
        [
            pl.BlockSpec((BLOCK, half), lambda i, s: (jnp.minimum(i, middle - 1), 0)),
            pl.BlockSpec((BLOCK, half), lambda i, s: (jnp.maximum(i - middle, 0), 0)),
            pl.BlockSpec((BLOCK, columns), lambda i, s: (at(i), 0)),
            pl.BlockSpec((up_native.shape[0], BLOCK), lambda i, s: (0, at(i))),
            whole(jnp.zeros((1, half))),
        ],
    )(place, *parts, proj_native, up_native, normed)


def after(value, *others):
    return lax.optimization_barrier((value,) + others)[0]


def swap(values, axis):
    return lax.ppermute(values, axis, [(0, 1), (1, 0)])


def part(values, index, count, axis):
    width = values.shape[axis] // count
    return lax.dynamic_slice_in_dim(values, index * width, width, axis)


def contract(left, right, left_dim, right_dim):
    return lax.dot_general(
        left, right, (((left_dim,), (right_dim,)), ((), ())), preferred_element_type=F32
    )


def exchange_order(bits, first):
    return [(first + k) % bits for k in range(bits)]


def relative_index(position, order):
    bits = len(order)
    return sum(((position >> (bits - 1 - k)) & 1) << order[k] for k in range(bits))


def relative_blocks(values, axis, device, order):
    count = 1 << len(order)
    return jnp.concatenate(
        [part(values, device ^ relative_index(p, order), count, axis) for p in range(count)],
        axis=axis,
    )


class Reduction:
    def __init__(self, keep, send, size, order):
        self.keep, self.size, self.order, self.step = keep, size, order, 0
        self.launch(send)

    def launch(self, send):
        bit = 1 << self.order[self.step]
        self.got = lax.ppermute(send, "dp", [(i, i ^ bit) for i in range(self.size)])

    def combine(self):
        got = self.got
        self.step += 1
        if self.step == len(self.order):
            self.keep = self.keep.astype(F32) + got.astype(F32)
            return self.keep
        half = self.keep.shape[0] // 2
        sums = (
            (self.keep[rows].astype(F32) + got[rows].astype(F32)).astype(BF16)
            for rows in (slice(0, half), slice(half, 2 * half))
        )
        self.keep, send = sums
        self.launch(send)
        return self.keep

    @property
    def done(self):
        return self.step == len(self.order)


def total_over(values, size, bits):
    for k in range(bits):
        values = values + lax.ppermute(values, "dp", [(i, i ^ (1 << k)) for i in range(size)])
    return values


def ordered(own, other, index, axis):
    return jnp.where(
        index == 0,
        jnp.concatenate([own, other], axis=axis),
        jnp.concatenate([other, own], axis=axis),
    )


def on_device(
    activations,
    grad_out,
    segments,
    first_gain,
    query_weight,
    key_weight,
    value_weight,
    query_down,
    query_up,
    key_down,
    key_up,
    value_down,
    value_up,
    query_map,
    key_map,
    output_weight,
    output_down,
    output_up,
    second_gain,
    gate_weight,
    up_weight,
    down_weight,
):
    size = lax.axis_size("dp")
    bits = size.bit_length() - 1
    device = lax.axis_index("dp")
    row = lax.axis_index("row")
    col = lax.axis_index("col")
    seq_rows = segments.shape[1]
    half_rows, feature_cols = activations.shape
    width = 2 * feature_cols
    blocks = seq_rows // BLOCK
    half_blocks = blocks // 2
    rank = query_down.shape[1]
    query_part = query_weight.shape[1] // 2
    key_part = key_weight.shape[1] // 2
    part_cols = query_part + 2 * key_part
    order = exchange_order(bits, 0)
    turned_order = exchange_order(bits, 1)
    mixed_order = [1, 0] + order[2:]

    def other_half(values, axis):
        return jnp.roll(values, values.shape[axis] // 2, axis)

    def sequence_order(values, axis):
        return jnp.where(row == 0, values, other_half(values, axis))

    def rows_of(index):
        return slice(index * BLOCK, (index + 1) * BLOCK)

    lane_blocks = feature_cols // LANES
    direct = lane_blocks == size

    def block_order(which, rows_of_pair=False):
        if not direct:
            return [jnp.int32(p) for p in range(lane_blocks)]
        blocks_of = [device ^ relative_index(p, which) for p in range(size)]
        if rows_of_pair:
            return [((b // (size // 2)) ^ col) * (size // 2) + b % (size // 2) for b in blocks_of]
        return blocks_of

    def places(*orders, rows_of_pair=False):
        entries = [col, row]
        for which in orders:
            entries += block_order(which, rows_of_pair)
        return jnp.stack([jnp.asarray(v, jnp.int32) for v in entries])

    place = places(order)

    def grads_of(sets, right, orders, right_turned=False, cut=(0, 1), pieces=2):
        if not direct:
            sets = [
                (
                    [
                        relative_blocks(
                            left[:, base * LANES : base * LANES + feature_cols], 1, device, which
                        )
                        for left in lefts
                    ],
                    0,
                )
                for (lefts, base), which in zip(sets, orders)
            ]
        outs = weight_grad(places(*orders), sets, right, pieces, False, right_turned, cut)
        return [outs[pieces * n : pieces * (n + 1)] for n in range(len(sets))]

    def ups(index):
        zeros_key = jnp.zeros((rank, key_part), BF16)
        zeros_query = jnp.zeros((rank, query_part), BF16)
        return jnp.concatenate(
            [
                jnp.concatenate([part(query_up, index, 2, 1), zeros_key, zeros_key], axis=1),
                jnp.concatenate([zeros_query, part(key_up, index, 2, 1), zeros_key], axis=1),
                jnp.concatenate([zeros_query, zeros_key, part(value_up, index, 2, 1)], axis=1),
                jnp.zeros((rank, part_cols), BF16),
            ],
            axis=0,
        )

    thin = jnp.concatenate(
        [jnp.transpose(v) for v in (query_down, key_down, value_down)] + [output_up], axis=0
    )
    gains = jnp.stack([first_gain, second_gain])
    inputs_far = swap(activations, "row")
    (
        inputs_other,
        grads_other,
        proj_got,
        gate_got,
        up_got,
        mlp_down_got,
        output_got,
        thin_got,
        gains_got,
        proj_own,
        proj_native,
        output_native,
    ) = exchange(
        activations,
        grad_out,
        (query_weight, key_weight, value_weight),
        gate_weight,
        up_weight,
        down_weight,
        output_weight,
        (thin, gains),
    )
    grads_far = swap(after(grad_out, inputs_far), "row")
    up_own = ups(col)
    up_native = jnp.concatenate([up_own, ups(1 - col)], axis=1)
    second_gain_full = jnp.concatenate([gains[1:], gains_got[1:]], axis=1)
    output_up_full = jnp.concatenate([output_up, thin_got[3 * rank :]], axis=1)
    output_up_full = jnp.pad(output_up_full, ((0, LANES - rank), (0, 0)))
    output_rows_own = part(output_weight, col, 2, 0)
    output_down_own = part(output_down, col, 2, 0)
    output_down_native = jnp.concatenate(
        [output_down_own, part(output_down, 1 - col, 2, 0)], axis=0
    )
    output_down_padded = jnp.pad(output_down_own, ((0, 0), (0, LANES - rank)))
    query_map_own = part(query_map, col, 2, 0)
    key_map_own = part(key_map, col, 2, 0)

    documents = segments[0]
    starts = jnp.sum((documents[None, :] < documents[:, None]).astype(jnp.int32), axis=1)
    marks = jnp.concatenate(
        [
            jnp.full((1,), seq_rows, jnp.int32),
            starts[BLOCK - WINDOW - 1 :: BLOCK],
            jnp.asarray(row, jnp.int32)[None],
        ]
    )
    starts = starts.reshape(1, 1, seq_rows)

    def project(index, mine, other, kept):
        return project_block(
            index,
            place,
            mine,
            other,
            (gains, gains_got),
            (proj_own, proj_got),
            (thin, thin_got),
            up_own,
            query_part,
            kept,
        )

    kept = project(0, activations, inputs_other, ())
    inputs_far = after(inputs_far, kept[0])
    inputs_far_other = swap(inputs_far, "col")
    kept = project(half_blocks, inputs_far, inputs_far_other, kept)
    normed_first, queries, keys_values, adapters, first_scale = kept
    keys_values = jnp.pad(keys_values, ((0, 0), (WINDOW, WINDOW)))
    mixed, inverse = attention_forward(
        marks, starts, queries, keys_values, query_map_own, key_map_own
    )

    d_hidden = hidden_grad(
        0, place, (after(grad_out, mixed), grads_other), down_weight, mlp_down_got, ()
    )
    mixed, grads_far, _ = lax.optimization_barrier((mixed, grads_far, d_hidden))
    mixed_pair = jnp.concatenate([mixed, swap(mixed, "col")], axis=0)
    adapter_sum = contract(mixed_pair, output_down_native, 0, 0)
    adapter_far = swap(other_half(adapter_sum, 0), "row")
    grads_far_other = swap(after(grads_far, mixed), "col")
    send_order = [(b + half_blocks) % blocks for b in range(blocks)]
    attended, attended_far = [None] * blocks, [None] * blocks
    pair = after(mixed_pair, grads_far)
    for b in send_order:
        attended[b] = contract(pair[:, rows_of(b)], output_native, 0, 0).astype(BF16)
        attended_far[send_order[b]] = swap(after(attended[b], adapter_far), "row")
        pair = after(pair, attended[b])
    out_adapter = (adapter_sum + adapter_far).astype(BF16)
    adapter_padded = jnp.pad(out_adapter, ((0, 0), (0, LANES - rank)))
    attended_other = [swap(attended[0], "col")] + [None] * (blocks - 1)
    d_hidden = hidden_grad(
        1,
        place,
        (after(grads_far, *attended, adapter_padded), grads_far_other),
        down_weight,
        mlp_down_got,
        (d_hidden,),
    )

    clock = (d_hidden,)
    kept, state = (), None
    for b in range(blocks):
        far = after(attended_far[b], *clock)
        far_other = swap(far, "col")
        if b + 1 < blocks:
            attended_other[b + 1] = swap(after(attended[b + 1], far), "col")
        inputs = (
            (activations, inputs_other)
            if b < half_blocks
            else (inputs_far, inputs_far_other)
        )
        outs = mlp_block(
            b,
            place,
            inputs,
            b % half_blocks,
            (attended[b], attended_other[b], far, far_other),
            adapter_padded,
            output_up_full,
            second_gain_full,
            gate_weight,
            gate_got,
            up_weight,
            up_got,
            d_hidden,
            kept,
            state,
            b < half_blocks,
        )
        kept = outs[:5]
        state = outs[5] if b < half_blocks else state
        clock = (kept[0],)
    hidden, d_gate, d_up, second_normed, second_scale = kept

    sums = {}

    def reduction(name, pair, which):
        sums[name] = Reduction(*pair, size, which)

    def settle(clock, *names):
        for name in names:
            sums[name].got = after(sums[name].got, *clock)
            clock = (sums[name].combine(),)
        return clock

    def arrived(values, *names):
        tied = lax.optimization_barrier((values,) + tuple(sums[name].got for name in names))
        for name, got in zip(names, tied[1:]):
            sums[name].got = got
        return tied[0]

    def scattered(values):
        return lax.psum_scatter(values, "dp", scatter_dimension=0, tiled=True).astype(F32)

    in_order = list(range(lane_blocks))

    def relative(which):
        return [(relative_index(p, which),) for p in range(size)] if direct else in_order

    def arranged(parts, which):
        if direct:
            return parts
        return [relative_blocks(values, 1, device, which) for values in parts]

    (gate_pair,) = pair_grad(
        "gate_grad",
        5,
        ([second_normed], 0),
        ([second_normed], lane_blocks),
        d_gate,
        in_order,
        in_order,
        True,
    )
    grad_gate_pair = scattered(gate_pair)
    down_outs = pair_grad(
        "down_grad",
        6,
        (arranged([grad_out, grads_far], order), 0),
        (arranged([grads_other, grads_far_other], turned_order), 0),
        after(hidden, gate_pair),
        relative(order),
        relative(turned_order),
        False,
    )
    own_down = down_outs[:2]
    reduction("down_own", own_down, order)
    reduction("down_got", down_outs[2:], turned_order)
    chip_far = second_grad(
        1, after(d_gate, own_down[0]), d_up, gate_weight, gate_got, up_weight, up_got
    )
    far_got_own = swap(chip_far, "row")
    chip_own = second_grad(
        0, after(d_gate, chip_far), d_up, gate_weight, gate_got, up_weight, up_got
    )
    far_got_far = swap(chip_own, "row")
    (up_pair,) = pair_grad(
        "up_grad",
        7,
        ([second_normed], 0),
        ([second_normed], lane_blocks),
        after(d_up, chip_own),
        in_order,
        in_order,
        True,
    )
    y_chip = down_product(after(hidden, up_pair), down_weight, mlp_down_got)
    clock = settle((y_chip,), "down_own", "down_got")

    totals = []
    for chip, got in ((chip_own, far_got_own), (chip_far, far_got_far)):
        total = (chip.astype(F32) + after(got, *clock).astype(F32)).astype(BF16)
        totals.append(total)
        clock = (total,)
    totals = [(total, swap(after(total, *clock), "col")) for total in totals]

    def back(index, grads, kept):
        return norm_back(
            index,
            place,
            totals[index],
            second_normed,
            second_scale,
            grads,
            second_gain_full,
            output_rows_own,
            output_got,
            output_up_full,
            output_down_padded,
            kept,
            index == 0,
        )

    outs = back(0, (grad_out, grads_other), ())
    kept, gain_sum, grad_state = outs[:3], outs[3], outs[4]
    grad_up_pair = scattered(after(up_pair, kept[0]))
    outs = back(1, (grads_far, grads_far_other), kept)
    kept = outs[:3]
    d_mixed, d_mine, d_out_padded = kept
    grad_second_gain = gain_sum + outs[3]
    d_out_adapter = d_out_padded[:, :rank]
    y_far = swap(after(y_chip, kept[0])[half_rows:], "row")
    grad_output_up = contract(out_adapter, d_mine, 0, 0)
    grad_output_down = contract(d_out_adapter, mixed, 0, 1)
    lefts = mixed_pair
    if not direct:
        lefts = relative_blocks(ordered(mixed, mixed_pair[query_part:], col, 0), 0, device, order)
    output_pair = weight_grad(
        places(order, rows_of_pair=True),
        [([lefts], 0)],
        after(d_mine, grad_output_up, grad_output_down),
        2,
        True,
    )
    reduction("output", output_pair, order)
    clock = (output_pair[0],)

    d_queries, d_keys, d_values, grad_query_map, grad_key_map = attention_backward(
        marks,
        starts,
        queries,
        keys_values,
        query_map_own,
        key_map_own,
        after(d_mixed, *clock),
        mixed,
        inverse,
    )

    d_queries = arrived(d_queries, "output", "down_own", "down_got")
    d_keys, d_values, _ = lax.optimization_barrier((d_keys, d_values, d_queries))
    d_parts = (d_queries, d_keys, d_values)
    d_parts += tuple(swap(values, "col") for values in d_parts)
    clock = tuple(sums[name].combine() for name in ("output", "down_own", "down_got"))
    d_first_far, d_first, d_turned, adapter_sum, gain_term = first_back(
        place, (after(d_queries, y_far, *clock),) + d_parts[1:], proj_native, up_native, normed_first
    )
    adapter_far = swap(other_half(adapter_sum, 1), "row")
    gain_far = swap(gain_term, "row")
    (proj_a,) = grads_of([([normed_first], 0)], d_turned, (order,), False, (0, 2), 1)
    (proj_b,) = grads_of(
        [([normed_first], 0)], after(d_turned, proj_a[0]), (mixed_order,), False, (1, 2), 1
    )
    adapter_far, gain_far, _ = lax.optimization_barrier((adapter_far, gain_far, proj_b[0]))
    d_adapter = (adapter_sum + adapter_far).astype(BF16)
    grad_down = contract(d_adapter, normed_first[:, :feature_cols], 1, 0)[: 3 * rank]
    grad_up = contract(adapters, d_turned[:, :part_cols], 0, 0)
    grad_up = jnp.concatenate(
        [
            grad_up[n * rank : (n + 1) * rank, first : first + count]
            for n, (first, count) in enumerate(
                ((0, query_part), (query_part, key_part), (query_part + key_part, key_part))
            )
        ],
        axis=1,
    )
    down_term = jnp.sum(thin[: 3 * rank].astype(F32) * grad_down, axis=0, keepdims=True)
    grad_first_gain = (gain_term + gain_far + down_term) / first_gain[None]
    result = (state + y_chip[:half_rows].astype(F32) + y_far.astype(F32)).astype(BF16)

    def sides(pair):
        half = pair.shape[1] // 2
        return ordered(pair[:, :half], pair[:, half:], col, 1)

    grad_gate = sides(grad_gate_pair)
    clock = settle((grad_up, result, grad_gate), "output", "down_own", "down_got")
    d_first = d_first + contract(d_adapter[:, :half_rows], thin, 0, 0)
    tied_down = None
    if sums["down_own"].done and sums["down_got"].done:
        whole_down = ordered(sums["down_own"].keep, sums["down_got"].keep, col, 1)
        tied_down = jnp.transpose(whole_down)
        clock += (tied_down,)
    d_first_far, totals, joined, reduced = finish(
        after(d_first_far, *clock),
        (
            after(grad_first_gain, d_first),
            grad_second_gain,
            grad_output_up,
            grad_down,
            grad_output_down,
            grad_up,
            grad_query_map,
            grad_key_map,
        ),
        (
            (5, 0, rank, (0, query_part), 1),
            (5, 0, rank, (query_part, key_part), 1),
            (5, 0, rank, (query_part + key_part, key_part), 1),
            (6, 0, 0, (), 0),
            (7, 0, 0, (), 0),
            (4, 0, rank, (0, query_part), 1),
        ),
        (proj_a[0], proj_b[0]),
        (order, mixed_order),
    )
    d_first = d_first + d_first_far.astype(F32)
    first_scale = first_scale[:half_rows]
    hat_own = activations.astype(F32) * first_scale
    grad_hat = d_first * first_gain
    inner = jnp.sum(grad_hat * hat_own, axis=1)
    inner = ((inner + swap(inner, "col")) / width)[:, None]
    grad_activations = grad_state + first_scale * (grad_hat - hat_own * inner)
    grad_proj_a, grad_proj_b = reduced
    clock = (totals[0],)
    while any(not item.done for item in sums.values()):
        clock = settle(clock, *(name for name, item in sums.items() if not item.done))
    down_total = jnp.transpose(totals[3])

    def unpacked_maps(maps):
        half = maps.shape[2] // 2
        return jnp.concatenate([maps[:, :, :half], maps[:, :, half:]], axis=1)

    proj_grads = [
        ordered(
            grad_proj_a[:, first : first + count],
            grad_proj_b[:, first : first + count],
            col,
            1,
        )
        for first, count in (
            (0, query_part),
            (query_part, key_part),
            (query_part + key_part, key_part),
        )
    ]

    grad_up_weight = sides(grad_up_pair)
    grad_down_weight = tied_down
    if tied_down is None:
        whole_down = ordered(sums["down_own"].keep, sums["down_got"].keep, col, 1)
        grad_down_weight = jnp.transpose(whole_down)
    return (
        result,
        grad_activations,
        totals[0][0],
        proj_grads[0],
        proj_grads[1],
        proj_grads[2],
        down_total[:, :rank],
        joined[0],
        down_total[:, rank : 2 * rank],
        joined[1],
        down_total[:, 2 * rank : 3 * rank],
        joined[2],
        unpacked_maps(joined[3]),
        unpacked_maps(joined[4]),
        sums["output"].keep,
        jnp.transpose(joined[5]),
        totals[2],
        totals[1][0],
        grad_gate,
        grad_up_weight,
        grad_down_weight,
    )


def solution(mesh):
    placed = (
        P(("dp", "row"), "col"),
        P(("dp", "row"), "col"),
        P("dp", None),
        P("col"),
        P("col", "row"),
        P("col", "row"),
        P("col", "row"),
        P("col", None),
        P(None, "row"),
        P("col", None),
        P(None, "row"),
        P("col", None),
        P(None, "row"),
        P("row", None, None),
        P("row", None, None),
        P("row", "col"),
        P("row", None),
        P(None, "col"),
        P("col"),
        P("col", "row"),
        P("col", "row"),
        P("row", "col"),
    )
    return jax.shard_map(
        on_device,
        mesh=mesh,
        in_specs=placed,
        out_specs=(
            P(("dp", "row"), "col"),
            P(("dp", "row"), "col"),
            P("col"),
            P(("col", "dp"), "row"),
            P(("col", "dp"), "row"),
            P(("col", "dp"), "row"),
            P("col", None),
            P(None, "row"),
            P("col", None),
            P(None, "row"),
            P("col", None),
            P(None, "row"),
            P("row", None, None),
            P("row", None, None),
            P(("row", "dp"), "col"),
            P("row", None),
            P(None, "col"),
            P("col"),
            P(("col", "dp"), "row"),
            P(("col", "dp"), "row"),
            P("row", ("col", "dp")),
        ),
        check_vma=False,
    )
```
